32 devices in a mesh: dp: 8 (over z, x), mp: 4 (over y, core).
Axes of the slice: x: 2, y: 2, z: 4, core: 2. Of those that a mesh axis runs over, the one named last changes fastest.
Arguments:
- tokens: bfloat16 [2, 40960, 1024], P(None, ('dp', 'mp')), may hold values from -6 to 6
- cotangent: bfloat16 [2, 40960, 1024], P(None, ('dp', 'mp')), may hold values from -6 to 6
- qkv_weight: bfloat16 [3, 1024, 1024], P(None, None, 'mp'), may hold values from -0.1875 to 0.1875
- out_weight: bfloat16 [1024, 1024], P('mp'), may hold values from -0.75 to 0.75
- up_weight: bfloat16 [1024, 4096], P(None, 'mp'), may hold values from -0.1875 to 0.1875
- down_weight: bfloat16 [4096, 1024], P('mp'), may hold values from -0.09375 to 0.09375
- rel_bias: float32 [16, 2025], P('mp'), may hold values from -4 to 4
- ada_weight: bfloat16 [1024, 6144], P('mp'), may hold values from -0.1875 to 0.1875
- ada_bias: float32 [6144], replicated, may hold values from -3 to 3
- class_embed: float32 [1000, 1024], P(None, 'mp'), may hold values from -5 to 5
- window_clip: int32 [2, 128], P(None, 'dp'), may hold values from 0 to 7, as said below
- timesteps: int32 [2, 8], replicated, may hold values from 0 to 999
- class_ids: int32 [2, 8], replicated, may hold values from 0 to 999
Outputs:
- block_out: bfloat16 [2, 40960, 1024], P(None, ('dp', 'mp'))
- token_grad: bfloat16 [2, 40960, 1024], P(None, ('dp', 'mp'))
- qkv_grad: float32 [3, 1024, 1024], P(None, None, 'mp')
- out_grad: float32 [1024, 1024], P('mp')
- up_grad: float32 [1024, 4096], P(None, 'mp')
- down_grad: float32 [4096, 1024], P('mp')
- rel_grad: float32 [16, 2025], P('mp')
- ada_weight_grad: float32 [1024, 6144], P('mp')
- ada_bias_grad: float32 [6144], replicated
- class_grad: float32 [1000, 1024], P(None, 'mp')
The draws below stay inside these ranges and needn't reach their ends.
Inputs may be any that keep to these rules, and one draw needn't show every extreme that they name: `window_clip`: in each micro-batch, one clip drawn from the seed holds the first window of every index of dp.
All inputs are finite; a program needn't handle non-finite values.
Results may differ from the reference program's by a relative error of at most 0.02.
The reference program's roundings to bfloat16 on the way count: a program that leaves them out, or rounds other values in their place, can miss the bound.
Values may be sent and summed in bfloat16 or wider, within the bound.
No kernel may reach another device: no remote copies, remote signals or barrier semaphores. Data moves between devices by JAX's collectives and lax.ppermute only.
A program may use at most 640 MiB of HBM per device.

```python
import math
import jax
import jax.numpy as jnp
from jax import lax

D = 1024
HEADS = 16
HEAD_DIM = 64
FF = 4096
CLASSES = 1000
WIN_T = 5
WIN_H = 8
WIN_W = 8
MICRO = 2
WIN_DEV = 16
WIN_TOK = 320
NREL = 2025
CLIPS = 8
WINDOWS = 128
ROWS = 40960


def draw_window_clip(key, part):
    scattered = jax.random.randint(jax.random.fold_in(key, 11), (MICRO, WINDOWS), 0, CLIPS)
    spanning = jax.random.randint(jax.random.fold_in(key, 12), (MICRO, 1), 0, CLIPS)
    leading = (jnp.arange(WINDOWS) % WIN_DEV == 0)[None, :]
    return jnp.where(leading, spanning, scattered).astype(jnp.int32)


def touch_ends(values, key, smallest, largest):
    longest = values.shape.index(max(values.shape))
    spots = []
    for shift in (0, 1):
        where = [jax.random.randint(jax.random.fold_in(key, axis), (), 0, length) for axis, length in enumerate(values.shape)]
        where[longest] = (where[longest] + shift) % values.shape[longest]
        spots.append(tuple(where))
    return values.at[spots[0]].set(smallest).at[spots[1]].set(largest)


def levels(key, shape, cuts, least, top_value):
    def one(position, shards_of):
        steps = jax.random.uniform(jax.random.fold_in(jax.random.fold_in(key, 6), position), (shards_of,), jnp.float32, least / len(cuts), top_value / len(cuts))
        return jnp.repeat(jnp.exp(steps), shape[position] // shards_of).reshape((-1,) + (1,) * (len(shape) - position - 1))

    level = one(*cuts[0])
    for cut in cuts[1:]:
        level = level * one(*cut)
    return level


def scatter_about(own_key, dims, scale, limit, cuts=(), held_as=jnp.bfloat16):
    factor_of = levels(own_key, dims, cuts, -0.22, 0.18) if cuts else 1.0
    values = jax.random.normal(own_key, dims, jnp.float32) * scale * factor_of
    return jnp.minimum(jnp.maximum(values, -limit), limit).astype(held_as)


def setup_inputs(seed: int = 0) -> dict:
    arg_keys = jax.random.split(jax.random.key(seed), 14)
    tokens = scatter_about(arg_keys[0], (MICRO, ROWS, D), 1.0, 6.0, ((1, 32),))
    cotangent = scatter_about(arg_keys[1], (MICRO, ROWS, D), 1.0, 6.0, ((1, 32),))
    qkv_weight = scatter_about(arg_keys[2], (3, D, D), D ** -0.5, 0.1875, ((2, 4),))
    out_weight = scatter_about(arg_keys[3], (D, D), (max(D // 16, 1)) ** -0.5, 0.75, ((0, 4),))
    up_weight = scatter_about(arg_keys[4], (D, FF), D ** -0.5, 0.1875, ((1, 4),))
    down_weight = scatter_about(arg_keys[5], (FF, D), FF ** -0.5, 0.09375, ((0, 4),))
    rel_bias = scatter_about(arg_keys[6], (HEADS, NREL), 1.0, 4.0, ((0, 4),), jnp.float32)
    ada_weight = scatter_about(arg_keys[7], (D, 6 * D), D ** -0.5, 0.1875, ((0, 4),))
    ada_bias = scatter_about(arg_keys[8], (6 * D,), 0.5, 3.0, (), jnp.float32)
    class_embed = scatter_about(arg_keys[9], (CLASSES, D), 1.0, 5.0, ((1, 4),), jnp.float32)
    window_clip = draw_window_clip(jax.random.fold_in(arg_keys[13], 71), 0)
    timesteps = touch_ends(jax.random.randint(arg_keys[11], (MICRO, CLIPS), 0, 1000), jax.random.fold_in(arg_keys[11], 1), 0, 999).astype(jnp.int32)
    class_ids = touch_ends(jax.random.randint(arg_keys[12], (MICRO, CLIPS), 0, CLASSES), jax.random.fold_in(arg_keys[12], 1), 0, CLASSES - 1).astype(jnp.int32)
    return {"tokens": tokens, "cotangent": cotangent, "qkv_weight": qkv_weight, "out_weight": out_weight, "up_weight": up_weight, "down_weight": down_weight, "rel_bias": rel_bias, "ada_weight": ada_weight, "ada_bias": ada_bias, "class_embed": class_embed, "window_clip": window_clip, "timesteps": timesteps, "class_ids": class_ids}


epsilon = 1e-06
highest = lax.Precision.HIGHEST

@jax.custom_vjp
def low(v):
    return lax.optimization_barrier(v.astype(jnp.bfloat16)).astype(jnp.float32)

@jax.custom_vjp
def low_back(v):
    return v

def low_keep(v):
    return (low(v), None)

def low_pass(kept, grad):
    return (grad,)

def back_keep(v):
    return (v, None)

def back_low(kept, grad):
    return (low(grad),)
low.defvjp(low_keep, low_pass)
low_back.defvjp(back_keep, back_low)

def layer_norm(values):
    centred = values - lax.optimization_barrier(jnp.mean(values, axis=-1, keepdims=True))
    return centred * lax.rsqrt(lax.optimization_barrier(jnp.mean(centred * centred, axis=-1, keepdims=True)) + epsilon)

def gelu_tanh(values):
    return 0.5 * values * (1.0 + jnp.tanh(0.7978845608028654 * (values + 0.044715 * values * values * values)))

def relative_index():
    places = jnp.arange(WIN_TOK)
    along_time = places // (WIN_H * WIN_W)
    along_rows = places // WIN_W % WIN_H
    along_cols = places % WIN_W
    diff_time = along_time[:, None] - along_time[None, :] + WIN_T - 1
    diff_rows = along_rows[:, None] - along_rows[None, :] + WIN_H - 1
    diff_cols = along_cols[:, None] - along_cols[None, :] + WIN_W - 1
    return ((diff_time * (2 * WIN_H - 1) + diff_rows) * (2 * WIN_W - 1) + diff_cols).astype(jnp.int32)

def step_embedding(steps):
    half_width = D // 2
    frequency = jnp.exp(-math.log(10000.0) * jnp.arange(half_width).astype(jnp.float32) / half_width)
    angle = steps.astype(jnp.float32)[..., None] * frequency
    return jnp.concatenate([jnp.sin(angle), jnp.cos(angle)], axis=-1)

def conditioning(weight_in, bias_in, table_in, step_embed, class_ids):
    condition = step_embed + table_in[class_ids]
    lowered = low(jax.nn.silu(condition))
    return jnp.einsum('mcd,de->mce', lowered, weight_in, precision=highest) + bias_in

def window_block(inputs_f, window_mod, qkv_w, out_w, up_w, down_w, rel_table):
    count_win = inputs_f.shape[0]
    parts = [piece[:, None, :] for piece in jnp.split(window_mod, 6, axis=-1)]
    shift_one, scale_one, gate_one, shift_two, scale_two, gate_two = parts
    normed_one = layer_norm(inputs_f)
    attn_in = low(normed_one * (1.0 + scale_one) + shift_one)
    projected = low_back(low(jnp.einsum('wid,sde->swie', attn_in, qkv_w, precision=highest)))
    queries = projected[0].reshape(count_win, WIN_TOK, HEADS, HEAD_DIM)
    keys_in = projected[1].reshape(count_win, WIN_TOK, HEADS, HEAD_DIM)
    values_in = projected[2].reshape(count_win, WIN_TOK, HEADS, HEAD_DIM)
    bias_table = rel_table[:, relative_index()]
    scores = jnp.einsum('wihd,wjhd->whij', queries, keys_in, precision=highest) * HEAD_DIM ** (-0.5) + bias_table[None]
    scores = low_back(scores)
    row_max = lax.optimization_barrier(jnp.max(scores, axis=-1, keepdims=True))
    exponent = jnp.exp(scores - row_max)
    probs = exponent / lax.optimization_barrier(jnp.sum(exponent, axis=-1, keepdims=True))
    mixed = jnp.einsum('whij,wjhd->wihd', low(probs), values_in, precision=highest)
    mixed = low_back(low(mixed)).reshape(count_win, WIN_TOK, D)
    attn_out = low_back(jnp.einsum('wie,ed->wid', mixed, out_w, precision=highest))
    resid = inputs_f + gate_one * attn_out
    normed_two = layer_norm(resid)
    mlp_in = low(normed_two * (1.0 + scale_two) + shift_two)
    hidden = low_back(jnp.einsum('wid,df->wif', mlp_in, up_w, precision=highest))
    activated = low(gelu_tanh(hidden))
    mlp_out = low_back(jnp.einsum('wif,fd->wid', activated, down_w, precision=highest))
    return resid + gate_two * mlp_out

def reference(tokens, cotangent, qkv_weight, out_weight, up_weight, down_weight, rel_bias, ada_weight, ada_bias, class_embed, window_clip, timesteps, class_ids):
    weights = (qkv_weight.astype(jnp.float32), out_weight.astype(jnp.float32), up_weight.astype(jnp.float32), down_weight.astype(jnp.float32), rel_bias.astype(jnp.float32))
    step_embed = step_embedding(timesteps)
    modulation, cond_back = jax.vjp(lambda weight_in, bias_in, table_in: conditioning(weight_in, bias_in, table_in, step_embed, class_ids), ada_weight.astype(jnp.float32), ada_bias.astype(jnp.float32), class_embed.astype(jnp.float32))
    group_size = 8
    block_count = MICRO * WINDOWS // group_size
    token_blocks = tokens.reshape(block_count, group_size, WIN_TOK, D)
    cot_blocks = cotangent.reshape(block_count, group_size, WIN_TOK, D)
    clip_blocks = window_clip.reshape(block_count, group_size).astype(jnp.int32)
    micro_of = (jnp.arange(block_count) // (WINDOWS // group_size)).astype(jnp.int32)

    def one_block(carried, item_in):
        grads, mod_grad = carried
        token_in, cot_in, clip_in, micro_in = item_in
        window_mod = modulation[micro_in][clip_in]
        result, back_fn = jax.vjp(window_block, token_in.astype(jnp.float32), window_mod, *weights)
        cots = back_fn(cot_in.astype(jnp.float32))
        mod_grad = mod_grad.at[micro_in, clip_in].add(cots[1])
        grads = tuple((total + extra for total, extra in zip(grads, cots[2:])))
        return ((grads, mod_grad), (result.astype(jnp.bfloat16), cots[0].astype(jnp.bfloat16)))
    zeros_in = (tuple((jnp.zeros(weight.shape, jnp.float32) for weight in weights)), jnp.zeros((MICRO, CLIPS, 6 * D), jnp.float32))
    (grads, mod_grad), (outputs, token_grads) = lax.scan(one_block, zeros_in, (token_blocks, cot_blocks, clip_blocks, micro_of))
    ada_w_grad, ada_b_grad, class_table_grad = cond_back(mod_grad)
    return (outputs.reshape(MICRO, ROWS, D), token_grads.reshape(MICRO, ROWS, D), grads[0], grads[1], grads[2], grads[3], grads[4], ada_w_grad, ada_b_grad, class_table_grad)
```

```python
import functools
import math

import jax
import jax.numpy as jnp
from jax import lax
from jax.experimental import pallas as pl
from jax.experimental.pallas import tpu as pltpu
from jax.sharding import PartitionSpec as P

WIN_T = 5
WIN_H = 8
WIN_W = 8
WIN_TOK = WIN_T * WIN_H * WIN_W
FRAME = WIN_H * WIN_W
PAD_TOK = 384
HEAD_DIM = 64
N_TIME, N_ROW, N_COL = 2 * WIN_T - 1, 2 * WIN_H - 1, 2 * WIN_W - 1

BF = jnp.bfloat16
F32 = jnp.float32
epsilon = 1e-06
highest = lax.Precision.HIGHEST
GELU_A = 0.7978845608028654
GELU_B = GELU_A * 0.044715
VMEM_LIMIT = 60 * 1024 * 1024


def dot(left, right, left_dim=1, right_dim=0):
    return lax.dot_general(
        left, right, (((left_dim,), (right_dim,)), ((), ())), preferred_element_type=F32
    )


def params():
    return pltpu.CompilerParams(vmem_limit_bytes=VMEM_LIMIT)


def shaped(shape, dtype):
    return jax.ShapeDtypeStruct(shape, dtype)


def row_spec(rows, cols):
    return pl.BlockSpec((rows, cols), lambda i: (i, 0))


def part_spec(rows, cols):
    return pl.BlockSpec((3, rows, cols), lambda i: (0, i, 0))


def whole_spec(shape):
    return pl.BlockSpec(shape, lambda i: (0,) * len(shape))


def mod_spec(count, cols):
    return pl.BlockSpec((None, count, cols), lambda i: (i, 0, 0))


def cost(flops, nbytes, transcendentals=0):
    return pl.CostEstimate(
        flops=int(flops), bytes_accessed=int(nbytes), transcendentals=int(transcendentals)
    )


def normalise(values):
    centred = values - jnp.mean(values, axis=-1, keepdims=True)
    inverse = lax.rsqrt(jnp.mean(centred * centred, axis=-1, keepdims=True) + epsilon)
    return centred * inverse, inverse


def normalise_back(normed, inverse, grad_in):
    return inverse * (
        grad_in
        - jnp.mean(grad_in, axis=-1, keepdims=True)
        - normed * jnp.mean(grad_in * normed, axis=-1, keepdims=True)
    )


def swap(value, axis, size, bit):
    return lax.ppermute(value, axis, [(i, i ^ bit) for i in range(size)])


def bits_of(size):
    return [1 << b for b in range(size.bit_length() - 1)]


def add_low(left, right):
    return (left.astype(F32) + right.astype(F32)).astype(left.dtype)


def gather_shards(own, axis, size):
    shards = {0: own}
    for bit in bits_of(size):
        for mask in list(shards):
            shards[mask ^ bit] = swap(shards[mask], axis, size, bit)
    return shards


def reduce_shards(terms, axis, size):
    terms = dict(terms)
    for bit in bits_of(size):
        for mask in [m for m in terms if m & bit]:
            terms[mask ^ bit] = add_low(terms[mask ^ bit], swap(terms.pop(mask), axis, size, bit))
    return terms[0]


def reduce_all(value, axis, size):
    for bit in bits_of(size):
        value = add_low(value, swap(value, axis, size, bit))
    return value


def reduce_split(value, axis, size):
    index = lax.axis_index(axis)
    for bit in bits_of(size):
        half = value.shape[0] // 2
        mine = (index // bit) % 2
        keep = lax.dynamic_slice_in_dim(value, mine * half, half, 0)
        send = lax.dynamic_slice_in_dim(value, (1 - mine) * half, half, 0)
        value = add_low(keep, swap(send, axis, size, bit))
    for bit in reversed(bits_of(size)):
        other = swap(value, axis, size, bit)
        first = (index // bit) % 2 == 0
        value = jnp.where(
            first,
            jnp.concatenate([value, other], axis=0),
            jnp.concatenate([other, value], axis=0),
        )
    return value


def place_hot():
    place = jnp.arange(FRAME)
    row, col = place // WIN_W, place % WIN_W
    offset = (row[:, None] - row[None, :] + WIN_H - 1) * N_COL + (
        col[:, None] - col[None, :] + WIN_W - 1
    )
    return (offset.reshape(1, -1) == jnp.arange(N_ROW * N_COL)[:, None]).astype(F32)


def bias_strips(rel_table):
    heads = rel_table.shape[0]

    def strip(cube):
        blocks = lax.dot(cube.reshape(heads * N_TIME, N_ROW * N_COL), place_hot(), precision=highest)
        blocks = blocks.reshape(heads, N_TIME, FRAME, FRAME)[:, ::-1]
        blocks = blocks.transpose(0, 2, 1, 3).reshape(heads, FRAME, N_TIME * FRAME)
        return jnp.pad(blocks, ((0, 0), (0, 0), (0, FRAME)))

    cube = rel_table.reshape(heads, N_TIME, N_ROW * N_COL)
    return strip(cube), strip(cube[:, ::-1, ::-1])


def collect_strips(strip_grad):
    heads = strip_grad.shape[0]
    blocks = strip_grad[:, :, : N_TIME * FRAME].reshape(heads, FRAME, N_TIME, FRAME)
    blocks = blocks.transpose(0, 2, 1, 3).reshape(heads * N_TIME, FRAME * FRAME)
    cube = lax.dot_general(blocks, place_hot(), (((1,), (1,)), ((), ())), precision=highest)
    return cube.reshape(heads, N_TIME, N_ROW * N_COL)[:, :, ::-1].reshape(heads, -1)


def strip_column(frame):
    return (WIN_T - 1 - frame) * FRAME


def spread_strips(strip_ref, table, fill):
    for head in range(table.shape[0]):
        strip = strip_ref[head]
        for frame in range(WIN_T):
            column = strip_column(frame)
            table[head, frame * FRAME : (frame + 1) * FRAME, :WIN_TOK] = strip[
                :, column : column + WIN_TOK
            ]
        table[head, :, WIN_TOK:] = jnp.full((WIN_TOK, PAD_TOK - WIN_TOK), fill, F32)


def norm_kernel(tokens_ref, mod_ref, attn_in_ref):
    normed, _ = normalise(tokens_ref[...].astype(F32))
    attn_in_ref[...] = (normed * (1.0 + mod_ref[1:2]) + mod_ref[0:1]).astype(BF)


def norm_call(tokens, mods):
    rows, width = tokens.shape
    return pl.pallas_call(
        norm_kernel,
        grid=(rows // WIN_TOK,),
        in_specs=[row_spec(WIN_TOK, width), mod_spec(mods.shape[1], width)],
        out_specs=row_spec(WIN_TOK, width),
        out_shape=shaped((rows, width), BF),
        compiler_params=params(),
        cost_estimate=cost(10 * rows * width, 4 * rows * width),
        name="norm_in",
    )(tokens, mods)


def head_copies(value, heads):
    if heads == 1:
        return [value]
    lane = lax.broadcasted_iota(jnp.int32, value.shape, 1) // HEAD_DIM
    return [jnp.where(lane == head, value, jnp.zeros_like(value)) for head in range(heads)]


def pad_rows(value):
    return jnp.concatenate(
        [value, jnp.zeros((PAD_TOK - WIN_TOK, value.shape[1]), value.dtype)], axis=0
    )


def attend_kernel(x_ref, w_ref, strip_ref, qkv_ref, mixed_ref, lse_ref, table, columns):
    heads = strip_ref.shape[0]

    @pl.when(pl.program_id(0) == 0)
    def _():
        spread_strips(strip_ref, table, -1e30)
        columns[...] = jnp.zeros_like(columns)

    x = x_ref[...]
    query = dot(x, w_ref[0]).astype(BF)
    key = dot(x, w_ref[1]).astype(BF)
    value = dot(x, w_ref[2]).astype(BF)
    qkv_ref[0] = query
    qkv_ref[1] = key
    qkv_ref[2] = value
    scaled = query * jnp.asarray(HEAD_DIM**-0.5, BF)
    scores = dot(jnp.concatenate(head_copies(scaled, heads), axis=0), pad_rows(key), 1, 1)
    probs = []
    for head in range(heads):
        score = scores[head * WIN_TOK : (head + 1) * WIN_TOK] + table[head]
        top = jnp.max(score, axis=1, keepdims=True)
        exponent = jnp.exp(score - top)
        total = jnp.sum(exponent, axis=1, keepdims=True)
        probs.append((exponent * (1.0 / total)).astype(BF))
        columns[:WIN_TOK, head : head + 1] = top + jnp.log(total)
    values = jnp.concatenate([pad_rows(part) for part in head_copies(value, heads)], axis=0)
    mixed_ref[...] = dot(jnp.concatenate(probs, axis=1), values).astype(BF)
    lse_ref[...] = columns[...].T[: lse_ref.shape[0]]


def attend_call(attn_in, weight, strip):
    rows, width = attn_in.shape
    cols = weight.shape[2]
    heads = strip.shape[0]
    windows = rows // WIN_TOK
    stat_rows = -(-heads // 8) * 8
    return pl.pallas_call(
        attend_kernel,
        grid=(windows,),
        in_specs=[row_spec(WIN_TOK, width), whole_spec(weight.shape), whole_spec(strip.shape)],
        out_specs=[
            part_spec(WIN_TOK, cols),
            row_spec(WIN_TOK, cols),
            mod_spec(stat_rows, PAD_TOK),
        ],
        out_shape=[
            shaped((3, rows, cols), BF),
            shaped((rows, cols), BF),
            shaped((windows, stat_rows, PAD_TOK), F32),
        ],
        scratch_shapes=[
            pltpu.VMEM((heads, WIN_TOK, PAD_TOK), F32),
            pltpu.VMEM((PAD_TOK, 128), F32),
        ],
        compiler_params=params(),
        cost_estimate=cost(
            6 * rows * width * cols + 16 * rows * PAD_TOK * cols, 2 * rows * width + 8 * rows * cols
        ),
        name="attend",
    )(attn_in, weight, strip)


def attend_back_kernel(
    grad_ref, out_w_ref, qkv_ref, mixed_ref, lse_ref, strip_ref, dqkv_ref, dstrip_ref, table, total
):
    heads = strip_ref.shape[0]
    cols = out_w_ref.shape[0]
    step = pl.program_id(0)

    @pl.when(step == 0)
    def _():
        spread_strips(strip_ref, table, 0.0)
        total[...] = jnp.zeros_like(total)

    grad_mixed = dot(grad_ref[...], out_w_ref[...], 1, 1).astype(BF)
    query = qkv_ref[0]
    key = qkv_ref[1]
    value = qkv_ref[2]
    scale = jnp.asarray(HEAD_DIM**-0.5, BF)
    product = grad_mixed.astype(F32) * mixed_ref[...].astype(F32)
    upper = product.astype(BF)
    lower = (product - upper.astype(F32)).astype(BF)
    head_rows = (lse_ref.shape[0], cols)
    head_hot = (
        lax.broadcasted_iota(jnp.int32, head_rows, 1) // HEAD_DIM
        == lax.broadcasted_iota(jnp.int32, head_rows, 0)
    ).astype(BF)
    inner = dot(head_hot, pad_rows(upper), 1, 1) + dot(head_hot, pad_rows(lower), 1, 1)
    keys = jnp.concatenate(head_copies(key * scale, heads), axis=0)
    values = jnp.concatenate(head_copies(value, heads), axis=0)
    query_pad = pad_rows(query)
    grad_pad = pad_rows(grad_mixed)
    scores = dot(keys, query_pad, 1, 1)
    grad_probs = dot(values, grad_pad, 1, 1)
    probs = []
    grad_scores = []
    for head in range(heads):
        span = slice(head * WIN_TOK, (head + 1) * WIN_TOK)
        prob = jnp.exp(scores[span] + table[head] - lse_ref[head : head + 1, :])
        grad_score = (prob * (grad_probs[span] - inner[head : head + 1, :])).astype(BF)
        probs.append(prob.astype(BF))
        grad_scores.append(grad_score)
        total[head] += grad_score.astype(F32)
    wide = jnp.concatenate(grad_scores, axis=1)
    grad_value = dot(
        jnp.concatenate(probs, axis=1), jnp.concatenate(head_copies(grad_pad, heads), axis=0)
    )
    grad_key = dot(wide, jnp.concatenate(head_copies(query_pad * scale, heads), axis=0))
    grad_query = dot(jnp.concatenate(grad_scores, axis=0), keys, 0, 0)[:WIN_TOK]
    dqkv_ref[0] = grad_query.astype(BF)
    dqkv_ref[1] = grad_key.astype(BF)
    dqkv_ref[2] = grad_value.astype(BF)

    @pl.when(step == pl.num_programs(0) - 1)
    def _():
        dstrip_ref[...] = jnp.zeros_like(dstrip_ref)
        for head in range(heads):
            for frame in range(WIN_T):
                column = strip_column(frame)
                dstrip_ref[head, :, column : column + WIN_TOK] += total[
                    head, frame * FRAME : (frame + 1) * FRAME, :WIN_TOK
                ]


def attend_back_call(grad_attn, out_weight, qkv, mixed, lse, strip):
    rows, width = grad_attn.shape
    cols = out_weight.shape[0]
    heads = strip.shape[0]
    return pl.pallas_call(
        attend_back_kernel,
        grid=(rows // WIN_TOK,),
        in_specs=[
            row_spec(WIN_TOK, width),
            whole_spec(out_weight.shape),
            part_spec(WIN_TOK, cols),
            row_spec(WIN_TOK, cols),
            mod_spec(lse.shape[1], PAD_TOK),
            whole_spec(strip.shape),
        ],
        out_specs=[part_spec(WIN_TOK, cols), whole_spec(strip.shape)],
        out_shape=[shaped((3, rows, cols), BF), shaped(strip.shape, F32)],
        scratch_shapes=[pltpu.VMEM((heads, WIN_TOK, PAD_TOK), F32)] * 2,
        compiler_params=params(),
        cost_estimate=cost(
            2 * rows * width * cols + 40 * rows * PAD_TOK * cols, 2 * rows * width + 14 * rows * cols
        ),
        name="attend_back",
    )(grad_attn, out_weight, qkv, mixed, lse, strip)


def middle_kernel(*refs, count):
    mixed_refs = refs[:count]
    weight_refs = refs[count : 2 * count]
    tokens_ref, cot_ref, mod_ref, attn_out_ref, mlp_in_ref, grad_mlp_ref = refs[2 * count :]
    attn_out = dot(mixed_refs[0][...], weight_refs[0][...])
    for mixed_ref, weight_ref in zip(mixed_refs[1:], weight_refs[1:]):
        attn_out = attn_out + dot(mixed_ref[...], weight_ref[...])
    attn_out_ref[...] = attn_out
    resid = tokens_ref[...].astype(F32) + mod_ref[2:3] * attn_out
    normed, _ = normalise(resid)
    mlp_in_ref[...] = (normed * (1.0 + mod_ref[4:5]) + mod_ref[3:4]).astype(BF)
    grad_mlp_ref[...] = (mod_ref[5:6] * cot_ref[...].astype(F32)).astype(BF)


def middle_call(mixed, weights, tokens, cotangent, mods):
    rows, width = tokens.shape
    count = len(mixed)
    row = row_spec(WIN_TOK, width)
    return pl.pallas_call(
        functools.partial(middle_kernel, count=count),
        grid=(rows // WIN_TOK,),
        in_specs=[row_spec(WIN_TOK, part.shape[1]) for part in mixed]
        + [whole_spec(part.shape) for part in weights]
        + [row, row, mod_spec(mods.shape[1], width)],
        out_specs=[row, row, row],
        out_shape=[
            shaped((rows, width), F32),
            shaped((rows, width), BF),
            shaped((rows, width), BF),
        ],
        compiler_params=params(),
        cost_estimate=cost(2 * rows * width * width, 16 * rows * width),
        name="middle",
    )(*mixed, *weights, tokens, cotangent, mods)


def mlp_kernel(*refs, chunk, first):
    if first:
        x_ref, g_ref, up_ref, down_ref, out_ref, gin_ref, ddown_ref, dup_ref = refs[:8]
    else:
        x_ref, g_ref, up_ref, down_ref, out_in, gin_in, out_ref, gin_ref, ddown_ref, dup_ref = refs[
            :10
        ]
    act, ghid, down_total, up_total = refs[-4:]
    step = pl.program_id(0)
    hidden_width = up_ref.shape[1]
    x = x_ref[...]
    g = g_ref[...]
    for start in range(0, hidden_width, chunk):
        span = slice(start, start + chunk)
        hidden = dot(x, up_ref[:, span])
        grad_act = dot(g, down_ref[span, :], 1, 1)
        square = hidden * hidden
        tanh = jnp.tanh(hidden * (GELU_A + GELU_B * square))
        half = 0.5 * hidden
        act[:, span] = (half + half * tanh).astype(BF)
        slope = 0.5 + 0.5 * tanh + half * (1.0 - tanh * tanh) * (GELU_A + 3.0 * GELU_B * square)
        ghid[:, span] = (grad_act * slope).astype(BF)
    out = dot(act[...], down_ref[...])
    gin = dot(ghid[...], up_ref[...], 1, 1)
    if first:
        out_ref[...] = out
        gin_ref[...] = gin
    else:
        out_ref[...] = out_in[...] + out
        gin_ref[...] = gin_in[...] + gin

    @pl.when(step == 0)
    def _():
        down_total[...] = dot(act[...], g, 0, 0)
        up_total[...] = dot(x, ghid[...], 0, 0)

    @pl.when(step > 0)
    def _():
        down_total[...] += dot(act[...], g, 0, 0)
        up_total[...] += dot(x, ghid[...], 0, 0)

    @pl.when(step == pl.num_programs(0) - 1)
    def _():
        ddown_ref[...] = down_total[...].astype(BF)
        dup_ref[...] = up_total[...].astype(BF)


def mlp_call(x, g, up, down, sums):
    rows, width = x.shape
    hidden = up.shape[1]
    block = 512 if rows % 512 == 0 else WIN_TOK
    row = row_spec(block, width)
    first = sums is None
    extra = () if first else tuple(sums)
    return pl.pallas_call(
        functools.partial(mlp_kernel, chunk=min(512, hidden), first=first),
        grid=(rows // block,),
        in_specs=[row, row, whole_spec(up.shape), whole_spec(down.shape)] + [row] * len(extra),
        out_specs=[row, row, whole_spec(down.shape), whole_spec(up.shape)],
        out_shape=[
            shaped((rows, width), F32),
            shaped((rows, width), F32),
            shaped(down.shape, BF),
            shaped(up.shape, BF),
        ],
        scratch_shapes=[
            pltpu.VMEM((block, hidden), BF),
            pltpu.VMEM((block, hidden), BF),
            pltpu.VMEM(down.shape, F32),
            pltpu.VMEM(up.shape, F32),
        ],
        input_output_aliases={} if first else {4: 0, 5: 1},
        compiler_params=params(),
        cost_estimate=cost(
            12 * rows * width * hidden, 20 * rows * width + 8 * width * hidden, rows * hidden
        ),
        name="mlp",
    )(x, g, up, down, *extra)


def middle_back_kernel(
    tokens_ref, cot_ref, attn_out_ref, mlp_out_ref, gin_ref, mod_ref, out_ref, gres_ref, gattn_ref, sums_ref
):
    cot = cot_ref[...].astype(F32)
    attn_out = attn_out_ref[...]
    mlp_out = mlp_out_ref[...]
    gin = gin_ref[...]
    resid = tokens_ref[...].astype(F32) + mod_ref[2:3] * attn_out
    out_ref[...] = (resid + mod_ref[5:6] * mlp_out).astype(BF)
    normed, inverse = normalise(resid)
    gres = cot + normalise_back(normed, inverse, gin * (1.0 + mod_ref[4:5]))
    gres_ref[...] = gres
    gattn_ref[...] = (mod_ref[2:3] * gres).astype(BF)
    sums_ref[0:1] = jnp.sum(gres * attn_out, axis=0, keepdims=True)
    sums_ref[1:2] = jnp.sum(gin, axis=0, keepdims=True)
    sums_ref[2:3] = jnp.sum(gin * normed, axis=0, keepdims=True)
    sums_ref[3:4] = jnp.sum(cot * mlp_out, axis=0, keepdims=True)


def middle_back_call(tokens, cotangent, attn_out, mlp_out, gin, mods):
    rows, width = tokens.shape
    row = row_spec(WIN_TOK, width)
    windows = rows // WIN_TOK
    return pl.pallas_call(
        middle_back_kernel,
        grid=(windows,),
        in_specs=[row] * 5 + [mod_spec(mods.shape[1], width)],
        out_specs=[row, row, row, mod_spec(4, width)],
        out_shape=[
            shaped((rows, width), BF),
            shaped((rows, width), F32),
            shaped((rows, width), BF),
            shaped((windows, 4, width), F32),
        ],
        compiler_params=params(),
        cost_estimate=cost(40 * rows * width, 24 * rows * width),
        name="middle_back",
    )(tokens, cotangent, attn_out, mlp_out, gin, mods)


def last_kernel(*refs, count):
    dqkv_refs = refs[:count]
    weight_refs = refs[count : 2 * count]
    tokens_ref, gres_ref, mod_ref, out_ref, sums_ref = refs[2 * count :]
    gin = None
    for dqkv_ref, weight_ref in zip(dqkv_refs, weight_refs):
        for part in range(3):
            term = dot(dqkv_ref[part], weight_ref[part], 1, 1)
            gin = term if gin is None else gin + term
    normed, inverse = normalise(tokens_ref[...].astype(F32))
    out_ref[...] = (
        gres_ref[...] + normalise_back(normed, inverse, gin * (1.0 + mod_ref[1:2]))
    ).astype(BF)
    sums_ref[0:1] = jnp.sum(gin, axis=0, keepdims=True)
    sums_ref[1:2] = jnp.sum(gin * normed, axis=0, keepdims=True)


def last_call(dqkv, weights, tokens, gres, mods):
    rows, width = tokens.shape
    count = len(dqkv)
    row = row_spec(WIN_TOK, width)
    windows = rows // WIN_TOK
    return pl.pallas_call(
        functools.partial(last_kernel, count=count),
        grid=(windows,),
        in_specs=[part_spec(WIN_TOK, part.shape[2]) for part in dqkv]
        + [whole_spec(part.shape) for part in weights]
        + [row, row, mod_spec(mods.shape[1], width)],
        out_specs=[row, mod_spec(2, width)],
        out_shape=[shaped((rows, width), BF), shaped((windows, 2, width), F32)],
        compiler_params=params(),
        cost_estimate=cost(6 * rows * width * width, 16 * rows * width),
        name="last",
    )(*dqkv, *weights, tokens, gres, mods)


def body(
    n_dp,
    n_mp,
    tokens,
    cotangent,
    qkv_weight,
    out_weight,
    up_weight,
    down_weight,
    rel_bias,
    ada_weight,
    ada_bias,
    class_embed,
    window_clip,
    timesteps,
    class_ids,
):
    mp_index = lax.axis_index("mp")
    micro, local_rows, width = tokens.shape
    local_cols = class_embed.shape[1]
    clips = timesteps.shape[1]
    own_windows = local_rows // WIN_TOK
    rows = micro * local_rows
    tokens_flat = tokens.reshape(rows, width)
    cot_flat = cotangent.reshape(rows, width)
    masks = range(n_mp)
    order = sorted(masks, key=lambda m: int(format(m, "010b")[::-1], 2), reverse=True)

    columns = mp_index * local_cols + jnp.arange(local_cols)
    half_width = width // 2
    freq_index = (columns % half_width).astype(F32)
    frequency = jnp.exp(-math.log(10000.0) * freq_index / half_width)
    angle = timesteps.astype(F32)[..., None] * frequency
    step_embed = jnp.where(columns < half_width, jnp.sin(angle), jnp.cos(angle))
    class_hot = (class_ids[..., None] == jnp.arange(class_embed.shape[0])).astype(F32)
    condition = step_embed + jnp.einsum("mck,kd->mcd", class_hot, class_embed, precision=highest)
    lowered = jax.nn.silu(condition).astype(BF)
    mod_terms = jnp.einsum("mcd,de->mce", lowered, ada_weight, preferred_element_type=F32)
    modulation = reduce_all(mod_terms, "mp", n_mp) + ada_bias
    own_clip = lax.dynamic_slice_in_dim(window_clip, mp_index * own_windows, own_windows, 1)
    clip_hot = (own_clip[..., None] == jnp.arange(clips)).astype(F32)
    mods = jnp.einsum("mwc,mce->mwe", clip_hot, modulation, precision=highest)
    mods = mods.reshape(micro * own_windows, 6, width)

    qkv_w = gather_shards(qkv_weight, "mp", n_mp)
    rel_tables = gather_shards(rel_bias, "mp", n_mp)
    out_w = gather_shards(out_weight, "mp", n_mp)
    up_w = gather_shards(up_weight, "mp", n_mp)
    down_w = gather_shards(down_weight, "mp", n_mp)
    heads = rel_bias.shape[0]
    strips, strips_back = bias_strips(jnp.concatenate([rel_tables[m] for m in masks], axis=0))

    attn_in = norm_call(tokens_flat, mods)
    qkv, mixed, lse = {}, {}, {}
    for m in masks:
        qkv[m], mixed[m], lse[m] = attend_call(
            attn_in, qkv_w[m], strips[m * heads : (m + 1) * heads]
        )
    attn_out, mlp_in, grad_mlp = middle_call(
        [mixed[m] for m in masks], [out_w[m] for m in masks], tokens_flat, cot_flat, mods
    )
    sums = None
    down_terms, up_terms = {}, {}
    for m in order:
        mlp_out, gin, down_terms[m], up_terms[m] = mlp_call(
            mlp_in, grad_mlp, up_w[m], down_w[m], sums
        )
        sums = (mlp_out, gin)
    block_out, grad_resid, grad_attn, late_sums = middle_back_call(
        tokens_flat, cot_flat, attn_out, mlp_out, gin, mods
    )

    dqkv, qkv_terms, out_terms, rel_terms = {}, {}, {}, {}
    for m in order:
        out_terms[m] = dot(mixed[m], grad_attn, 0, 0).astype(BF)
        dqkv[m], strip_grad = attend_back_call(
            grad_attn, out_w[m], qkv[m], mixed[m], lse[m], strips_back[m * heads : (m + 1) * heads]
        )
        rel_terms[m] = collect_strips(strip_grad).astype(BF)
        qkv_terms[m] = jnp.einsum(
            "rd,sre->sde", attn_in, dqkv[m], preferred_element_type=F32
        ).astype(BF)
    token_grad, early_sums = last_call(
        [dqkv[m] for m in masks], [qkv_w[m] for m in masks], tokens_flat, grad_resid, mods
    )

    def total(terms):
        shard = reduce_shards(terms, "mp", n_mp)
        flat = shard.reshape(-1, shard.shape[-1])
        return reduce_split(flat, "dp", n_dp).reshape(shard.shape).astype(F32)

    down_grad = total(down_terms)
    up_grad = total(up_terms)
    out_grad = total(out_terms)
    qkv_grad = total(qkv_terms)
    rel_grad = reduce_all(reduce_shards(rel_terms, "mp", n_mp), "dp", n_dp).astype(F32)

    def clip_sums(window_sums):
        count = window_sums.shape[1]
        grouped = window_sums.reshape(micro, own_windows, count * width)
        part = jnp.einsum("mwc,mwe->mce", clip_hot, grouped, precision=highest).astype(BF)
        part = reduce_all(reduce_all(part, "mp", n_mp), "dp", n_dp)
        return part.astype(F32).reshape(micro, clips, count, width)

    late = clip_sums(late_sums)
    early = clip_sums(early_sums)
    mod_total = jnp.concatenate(
        [early, late[:, :, 0:1], late[:, :, 1:4]], axis=2
    ).reshape(micro, clips, 6 * width)
    ada_bias_grad = jnp.sum(mod_total, axis=(0, 1))
    ada_weight_grad = jnp.einsum(
        "mcd,mce->de", lowered.astype(F32), mod_total, precision=highest
    )
    grad_lowered = jnp.einsum(
        "mce,de->mcd", mod_total, ada_weight.astype(F32), precision=highest
    )
    grad_condition = jax.vjp(jax.nn.silu, condition)[1](grad_lowered)[0]
    class_grad = jnp.einsum("mck,mcd->kd", class_hot, grad_condition, precision=highest)
    return (
        block_out.reshape(tokens.shape),
        token_grad.reshape(tokens.shape),
        qkv_grad,
        out_grad,
        up_grad,
        down_grad,
        rel_grad,
        ada_weight_grad,
        ada_bias_grad,
        class_grad,
    )


def solution(mesh):
    rows = P(None, ("dp", "mp"), None)
    in_specs = (
        rows,
        rows,
        P(None, None, "mp"),
        P("mp", None),
        P(None, "mp"),
        P("mp", None),
        P("mp", None),
        P("mp", None),
        P(),
        P(None, "mp"),
        P(None, "dp"),
        P(),
        P(),
    )
    out_specs = (
        rows,
        rows,
        P(None, None, "mp"),
        P("mp", None),
        P(None, "mp"),
        P("mp", None),
        P("mp", None),
        P("mp", None),
        P(),
        P(None, "mp"),
    )
    step = functools.partial(body, mesh.shape["dp"], mesh.shape["mp"])
    return jax.shard_map(step, mesh=mesh, in_specs=in_specs, out_specs=out_specs, check_vma=False)
```

```python
import functools
import math

import jax
import jax.numpy as jnp
from jax import lax
from jax.experimental import pallas as pl
from jax.experimental.pallas import tpu as pltpu
from jax.sharding import PartitionSpec as P

WIN_T = 5
WIN_H = 8
WIN_W = 8
WIN_TOK = WIN_T * WIN_H * WIN_W
FRAME = WIN_H * WIN_W
PAD_TOK = 384
HEAD_DIM = 64
N_TIME, N_ROW, N_COL = 2 * WIN_T - 1, 2 * WIN_H - 1, 2 * WIN_W - 1

BF = jnp.bfloat16
F32 = jnp.float32
epsilon = 1e-06
highest = lax.Precision.HIGHEST
GELU_A = 0.7978845608028654
GELU_B = GELU_A * 0.044715
VMEM_LIMIT = 60 * 1024 * 1024


def dot(left, right, left_dim=1, right_dim=0):
    return lax.dot_general(
        left, right, (((left_dim,), (right_dim,)), ((), ())), preferred_element_type=F32
    )


def params():
    return pltpu.CompilerParams(vmem_limit_bytes=VMEM_LIMIT)


def shaped(shape, dtype):
    return jax.ShapeDtypeStruct(shape, dtype)


def row_spec(rows, cols):
    return pl.BlockSpec((rows, cols), lambda i: (i, 0))


def part_spec(rows, cols):
    return pl.BlockSpec((3, rows, cols), lambda i: (0, i, 0))


def whole_spec(shape):
    return pl.BlockSpec(shape, lambda i: (0,) * len(shape))


def mod_spec(count, cols):
    return pl.BlockSpec((None, count, cols), lambda i: (i, 0, 0))


def cost(micros, scale=1.0):
    return pl.CostEstimate(
        flops=int(micros * scale * 1e9), bytes_accessed=int(micros * scale * 3.5e6), transcendentals=0
    )


def call_after(kernel, deps, *, in_specs, **rest):
    deps = tuple(deps)
    count = len(in_specs)

    def run(*refs):
        kernel(*refs[:count], *refs[count + len(deps) :])

    call = pl.pallas_call(
        run, in_specs=list(in_specs) + [pl.BlockSpec(memory_space=pl.ANY)] * len(deps), **rest
    )
    return lambda *args: call(*args, *deps)


def after(value, *deps):
    return lax.optimization_barrier((value, *deps))[0]


def normalise(values):
    centred = values - jnp.mean(values, axis=-1, keepdims=True)
    inverse = lax.rsqrt(jnp.mean(centred * centred, axis=-1, keepdims=True) + epsilon)
    return centred * inverse, inverse


def normalise_back(normed, inverse, grad_in):
    return inverse * (
        grad_in
        - jnp.mean(grad_in, axis=-1, keepdims=True)
        - normed * jnp.mean(grad_in * normed, axis=-1, keepdims=True)
    )


def swap(value, axis, size, bit):
    return lax.ppermute(value, axis, [(i, i ^ bit) for i in range(size)])


def bits_of(size):
    return [1 << b for b in range(size.bit_length() - 1)]


def add_low(left, right):
    return (left.astype(F32) + right.astype(F32)).astype(left.dtype)


def gather_shards(own, axis, size):
    shards = {0: own}
    for bit in reversed(bits_of(size)):
        for mask in list(shards):
            shards[mask ^ bit] = swap(shards[mask], axis, size, bit)
    return shards


def reduce_all(value, axis, size):
    for bit in bits_of(size):
        value = add_low(value, swap(value, axis, size, bit))
    return value


def reduce_shards(terms, axis, size):
    terms = dict(terms)
    for bit in bits_of(size):
        for mask in [m for m in terms if m & bit]:
            terms[mask ^ bit] = add_low(terms[mask ^ bit], swap(terms.pop(mask), axis, size, bit))
    return terms[0]


def add_parts(parts):
    if len(parts) == 1:
        return parts[0]
    total = parts[0].astype(F32)
    for part in parts[1:]:
        total = total + part.astype(F32)
    return total.astype(BF)


def split_kernel(index_ref, *refs, count, terms):
    ins, outs = refs[:terms], refs[terms:]
    size = outs[0].shape[0]
    for k in range(count):
        start = pl.multiple_of((index_ref[0] ^ k) * size, size)
        total = ins[0][pl.ds(start, size), :].astype(F32)
        for ref in ins[1:]:
            total = total + ref[pl.ds(start, size), :].astype(F32)
        outs[k][...] = total.astype(BF)


def split_call(parts, index, count):
    rows, cols = parts[0].shape
    piece = (rows // count, cols)
    spec = pltpu.PrefetchScalarGridSpec(
        num_scalar_prefetch=1,
        grid=(1,),
        in_specs=[pl.BlockSpec((rows, cols), lambda i, f: (0, 0))] * len(parts),
        out_specs=[pl.BlockSpec(piece, lambda i, f: (0, 0))] * count,
    )
    return pl.pallas_call(
        functools.partial(split_kernel, count=count, terms=len(parts)),
        grid_spec=spec,
        out_shape=[shaped(piece, BF)] * count,
        compiler_params=params(),
        cost_estimate=cost(3),
        name="split",
    )(jnp.reshape(index, (1,)).astype(jnp.int32), *parts)


def assemble_kernel(index_ref, *refs):
    for k, ref in enumerate(refs[:-1]):

        @pl.when(pl.program_id(0) == k)
        def _():
            refs[-1][...] = ref[...].astype(F32)


def assemble_call(pieces, index):
    count = len(pieces)
    rows, cols = pieces[0].shape
    far = count // 2

    def place(k, f):
        device = f[0] ^ k
        return ((device % 2) * far + device // 2, 0)

    spec = pltpu.PrefetchScalarGridSpec(
        num_scalar_prefetch=1,
        grid=(count,),
        in_specs=[pl.BlockSpec((rows, cols), lambda k, f: (0, 0))] * count,
        out_specs=pl.BlockSpec((rows, cols), place),
    )
    return pl.pallas_call(
        assemble_kernel,
        grid_spec=spec,
        out_shape=shaped((rows * count, cols), F32),
        compiler_params=params(),
        cost_estimate=cost(4),
        name="assemble",
    )(jnp.reshape(index, (1,)).astype(jnp.int32), *pieces)


class Steps:
    def __init__(self):
        self.jobs, self.token = [], None

    def swap(self, value, axis, size, bit):
        if self.token is not None:
            value = after(value, self.token)
        return swap(value, axis, size, bit)

    def arrive(self, value):
        return value if self.token is None else after(value, self.token)

    def step(self, token=None):
        self.token = token
        ties, jobs = [], []
        for job in self.jobs:
            try:
                ties += next(job)
            except StopIteration:
                continue
            jobs.append(job)
        self.jobs = jobs
        return ties if token is None else ties + [token]

    def finish(self):
        while self.jobs:
            self.step()


def gather_job(steps, own, shards, axis, size, hold):
    shards[0] = own
    even = {0: own}
    shards[1] = steps.swap(own, axis, size, 1)
    for bit in reversed(bits_of(size)[1:]):
        new = {mask ^ bit: steps.swap(part, axis, size, bit) for mask, part in even.items()}
        for _ in range(hold):
            yield []
        new = {mask: steps.arrive(part) for mask, part in new.items()}
        even.update(new)
        for mask, part in new.items():
            shards[mask] = part
            shards[mask ^ 1] = steps.swap(part, axis, size, 1)
        yield list(new.values())


class Sums:
    def __init__(self, steps, size, lag, hold):
        self.steps, self.size, self.lag, self.hold = steps, size, lag, hold
        self.parts = {mask: [] for mask in range(size)}
        nearest_first = sorted(range(1, size), key=lambda mask: (mask & -mask, mask))
        steps.jobs += [self.send(mask) for mask in nearest_first]

    def full(self, mask):
        low = mask & -mask if mask else self.size
        return len(self.parts[mask]) == low.bit_length()

    def add(self, mask, term):
        self.parts[mask].append(term)

    def send(self, mask):
        while not self.full(mask):
            yield []
        bit = mask & -mask
        for _ in range(self.lag if bit > 1 else 0):
            yield []
        other = self.steps.swap(add_parts(self.parts[mask]), "mp", self.size, bit)
        for _ in range(self.hold if bit > 1 else 1):
            yield []
        other = self.steps.arrive(other)
        self.add(mask ^ bit, other)
        yield [other]


def psum_job(sums, n_dp, turn, out, name):
    while not all(part.full(0) for part in sums):
        yield []
    values = [add_parts(part.parts[0]) for part in sums]
    group = [(place + turn) % n_dp for place in range(n_dp)]
    totals = lax.psum(values, "dp", axis_index_groups=[group])
    out[name] = totals
    yield values


def all_job(steps, value, n_mp, n_dp, out, name):
    ready = []
    for axis, size in (("mp", n_mp), ("dp", n_dp)):
        for bit in bits_of(size):
            other = steps.swap(value, axis, size, bit)
            yield ready
            value = add_low(value, steps.arrive(other))
            ready = [value]
    out[name] = value
    yield ready


def spread_job(steps, sums, n_dp, out, name):
    while not sums.full(0):
        yield []
    index = lax.axis_index("dp")
    keep, send = split_call(sums.parts[0], index % 2, 2)
    other = steps.swap(send, "dp", n_dp, 1)
    yield [send]
    other = steps.arrive(other)
    pieces = split_call([keep, other], index // 2, n_dp // 2)
    others = [steps.swap(pieces[k], "dp", n_dp, 2 * k) for k in range(1, n_dp // 2)]
    yield [other]
    total = add_parts([pieces[0]] + others)
    whole = [total] + [steps.swap(total, "dp", n_dp, k) for k in range(1, n_dp)]
    yield others
    yield []
    out[name] = assemble_call(whole, index)
    yield whole


def place_hot():
    place = jnp.arange(FRAME)
    row, col = place // WIN_W, place % WIN_W
    offset = (row[:, None] - row[None, :] + WIN_H - 1) * N_COL + (
        col[:, None] - col[None, :] + WIN_W - 1
    )
    return (offset.reshape(1, -1) == jnp.arange(N_ROW * N_COL)[:, None]).astype(F32)


def bias_blocks(rel_table):
    heads = rel_table.shape[0]
    cube = rel_table.reshape(heads * N_TIME, N_ROW * N_COL)
    return lax.dot(cube, place_hot(), precision=highest).reshape(heads, N_TIME, FRAME, FRAME)


def collect_blocks(block_grad):
    heads = block_grad.shape[0]
    flat = block_grad.reshape(heads * N_TIME, FRAME * FRAME)
    cube = lax.dot_general(flat, place_hot(), (((1,), (1,)), ((), ())), precision=highest)
    return cube[:, ::-1].reshape(heads, -1)


def frame_span(frame):
    return slice(frame * FRAME, (frame + 1) * FRAME)


def spread_blocks(blocks_ref, table, fill, transposed):
    for head in range(table.shape[0]):
        for offset in range(N_TIME):
            block = blocks_ref[head, offset]
            if transposed:
                block = block.T
            for query in range(WIN_T):
                key = query - (offset - WIN_T + 1)
                if 0 <= key < WIN_T:
                    row, col = (key, query) if transposed else (query, key)
                    table[head, frame_span(row), frame_span(col)] = block
        table[head, :, WIN_TOK:] = jnp.full((WIN_TOK, PAD_TOK - WIN_TOK), fill, F32)


def norm_kernel(tokens_ref, mod_ref, attn_in_ref):
    normed, _ = normalise(tokens_ref[...].astype(F32))
    attn_in_ref[...] = (normed * (1.0 + mod_ref[1:2]) + mod_ref[0:1]).astype(BF)


def norm_call(tokens, mods, deps=()):
    rows, width = tokens.shape
    return call_after(
        norm_kernel,
        deps,
        grid=(rows // WIN_TOK,),
        in_specs=[row_spec(WIN_TOK, width), mod_spec(mods.shape[1], width)],
        out_specs=row_spec(WIN_TOK, width),
        out_shape=shaped((rows, width), BF),
        compiler_params=params(),
        cost_estimate=cost(8),
        name="norm_in",
    )(tokens, mods)


def head_copies(value, heads):
    if heads == 1:
        return [value]
    lane = lax.broadcasted_iota(jnp.int32, value.shape, 1) // HEAD_DIM
    return [jnp.where(lane == head, value, jnp.zeros_like(value)) for head in range(heads)]


def pad_rows(value):
    return jnp.concatenate(
        [value, jnp.zeros((PAD_TOK - WIN_TOK, value.shape[1]), value.dtype)], axis=0
    )


def attend_kernel(x_ref, w_ref, blocks_ref, qkv_ref, mixed_ref, lse_ref, table, columns):
    heads = blocks_ref.shape[0]

    @pl.when(pl.program_id(0) == 0)
    def _():
        spread_blocks(blocks_ref, table, -1e30, False)
        columns[...] = jnp.zeros_like(columns)

    x = x_ref[...]
    query = dot(x, w_ref[0]).astype(BF)
    key = dot(x, w_ref[1]).astype(BF)
    value = dot(x, w_ref[2]).astype(BF)
    qkv_ref[0] = query
    qkv_ref[1] = key
    qkv_ref[2] = value
    scaled = query * jnp.asarray(HEAD_DIM**-0.5, BF)
    scores = dot(jnp.concatenate(head_copies(scaled, heads), axis=0), pad_rows(key), 1, 1)
    probs = []
    for head in range(heads):
        score = scores[head * WIN_TOK : (head + 1) * WIN_TOK] + table[head]
        top = jnp.max(score, axis=1, keepdims=True)
        exponent = jnp.exp(score - top)
        total = jnp.sum(exponent, axis=1, keepdims=True)
        probs.append((exponent * (1.0 / total)).astype(BF))
        columns[:WIN_TOK, head : head + 1] = top + jnp.log(total)
    values = jnp.concatenate([pad_rows(part) for part in head_copies(value, heads)], axis=0)
    mixed_ref[...] = dot(jnp.concatenate(probs, axis=1), values).astype(BF)
    lse_ref[...] = columns[...].T[: lse_ref.shape[0]]


def attend_call(attn_in, weight, blocks, deps=()):
    rows, width = attn_in.shape
    cols = weight.shape[2]
    heads = blocks.shape[0]
    windows = rows // WIN_TOK
    stat_rows = -(-heads // 8) * 8
    return call_after(
        attend_kernel,
        deps,
        grid=(windows,),
        in_specs=[row_spec(WIN_TOK, width), whole_spec(weight.shape), whole_spec(blocks.shape)],
        out_specs=[
            part_spec(WIN_TOK, cols),
            row_spec(WIN_TOK, cols),
            mod_spec(stat_rows, PAD_TOK),
        ],
        out_shape=[
            shaped((3, rows, cols), BF),
            shaped((rows, cols), BF),
            shaped((windows, stat_rows, PAD_TOK), F32),
        ],
        scratch_shapes=[
            pltpu.VMEM((heads, WIN_TOK, PAD_TOK), F32),
            pltpu.VMEM((PAD_TOK, 128), F32),
        ],
        compiler_params=params(),
        cost_estimate=cost(19),
        name="attend",
    )(attn_in, weight, blocks)


def attend_back_kernel(
    grad_ref, out_w_ref, qkv_ref, mixed_ref, lse_ref, blocks_ref, x_ref, dqkv_ref, dblocks_ref, dw_ref, table, total, x_all, d_all
):
    heads = blocks_ref.shape[0]
    cols = out_w_ref.shape[0]
    step = pl.program_id(0)

    @pl.when(step == 0)
    def _():
        spread_blocks(blocks_ref, table, 0.0, True)
        total[...] = jnp.zeros_like(total)

    grad_mixed = dot(grad_ref[...], out_w_ref[...], 1, 1).astype(BF)
    query = qkv_ref[0]
    key = qkv_ref[1]
    value = qkv_ref[2]
    scale = jnp.asarray(HEAD_DIM**-0.5, BF)
    product = grad_mixed.astype(F32) * mixed_ref[...].astype(F32)
    upper = product.astype(BF)
    lower = (product - upper.astype(F32)).astype(BF)
    head_rows = (lse_ref.shape[0], cols)
    head_hot = (
        lax.broadcasted_iota(jnp.int32, head_rows, 1) // HEAD_DIM
        == lax.broadcasted_iota(jnp.int32, head_rows, 0)
    ).astype(BF)
    inner = dot(head_hot, pad_rows(upper), 1, 1) + dot(head_hot, pad_rows(lower), 1, 1)
    keys = jnp.concatenate(head_copies(key * scale, heads), axis=0)
    values = jnp.concatenate(head_copies(value, heads), axis=0)
    query_pad = pad_rows(query)
    grad_pad = pad_rows(grad_mixed)
    scores = dot(keys, query_pad, 1, 1)
    grad_probs = dot(values, grad_pad, 1, 1)
    probs = []
    grad_scores = []
    for head in range(heads):
        span = slice(head * WIN_TOK, (head + 1) * WIN_TOK)
        prob = jnp.exp(scores[span] + table[head] - lse_ref[head : head + 1, :])
        grad_score = (prob * (grad_probs[span] - inner[head : head + 1, :])).astype(BF)
        probs.append(prob.astype(BF))
        grad_scores.append(grad_score)
        total[head] += grad_score.astype(F32)
    wide = jnp.concatenate(grad_scores, axis=1)
    grad_value = dot(
        jnp.concatenate(probs, axis=1), jnp.concatenate(head_copies(grad_pad, heads), axis=0)
    )
    grad_key = dot(wide, jnp.concatenate(head_copies(query_pad * scale, heads), axis=0))
    grad_query = dot(jnp.concatenate(grad_scores, axis=0), keys, 0, 0)[:WIN_TOK]
    rows = pl.ds(pl.multiple_of(step * WIN_TOK, WIN_TOK), WIN_TOK)
    x_all[rows, :] = x_ref[...]
    for part, grad in enumerate((grad_query, grad_key, grad_value)):
        grad = grad.astype(BF)
        dqkv_ref[part] = grad
        d_all[part, rows, :] = grad

    @pl.when(step == pl.num_programs(0) - 1)
    def _():
        for part in range(3):
            dw_ref[part] = dot(x_all[...], d_all[part], 0, 0).astype(BF)
        for head in range(heads):
            for offset in range(N_TIME):
                block = None
                for query in range(WIN_T):
                    key = query - (offset - WIN_T + 1)
                    if 0 <= key < WIN_T:
                        part = total[head, frame_span(key), frame_span(query)]
                        block = part if block is None else block + part
                dblocks_ref[head, offset] = block


def attend_back_call(grad_attn, out_weight, qkv, mixed, lse, blocks, attn_in, deps=()):
    rows, width = grad_attn.shape
    cols = out_weight.shape[0]
    heads = blocks.shape[0]
    return call_after(
        attend_back_kernel,
        deps,
        grid=(rows // WIN_TOK,),
        in_specs=[
            row_spec(WIN_TOK, width),
            whole_spec(out_weight.shape),
            part_spec(WIN_TOK, cols),
            row_spec(WIN_TOK, cols),
            mod_spec(lse.shape[1], PAD_TOK),
            whole_spec(blocks.shape),
            row_spec(WIN_TOK, width),
        ],
        out_specs=[
            part_spec(WIN_TOK, cols),
            whole_spec(blocks.shape),
            whole_spec((3, width, cols)),
        ],
        out_shape=[
            shaped((3, rows, cols), BF),
            shaped(blocks.shape, F32),
            shaped((3, width, cols), BF),
        ],
        scratch_shapes=[pltpu.VMEM((heads, WIN_TOK, PAD_TOK), F32)] * 2
        + [pltpu.VMEM((rows, width), BF), pltpu.VMEM((3, rows, cols), BF)],
        compiler_params=params(),
        cost_estimate=cost(30),
        name="attend_back",
    )(grad_attn, out_weight, qkv, mixed, lse, blocks, attn_in)


def middle_kernel(*refs, count):
    mixed_refs = refs[:count]
    weight_refs = refs[count : 2 * count]
    tokens_ref, cot_ref, mod_ref, attn_out_ref, mlp_in_ref, grad_mlp_ref = refs[2 * count :]
    attn_out = dot(mixed_refs[0][...], weight_refs[0][...])
    for mixed_ref, weight_ref in zip(mixed_refs[1:], weight_refs[1:]):
        attn_out = attn_out + dot(mixed_ref[...], weight_ref[...])
    attn_out_ref[...] = attn_out
    resid = tokens_ref[...].astype(F32) + mod_ref[2:3] * attn_out
    normed, _ = normalise(resid)
    mlp_in_ref[...] = (normed * (1.0 + mod_ref[4:5]) + mod_ref[3:4]).astype(BF)
    grad_mlp_ref[...] = (mod_ref[5:6] * cot_ref[...].astype(F32)).astype(BF)


def middle_call(mixed, weights, tokens, cotangent, mods, deps=()):
    rows, width = tokens.shape
    count = len(mixed)
    row = row_spec(WIN_TOK, width)
    return call_after(
        functools.partial(middle_kernel, count=count),
        deps,
        grid=(rows // WIN_TOK,),
        in_specs=[row_spec(WIN_TOK, part.shape[1]) for part in mixed]
        + [whole_spec(part.shape) for part in weights]
        + [row, row, mod_spec(mods.shape[1], width)],
        out_specs=[row, row, row],
        out_shape=[
            shaped((rows, width), F32),
            shaped((rows, width), BF),
            shaped((rows, width), BF),
        ],
        compiler_params=params(),
        cost_estimate=cost(16),
        name="middle",
    )(*mixed, *weights, tokens, cotangent, mods)


def mlp_kernel(*refs, chunk, first):
    x_ref, g_ref, up_ref, down_ref = refs[:4]
    rest = refs[4:] if first else refs[6:]
    out_ref, gin_ref = rest[:2]
    ddown_refs, dup_refs = rest[2:4], rest[4:6]
    down_total, up_total, act, ghid = rest[6:]
    step = pl.program_id(0)
    hidden_width = up_ref.shape[1]
    x = x_ref[...]
    g = g_ref[...]
    for start in range(0, hidden_width, chunk):
        span = slice(start, start + chunk)
        hidden = dot(x, up_ref[:, span])
        grad_act = dot(g, down_ref[span, :], 1, 1)
        square = hidden * hidden
        tanh = jnp.tanh(hidden * (GELU_A + GELU_B * square))
        half = 0.5 * hidden
        act[:, span] = (half + half * tanh).astype(BF)
        slope = 0.5 + 0.5 * tanh + half * (1.0 - tanh * tanh) * (GELU_A + 3.0 * GELU_B * square)
        ghid[:, span] = (grad_act * slope).astype(BF)
    out = dot(act[...], down_ref[...])
    gin = dot(ghid[...], up_ref[...], 1, 1)
    if first:
        out_ref[...] = out
        gin_ref[...] = gin
    else:
        out_ref[...] = refs[4][...] + out
        gin_ref[...] = refs[5][...] + gin

    @pl.when(step == 0)
    def _():
        down_total[...] = dot(act[...], g, 0, 0)
        up_total[...] = dot(x, ghid[...], 0, 0)

    @pl.when(step > 0)
    def _():
        down_total[...] += dot(act[...], g, 0, 0)
        up_total[...] += dot(x, ghid[...], 0, 0)

    @pl.when(step == pl.num_programs(0) - 1)
    def _():
        for total, halves in ((down_total, ddown_refs), (up_total, dup_refs)):
            size = halves[0].shape[0]
            halves[0][...] = total[:size].astype(BF)
            halves[1][...] = total[size:].astype(BF)


def mlp_call(x, g, up, down, sums, deps=()):
    rows, width = x.shape
    hidden = up.shape[1]
    block = 512 if rows % 512 == 0 else WIN_TOK
    row = row_spec(block, width)
    first = sums is None
    extra = () if first else tuple(sums)
    halves = [(hidden // 2, width)] * 2 + [(width // 2, hidden)] * 2
    out = call_after(
        functools.partial(mlp_kernel, chunk=min(512, hidden), first=first),
        deps,
        grid=(rows // block,),
        in_specs=[row, row, whole_spec(up.shape), whole_spec(down.shape)] + [row] * len(extra),
        out_specs=[row, row] + [whole_spec(shape) for shape in halves],
        out_shape=[shaped((rows, width), F32)] * 2 + [shaped(shape, BF) for shape in halves],
        scratch_shapes=[
            pltpu.VMEM(down.shape, F32),
            pltpu.VMEM(up.shape, F32),
            pltpu.VMEM((block, hidden), BF),
            pltpu.VMEM((block, hidden), BF),
        ],
        input_output_aliases={} if first else {4: 0, 5: 1},
        compiler_params=params(),
        cost_estimate=cost(46),
        name="mlp",
    )(x, g, up, down, *extra)
    return out[0], out[1], out[2:]


def middle_back_kernel(
    tokens_ref, cot_ref, attn_out_ref, mlp_out_ref, gin_ref, mod_ref, out_ref, gres_ref, gattn_ref, sums_ref
):
    cot = cot_ref[...].astype(F32)
    attn_out = attn_out_ref[...]
    mlp_out = mlp_out_ref[...]
    gin = gin_ref[...]
    resid = tokens_ref[...].astype(F32) + mod_ref[2:3] * attn_out
    out_ref[...] = (resid + mod_ref[5:6] * mlp_out).astype(BF)
    normed, inverse = normalise(resid)
    gres = cot + normalise_back(normed, inverse, gin * (1.0 + mod_ref[4:5]))
    gres_ref[...] = gres
    gattn_ref[...] = (mod_ref[2:3] * gres).astype(BF)
    sums_ref[0:1] = jnp.sum(gres * attn_out, axis=0, keepdims=True)
    sums_ref[1:2] = jnp.sum(gin, axis=0, keepdims=True)
    sums_ref[2:3] = jnp.sum(gin * normed, axis=0, keepdims=True)
    sums_ref[3:4] = jnp.sum(cot * mlp_out, axis=0, keepdims=True)


def middle_back_call(tokens, cotangent, attn_out, mlp_out, gin, mods, deps=()):
    rows, width = tokens.shape
    row = row_spec(WIN_TOK, width)
    windows = rows // WIN_TOK
    return call_after(
        middle_back_kernel,
        deps,
        grid=(windows,),
        in_specs=[row] * 5 + [mod_spec(mods.shape[1], width)],
        out_specs=[row, row, row, mod_spec(4, width)],
        out_shape=[
            shaped((rows, width), BF),
            shaped((rows, width), F32),
            shaped((rows, width), BF),
            shaped((windows, 4, width), F32),
        ],
        compiler_params=params(),
        cost_estimate=cost(24),
        name="middle_back",
    )(tokens, cotangent, attn_out, mlp_out, gin, mods)


def last_kernel(*refs, count):
    dqkv_refs = refs[:count]
    weight_refs = refs[count : 2 * count]
    tokens_ref, gres_ref, mod_ref, out_ref, sums_ref = refs[2 * count :]
    gin = None
    for dqkv_ref, weight_ref in zip(dqkv_refs, weight_refs):
        for part in range(3):
            term = dot(dqkv_ref[part], weight_ref[part], 1, 1)
            gin = term if gin is None else gin + term
    normed, inverse = normalise(tokens_ref[...].astype(F32))
    out_ref[...] = (
        gres_ref[...] + normalise_back(normed, inverse, gin * (1.0 + mod_ref[1:2]))
    ).astype(BF)
    sums_ref[0:1] = jnp.sum(gin, axis=0, keepdims=True)
    sums_ref[1:2] = jnp.sum(gin * normed, axis=0, keepdims=True)


def last_call(dqkv, weights, tokens, gres, mods, deps=()):
    rows, width = tokens.shape
    count = len(dqkv)
    row = row_spec(WIN_TOK, width)
    windows = rows // WIN_TOK
    return call_after(
        functools.partial(last_kernel, count=count),
        deps,
        grid=(windows,),
        in_specs=[part_spec(WIN_TOK, part.shape[2]) for part in dqkv]
        + [whole_spec(part.shape) for part in weights]
        + [row, row, mod_spec(mods.shape[1], width)],
        out_specs=[row, mod_spec(2, width)],
        out_shape=[shaped((rows, width), BF), shaped((windows, 2, width), F32)],
        compiler_params=params(),
        cost_estimate=cost(28),
        name="last",
    )(*dqkv, *weights, tokens, gres, mods)


def body(
    n_dp,
    n_mp,
    tokens,
    cotangent,
    qkv_weight,
    out_weight,
    up_weight,
    down_weight,
    rel_bias,
    ada_weight,
    ada_bias,
    class_embed,
    window_clip,
    timesteps,
    class_ids,
):
    mp_index = lax.axis_index("mp")
    micro, local_rows, width = tokens.shape
    local_cols = class_embed.shape[1]
    clips = timesteps.shape[1]
    own_windows = local_rows // WIN_TOK
    rows = micro * local_rows
    tokens_flat = tokens.reshape(rows, width)
    cot_flat = cotangent.reshape(rows, width)
    masks = range(n_mp)

    columns = mp_index * local_cols + jnp.arange(local_cols)
    half_width = width // 2
    freq_index = (columns % half_width).astype(F32)
    frequency = jnp.exp(-math.log(10000.0) * freq_index / half_width)
    angle = timesteps.astype(F32)[..., None] * frequency
    step_embed = jnp.where(columns < half_width, jnp.sin(angle), jnp.cos(angle))
    class_hot = (class_ids[..., None] == jnp.arange(class_embed.shape[0])).astype(F32)
    condition = step_embed + jnp.einsum("mck,kd->mcd", class_hot, class_embed, precision=highest)
    lowered = jax.nn.silu(condition).astype(BF)
    mod_terms = jnp.einsum("mcd,de->mce", lowered, ada_weight, preferred_element_type=F32)
    near_terms = add_low(mod_terms, swap(mod_terms, "mp", n_mp, 1))
    modulation = near_terms
    for bit in bits_of(n_mp)[1:]:
        modulation = add_low(modulation, swap(modulation, "mp", n_mp, bit))
    modulation = modulation + ada_bias
    own_clip = lax.dynamic_slice_in_dim(window_clip, mp_index * own_windows, own_windows, 1)
    clip_hot = (own_clip[..., None] == jnp.arange(clips)).astype(F32)
    mods = jnp.einsum("mwc,mce->mwe", clip_hot, modulation, precision=highest)
    mods = mods.reshape(micro * own_windows, 6, width)

    steps = Steps()
    rel_tables = gather_shards(rel_bias, "mp", n_mp)
    blocks = bias_blocks(jnp.concatenate([rel_tables[m] for m in masks], axis=0))
    heads = rel_bias.shape[0]
    blocks = {m: blocks[m * heads : (m + 1) * heads] for m in masks}

    def gather(own, hold):
        shards = {}
        steps.jobs.append(gather_job(steps, own, shards, "mp", n_mp, hold))
        return shards

    def need(shards, mask, ties, token):
        while mask not in shards:
            ties = ties + steps.step(token)
        return ties

    qkv_w = gather(qkv_weight, 3)
    steps.step(modulation)
    attn_in = norm_call(tokens_flat, mods)
    out_w = gather(out_weight, 3)
    ties = steps.step(attn_in)
    qkv, mixed, lse = {}, {}, {}
    for m in masks:
        ties = need(qkv_w, m, ties, attn_in)
        qkv[m], mixed[m], lse[m] = attend_call(attn_in, qkv_w[m], blocks[m], ties)
        if m == 0:
            down_w = gather(down_weight, 4)
        elif m == 2 or m == n_mp - 1 == 1:
            up_w = gather(up_weight, 3)
        ties = steps.step(mixed[m])
    for m in masks:
        ties = need(out_w, m, ties, mixed[0])
    attn_out, mlp_in, grad_mlp = middle_call(
        [mixed[m] for m in masks], [out_w[m] for m in masks], tokens_flat, cot_flat, mods, ties
    )
    ties = steps.step(mlp_in)
    wide_sums = [Sums(steps, n_mp, lag, 1) for lag in (0, 0, 1, 2)]
    grads = {}
    steps.jobs.append(psum_job(wide_sums[:2], n_dp, 0, grads, "down"))
    steps.jobs.append(psum_job(wide_sums[2:], n_dp, 2, grads, "up"))
    sums = None
    for m in [m for m in masks if m % 2] + [m for m in reversed(masks) if m % 2 == 0]:
        ties = need(down_w, m, need(up_w, m, ties, mlp_in), mlp_in)
        mlp_out, gin, wide_terms = mlp_call(mlp_in, grad_mlp, up_w[m], down_w[m], sums, ties)
        sums = (mlp_out, gin)
        for wide_sum, term in zip(wide_sums, wide_terms):
            wide_sum.add(m, term)
        ties = steps.step(wide_terms[0])
    block_out, grad_resid, grad_attn, late_sums = middle_back_call(
        tokens_flat, cot_flat, attn_out, mlp_out, gin, mods, ties
    )

    def clip_sums(window_sums):
        grouped = window_sums.reshape(micro, own_windows, -1)
        return jnp.einsum("mwc,mwe->mce", clip_hot, grouped, precision=highest).astype(BF)

    steps.jobs.append(all_job(steps, clip_sums(late_sums), n_mp, n_dp, grads, "late"))

    out_sum = Sums(steps, n_mp, 0, 1)
    qkv_sum = Sums(steps, n_mp, 0, 1)
    steps.jobs.append(psum_job([out_sum], n_dp, 4, grads, "out"))
    steps.jobs.append(spread_job(steps, qkv_sum, n_dp, grads, "qkv"))
    dqkv, block_grads = {}, {}
    for m in masks:
        out_sum.add(m, dot(mixed[m], grad_attn, 0, 0).astype(BF))
    ties = steps.step(grad_attn)
    for m in reversed(masks):
        dqkv[m], block_grads[m], qkv_term = attend_back_call(
            grad_attn, out_w[m], qkv[m], mixed[m], lse[m], blocks[m], attn_in, ties
        )
        qkv_sum.add(m, qkv_term.reshape(-1, qkv_term.shape[2]))
        ties = steps.step(qkv_term)
    token_grad, early_sums = last_call(
        [dqkv[m] for m in masks], [qkv_w[m] for m in masks], tokens_flat, grad_resid, mods, ties
    )
    steps.jobs.append(all_job(steps, clip_sums(early_sums), n_mp, n_dp, grads, "early"))
    steps.step(token_grad)
    steps.finish()
    down_grad, up_grad, out_grad = [
        jnp.concatenate([after(part, token_grad) for part in grads[name]], axis=0).astype(F32)
        for name in ("down", "up", "out")
    ]
    qkv_grad = grads["qkv"].reshape(qkv_weight.shape)
    rel_grads = collect_blocks(jnp.concatenate([block_grads[m] for m in masks], axis=0)).astype(BF)
    rel_terms = {m: rel_grads[m * heads : (m + 1) * heads] for m in masks}
    rel_grad = reduce_all(reduce_shards(rel_terms, "mp", n_mp), "dp", n_dp).astype(F32)

    late = grads["late"].astype(F32).reshape(micro, clips, -1, width)
    early = grads["early"].astype(F32).reshape(micro, clips, -1, width)
    mod_total = jnp.concatenate(
        [early, late[:, :, 0:1], late[:, :, 1:4]], axis=2
    ).reshape(micro, clips, 6 * width)
    ada_bias_grad = jnp.sum(mod_total, axis=(0, 1))
    ada_weight_grad = jnp.einsum(
        "mcd,mce->de", lowered.astype(F32), mod_total, precision=highest
    )
    grad_lowered = jnp.einsum(
        "mce,de->mcd", mod_total, ada_weight.astype(F32), precision=highest
    )
    grad_condition = jax.vjp(jax.nn.silu, condition)[1](grad_lowered)[0]
    class_grad = jnp.einsum("mck,mcd->kd", class_hot, grad_condition, precision=highest)
    return (
        block_out.reshape(tokens.shape),
        token_grad.reshape(tokens.shape),
        qkv_grad,
        out_grad,
        up_grad,
        down_grad,
        rel_grad,
        ada_weight_grad,
        ada_bias_grad,
        class_grad,
    )


def solution(mesh):
    rows = P(None, ("dp", "mp"), None)
    in_specs = (
        rows,
        rows,
        P(None, None, "mp"),
        P("mp", None),
        P(None, "mp"),
        P("mp", None),
        P("mp", None),
        P("mp", None),
        P(),
        P(None, "mp"),
        P(None, "dp"),
        P(),
        P(),
    )
    out_specs = (
        rows,
        rows,
        P(None, None, "mp"),
        P("mp", None),
        P(None, "mp"),
        P("mp", None),
        P("mp", None),
        P("mp", None),
        P(),
        P(None, "mp"),
    )
    step = functools.partial(body, mesh.shape["dp"], mesh.shape["mp"])
    return jax.shard_map(step, mesh=mesh, in_specs=in_specs, out_specs=out_specs, check_vma=False)
```

```python
import functools
import math

import jax
import jax.numpy as jnp
from jax import lax
from jax.experimental import pallas as pl
from jax.experimental.pallas import tpu as pltpu
from jax.sharding import PartitionSpec as P

WIN_T = 5
WIN_H = 8
WIN_W = 8
WIN_TOK = WIN_T * WIN_H * WIN_W
FRAME = WIN_H * WIN_W
PAD_TOK = 384
HEAD_DIM = 64
N_TIME, N_ROW, N_COL = 2 * WIN_T - 1, 2 * WIN_H - 1, 2 * WIN_W - 1

BF = jnp.bfloat16
F32 = jnp.float32
epsilon = 1e-06
highest = lax.Precision.HIGHEST
GELU_A = 0.7978845608028654
GELU_B = GELU_A * 0.044715
VMEM_LIMIT = 60 * 1024 * 1024


def dot(left, right, left_dim=1, right_dim=0):
    return lax.dot_general(
        left, right, (((left_dim,), (right_dim,)), ((), ())), preferred_element_type=F32
    )


def params():
    return pltpu.CompilerParams(vmem_limit_bytes=VMEM_LIMIT)


def shaped(shape, dtype):
    return jax.ShapeDtypeStruct(shape, dtype)


def row_spec(rows, cols):
    return pl.BlockSpec((rows, cols), lambda i: (i, 0))


def part_spec(rows, cols):
    return pl.BlockSpec((3, rows, cols), lambda i: (0, i, 0))


def whole_spec(shape):
    return pl.BlockSpec(shape, lambda i: (0,) * len(shape))


def mod_spec(count, cols):
    return pl.BlockSpec((None, count, cols), lambda i: (i, 0, 0))


def cost(micros):
    return pl.CostEstimate(
        flops=int(micros * 1e9), bytes_accessed=int(micros * 3.5e6), transcendentals=0
    )


def call_after(kernel, deps, *, in_specs, **rest):
    deps = tuple(deps)
    count = len(in_specs)

    def run(*refs):
        kernel(*refs[:count], *refs[count + len(deps) :])

    call = pl.pallas_call(
        run, in_specs=list(in_specs) + [pl.BlockSpec(memory_space=pl.ANY)] * len(deps), **rest
    )
    return lambda *args: call(*args, *deps)


def after(value, *deps):
    return lax.optimization_barrier((value, *deps))[0]


def normalise(values):
    centred = values - jnp.mean(values, axis=-1, keepdims=True)
    inverse = lax.rsqrt(jnp.mean(centred * centred, axis=-1, keepdims=True) + epsilon)
    return centred * inverse, inverse


def normalise_back(normed, inverse, grad_in):
    return inverse * (
        grad_in
        - jnp.mean(grad_in, axis=-1, keepdims=True)
        - normed * jnp.mean(grad_in * normed, axis=-1, keepdims=True)
    )


def swap(value, axis, size, bit):
    return lax.ppermute(value, axis, [(i, i ^ bit) for i in range(size)])


def bits_of(size):
    return [1 << b for b in range(size.bit_length() - 1)]


def add_low(left, right):
    return (left.astype(F32) + right.astype(F32)).astype(left.dtype)


def gather_shards(own, axis, size):
    shards = {0: own}
    for bit in reversed(bits_of(size)):
        for mask in list(shards):
            shards[mask ^ bit] = swap(shards[mask], axis, size, bit)
    return shards


def reduce_all(value, axis, size):
    for bit in bits_of(size):
        value = add_low(value, swap(value, axis, size, bit))
    return value


def reduce_shards(terms, axis, size):
    terms = dict(terms)
    for bit in bits_of(size):
        for mask in [m for m in terms if m & bit]:
            terms[mask ^ bit] = add_low(terms[mask ^ bit], swap(terms.pop(mask), axis, size, bit))
    return terms[0]


def sum_kernel(*refs):
    total = refs[0][...].astype(F32)
    for ref in refs[1:-1]:
        total = total + ref[...].astype(F32)
    refs[-1][...] = total.astype(BF)


def add_parts(parts):
    if len(parts) == 1:
        return parts[0]
    rows, cols = parts[0].shape
    block = rows // 4 if rows % 64 == 0 and rows >= 512 else rows
    return pl.pallas_call(
        sum_kernel,
        grid=(rows // block,),
        in_specs=[row_spec(block, cols)] * len(parts),
        out_specs=row_spec(block, cols),
        out_shape=shaped((rows, cols), BF),
        compiler_params=params(),
        cost_estimate=cost(0.001),
        name="add",
    )(*parts)


def split_kernel(index_ref, *refs, count, terms):
    ins, outs = refs[:terms], refs[terms:]
    total = ins[0][...].astype(F32)
    for ref in ins[1:]:
        total = total + ref[...].astype(F32)
    total = total.astype(BF)
    for k in range(count):

        @pl.when(pl.program_id(0) == k)
        def _():
            outs[k][...] = total


def split_call(parts, index, count):
    rows, cols = parts[0].shape
    piece = (rows // count, cols)
    spec = pltpu.PrefetchScalarGridSpec(
        num_scalar_prefetch=1,
        grid=(count,),
        in_specs=[pl.BlockSpec(piece, lambda k, f: (f[0] ^ k, 0))] * len(parts),
        out_specs=[pl.BlockSpec(piece, lambda k, f: (0, 0))] * count,
    )
    return pl.pallas_call(
        functools.partial(split_kernel, count=count, terms=len(parts)),
        grid_spec=spec,
        out_shape=[shaped(piece, BF)] * count,
        compiler_params=params(),
        cost_estimate=cost(0.001),
        name="split",
    )(jnp.reshape(index, (1,)).astype(jnp.int32), *parts)


def assemble_kernel(index_ref, *refs):
    for k, ref in enumerate(refs[:-1]):

        @pl.when(pl.program_id(0) == k)
        def _():
            refs[-1][...] = ref[...].astype(refs[-1].dtype)


def assemble_call(pieces, index, dtype):
    count = len(pieces)
    rows, cols = pieces[0].shape
    spec = pltpu.PrefetchScalarGridSpec(
        num_scalar_prefetch=1,
        grid=(count,),
        in_specs=[pl.BlockSpec((rows, cols), lambda k, f: (0, 0))] * count,
        out_specs=pl.BlockSpec((rows, cols), lambda k, f: (f[0] ^ k, 0)),
    )
    return pl.pallas_call(
        assemble_kernel,
        grid_spec=spec,
        out_shape=shaped((rows * count, cols), dtype),
        compiler_params=params(),
        cost_estimate=cost(0.001),
        name="assemble",
    )(jnp.reshape(index, (1,)).astype(jnp.int32), *pieces)


class Steps:
    def __init__(self):
        self.jobs, self.token = [], None

    def swap(self, value, axis, size, bit):
        if self.token is not None:
            value = after(value, self.token)
        return swap(value, axis, size, bit)

    def arrive(self, value):
        return value if self.token is None else after(value, self.token)

    def step(self, token=None):
        self.token = token
        ties, jobs = [], []
        for job in self.jobs:
            try:
                ties += next(job)
            except StopIteration:
                continue
            jobs.append(job)
        self.jobs = jobs
        return ties if token is None else ties + [token]

    def finish(self):
        while self.jobs:
            self.step()


def gather_job(steps, own, shards, axis, size, hold):
    shards[0] = own
    even = {0: own}
    shards[1] = steps.swap(own, axis, size, 1)
    for bit in reversed(bits_of(size)[1:]):
        new = {mask ^ bit: steps.swap(part, axis, size, bit) for mask, part in even.items()}
        for _ in range(hold):
            yield []
        new = {mask: steps.arrive(part) for mask, part in new.items()}
        even.update(new)
        for mask, part in new.items():
            shards[mask] = part
            shards[mask ^ 1] = steps.swap(part, axis, size, 1)
        yield list(new.values())


class Sums:
    def __init__(self, steps, size, lag, hold):
        self.steps, self.size, self.lag, self.hold = steps, size, lag, hold
        self.parts = {mask: [] for mask in range(size)}
        nearest_first = sorted(range(1, size), key=lambda mask: (mask & -mask, mask))
        steps.jobs += [self.send(mask) for mask in nearest_first]

    def full(self, mask):
        low = mask & -mask if mask else self.size
        return len(self.parts[mask]) == low.bit_length()

    def add(self, mask, term):
        self.parts[mask].append(term)

    def send(self, mask):
        while not self.full(mask):
            yield []
        bit = mask & -mask
        for _ in range(self.lag if bit > 1 else 0):
            yield []
        other = self.steps.swap(add_parts(self.parts[mask]), "mp", self.size, bit)
        for _ in range(self.hold if bit > 1 else 1):
            yield []
        other = self.steps.arrive(other)
        self.add(mask ^ bit, other)
        yield [other]


def psum_job(sums, earlier, out, name):
    while not sums.full(0):
        yield []
    value = add_parts(sums.parts[0])
    yield [value]
    while earlier not in out:
        yield []
    out[name] = lax.psum(after(value, out[earlier]), "dp")


def all_job(steps, value, n_mp, n_dp, out, name):
    ready = []
    for axis, size in (("mp", n_mp), ("dp", n_dp)):
        for bit in bits_of(size):
            other = steps.swap(value, axis, size, bit)
            yield ready
            value = add_low(value, steps.arrive(other))
            ready = [value]
    out[name] = value
    yield ready


def spread_job(steps, sums, n_dp, offload, out, name):
    while not sums.full(0):
        yield []
    index = lax.axis_index("dp")
    count = n_dp // 2
    keep, send = split_call(sums.parts[0], index % 2, 2)
    other = steps.swap(send, "dp", n_dp, 1)
    yield [send]
    pieces = split_call([keep, steps.arrive(other)], index // 2, count)
    others = [steps.swap(pieces[k], "dp", n_dp, 2 * k) for k in range(1, count)]
    yield [other, *pieces]
    total = add_parts([pieces[0]] + [steps.arrive(part) for part in others])
    if offload:
        whole = lax.all_gather(total, "dp", axis=0)
        yield [total]
        yield []
        whole = steps.arrive(whole)
        out[name] = whole.reshape(count, 2, *total.shape)
        yield [whole]
        return
    others = [steps.swap(total, "dp", n_dp, 2 * k) for k in range(1, count)]
    yield [total]
    half = assemble_call([total] + [steps.arrive(part) for part in others], index // 2, BF)
    other = steps.swap(half, "dp", n_dp, 1)
    yield [half]
    out[name] = assemble_call([half, steps.arrive(other)], index % 2, F32)


def place_hot():
    place = jnp.arange(FRAME)
    row, col = place // WIN_W, place % WIN_W
    offset = (row[:, None] - row[None, :] + WIN_H - 1) * N_COL + (
        col[:, None] - col[None, :] + WIN_W - 1
    )
    return (offset.reshape(1, -1) == jnp.arange(N_ROW * N_COL)[:, None]).astype(F32)


def bias_blocks(rel_table):
    heads = rel_table.shape[0]
    cube = rel_table.reshape(heads * N_TIME, N_ROW * N_COL)
    return lax.dot(cube, place_hot(), precision=highest).reshape(heads, N_TIME, FRAME, FRAME)


def collect_blocks(block_grad):
    heads = block_grad.shape[0]
    flat = block_grad.reshape(heads * N_TIME, FRAME * FRAME)
    cube = lax.dot_general(flat, place_hot(), (((1,), (1,)), ((), ())), precision=highest)
    return cube[:, ::-1].reshape(heads, -1)


def block_spec(heads, place):
    return pl.BlockSpec((heads, N_TIME, FRAME, FRAME), lambda i: (place, 0, 0, 0))


def frame_span(frame):
    return slice(frame * FRAME, (frame + 1) * FRAME)


def spread_blocks(blocks_ref, table, fill, transposed):
    for head in range(table.shape[0]):
        for offset in range(N_TIME):
            block = blocks_ref[head, offset]
            if transposed:
                block = block.T
            for query in range(WIN_T):
                key = query - (offset - WIN_T + 1)
                if 0 <= key < WIN_T:
                    row, col = (key, query) if transposed else (query, key)
                    table[head, frame_span(row), frame_span(col)] = block
        table[head, :, WIN_TOK:] = jnp.full((WIN_TOK, PAD_TOK - WIN_TOK), fill, F32)


def norm_kernel(tokens_ref, mod_ref, attn_in_ref):
    normed, _ = normalise(tokens_ref[...].astype(F32))
    attn_in_ref[...] = (normed * (1.0 + mod_ref[1:2]) + mod_ref[0:1]).astype(BF)


def norm_call(tokens, mods, deps=()):
    rows, width = tokens.shape
    return call_after(
        norm_kernel,
        deps,
        grid=(rows // WIN_TOK,),
        in_specs=[row_spec(WIN_TOK, width), mod_spec(mods.shape[1], width)],
        out_specs=row_spec(WIN_TOK, width),
        out_shape=shaped((rows, width), BF),
        compiler_params=params(),
        cost_estimate=cost(8),
        name="norm_in",
    )(tokens, mods)


def head_copies(value, heads):
    if heads == 1:
        return [value]
    lane = lax.broadcasted_iota(jnp.int32, value.shape, 1) // HEAD_DIM
    return [jnp.where(lane == head, value, jnp.zeros_like(value)) for head in range(heads)]


def pad_rows(value):
    return jnp.concatenate(
        [value, jnp.zeros((PAD_TOK - WIN_TOK, value.shape[1]), value.dtype)], axis=0
    )


def attend_kernel(x_ref, w_ref, blocks_ref, qkv_ref, mixed_ref, lse_ref, table, columns):
    heads = blocks_ref.shape[0]

    @pl.when(pl.program_id(0) == 0)
    def _():
        spread_blocks(blocks_ref, table, -1e30, False)
        columns[...] = jnp.zeros_like(columns)

    x = x_ref[...]
    query = dot(x, w_ref[0]).astype(BF)
    key = dot(x, w_ref[1]).astype(BF)
    value = dot(x, w_ref[2]).astype(BF)
    qkv_ref[0] = query
    qkv_ref[1] = key
    qkv_ref[2] = value
    scaled = query * jnp.asarray(HEAD_DIM**-0.5, BF)
    scores = dot(jnp.concatenate(head_copies(scaled, heads), axis=0), pad_rows(key), 1, 1)
    probs = []
    for head in range(heads):
        score = scores[head * WIN_TOK : (head + 1) * WIN_TOK] + table[head]
        top = jnp.max(score, axis=1, keepdims=True)
        exponent = jnp.exp(score - top)
        total = jnp.sum(exponent, axis=1, keepdims=True)
        probs.append((exponent * (1.0 / total)).astype(BF))
        columns[:WIN_TOK, head : head + 1] = top + jnp.log(total)
    values = jnp.concatenate([pad_rows(part) for part in head_copies(value, heads)], axis=0)
    mixed_ref[...] = dot(jnp.concatenate(probs, axis=1), values).astype(BF)
    lse_ref[...] = columns[...].T[: lse_ref.shape[0]]


def attend_call(attn_in, weight, blocks, deps=()):
    rows, width = attn_in.shape
    cols = weight.shape[2]
    blocks, place, heads = blocks
    windows = rows // WIN_TOK
    stat_rows = -(-heads // 8) * 8
    return call_after(
        attend_kernel,
        deps,
        grid=(windows,),
        in_specs=[row_spec(WIN_TOK, width), whole_spec(weight.shape), block_spec(heads, place)],
        out_specs=[
            part_spec(WIN_TOK, cols),
            row_spec(WIN_TOK, cols),
            mod_spec(stat_rows, PAD_TOK),
        ],
        out_shape=[
            shaped((3, rows, cols), BF),
            shaped((rows, cols), BF),
            shaped((windows, stat_rows, PAD_TOK), F32),
        ],
        scratch_shapes=[
            pltpu.VMEM((heads, WIN_TOK, PAD_TOK), F32),
            pltpu.VMEM((PAD_TOK, 128), F32),
        ],
        compiler_params=params(),
        cost_estimate=cost(19),
        name="attend",
    )(attn_in, weight, blocks)


def attend_back_kernel(
    grad_ref, out_w_ref, qkv_ref, mixed_ref, lse_ref, blocks_ref, x_ref, dqkv_ref, dblocks_ref, dw_ref, table, total, x_all, d_all
):
    heads = blocks_ref.shape[0]
    cols = out_w_ref.shape[0]
    step = pl.program_id(0)

    @pl.when(step == 0)
    def _():
        spread_blocks(blocks_ref, table, 0.0, True)
        total[...] = jnp.zeros_like(total)

    grad_mixed = dot(grad_ref[...], out_w_ref[...], 1, 1).astype(BF)
    query = qkv_ref[0]
    key = qkv_ref[1]
    value = qkv_ref[2]
    scale = jnp.asarray(HEAD_DIM**-0.5, BF)
    product = grad_mixed.astype(F32) * mixed_ref[...].astype(F32)
    upper = product.astype(BF)
    lower = (product - upper.astype(F32)).astype(BF)
    head_rows = (lse_ref.shape[0], cols)
    head_hot = (
        lax.broadcasted_iota(jnp.int32, head_rows, 1) // HEAD_DIM
        == lax.broadcasted_iota(jnp.int32, head_rows, 0)
    ).astype(BF)
    inner = dot(head_hot, pad_rows(upper), 1, 1) + dot(head_hot, pad_rows(lower), 1, 1)
    keys = jnp.concatenate(head_copies(key * scale, heads), axis=0)
    values = jnp.concatenate(head_copies(value, heads), axis=0)
    query_pad = pad_rows(query)
    grad_pad = pad_rows(grad_mixed)
    scores = dot(keys, query_pad, 1, 1)
    grad_probs = dot(values, grad_pad, 1, 1)
    probs = []
    grad_scores = []
    for head in range(heads):
        span = slice(head * WIN_TOK, (head + 1) * WIN_TOK)
        prob = jnp.exp(scores[span] + table[head] - lse_ref[head : head + 1, :])
        grad_score = (prob * (grad_probs[span] - inner[head : head + 1, :])).astype(BF)
        probs.append(prob.astype(BF))
        grad_scores.append(grad_score)
        total[head] += grad_score.astype(F32)
    wide = jnp.concatenate(grad_scores, axis=1)
    grad_value = dot(
        jnp.concatenate(probs, axis=1), jnp.concatenate(head_copies(grad_pad, heads), axis=0)
    )
    grad_key = dot(wide, jnp.concatenate(head_copies(query_pad * scale, heads), axis=0))
    grad_query = dot(jnp.concatenate(grad_scores, axis=0), keys, 0, 0)[:WIN_TOK]
    rows = pl.ds(pl.multiple_of(step * WIN_TOK, WIN_TOK), WIN_TOK)
    x_all[rows, :] = x_ref[...]
    for part, grad in enumerate((grad_query, grad_key, grad_value)):
        grad = grad.astype(BF)
        dqkv_ref[part] = grad
        d_all[part, rows, :] = grad

    @pl.when(step == pl.num_programs(0) - 1)
    def _():
        for part in range(3):
            dw_ref[part] = dot(x_all[...], d_all[part], 0, 0).astype(BF)
        for head in range(heads):
            for offset in range(N_TIME):
                block = None
                for query in range(WIN_T):
                    key = query - (offset - WIN_T + 1)
                    if 0 <= key < WIN_T:
                        part = total[head, frame_span(key), frame_span(query)]
                        block = part if block is None else block + part
                dblocks_ref[head, offset] = block


def attend_back_call(grad_attn, out_weight, qkv, mixed, lse, blocks, attn_in, deps=()):
    rows, width = grad_attn.shape
    cols = out_weight.shape[0]
    blocks, place, heads = blocks
    return call_after(
        attend_back_kernel,
        deps,
        grid=(rows // WIN_TOK,),
        in_specs=[
            row_spec(WIN_TOK, width),
            whole_spec(out_weight.shape),
            part_spec(WIN_TOK, cols),
            row_spec(WIN_TOK, cols),
            mod_spec(lse.shape[1], PAD_TOK),
            block_spec(heads, place),
            row_spec(WIN_TOK, width),
        ],
        out_specs=[
            part_spec(WIN_TOK, cols),
            block_spec(heads, 0),
            whole_spec((3, width, cols)),
        ],
        out_shape=[
            shaped((3, rows, cols), BF),
            shaped((heads,) + blocks.shape[1:], F32),
            shaped((3, width, cols), BF),
        ],
        scratch_shapes=[pltpu.VMEM((heads, WIN_TOK, PAD_TOK), F32)] * 2
        + [pltpu.VMEM((rows, width), BF), pltpu.VMEM((3, rows, cols), BF)],
        compiler_params=params(),
        cost_estimate=cost(30),
        name="attend_back",
    )(grad_attn, out_weight, qkv, mixed, lse, blocks, attn_in)


def out_grad_kernel(grad_ref, *refs):
    count = len(refs) // 2
    for place in range(count):

        @pl.when(pl.program_id(0) == place)
        def _():
            refs[count + place][...] = dot(refs[place][...], grad_ref[...], 0, 0).astype(BF)


def out_grad_call(mixed, grad_attn):
    rows, width = grad_attn.shape
    cols = mixed[0].shape[1]
    return pl.pallas_call(
        out_grad_kernel,
        grid=(len(mixed),),
        in_specs=[whole_spec(grad_attn.shape)] + [whole_spec(part.shape) for part in mixed],
        out_specs=[whole_spec((cols, width))] * len(mixed),
        out_shape=[shaped((cols, width), BF)] * len(mixed),
        compiler_params=params(),
        cost_estimate=cost(0.001),
        name="out_grad",
    )(grad_attn, *mixed)


def middle_kernel(*refs, count):
    mixed_refs = refs[:count]
    weight_refs = refs[count : 2 * count]
    tokens_ref, cot_ref, mod_ref, attn_out_ref, mlp_in_ref, grad_mlp_ref = refs[2 * count :]
    attn_out = dot(mixed_refs[0][...], weight_refs[0][...])
    for mixed_ref, weight_ref in zip(mixed_refs[1:], weight_refs[1:]):
        attn_out = attn_out + dot(mixed_ref[...], weight_ref[...])
    attn_out_ref[...] = attn_out
    resid = tokens_ref[...].astype(F32) + mod_ref[2:3] * attn_out
    normed, _ = normalise(resid)
    mlp_in_ref[...] = (normed * (1.0 + mod_ref[4:5]) + mod_ref[3:4]).astype(BF)
    grad_mlp_ref[...] = (mod_ref[5:6] * cot_ref[...].astype(F32)).astype(BF)


def middle_call(mixed, weights, tokens, cotangent, mods, deps=()):
    rows, width = tokens.shape
    count = len(mixed)
    row = row_spec(WIN_TOK, width)
    return call_after(
        functools.partial(middle_kernel, count=count),
        deps,
        grid=(rows // WIN_TOK,),
        in_specs=[row_spec(WIN_TOK, part.shape[1]) for part in mixed]
        + [whole_spec(part.shape) for part in weights]
        + [row, row, mod_spec(mods.shape[1], width)],
        out_specs=[row, row, row],
        out_shape=[
            shaped((rows, width), F32),
            shaped((rows, width), BF),
            shaped((rows, width), BF),
        ],
        compiler_params=params(),
        cost_estimate=cost(16),
        name="middle",
    )(*mixed, *weights, tokens, cotangent, mods)


def mlp_kernel(*refs, chunk, first):
    x_ref, g_ref, up_ref, down_ref = refs[:4]
    rest = refs[4:] if first else refs[6:]
    out_ref, gin_ref = rest[:2]
    ddown_ref, dup_ref, down_total, up_total, act, ghid = rest[2:]
    step = pl.program_id(0)
    hidden_width = up_ref.shape[1]
    x = x_ref[...]
    g = g_ref[...]
    for start in range(0, hidden_width, chunk):
        span = slice(start, start + chunk)
        hidden = dot(x, up_ref[:, span])
        grad_act = dot(g, down_ref[span, :], 1, 1)
        square = hidden * hidden
        tanh = jnp.tanh(hidden * (GELU_A + GELU_B * square))
        half = 0.5 * hidden
        act[:, span] = (half + half * tanh).astype(BF)
        slope = 0.5 + 0.5 * tanh + half * (1.0 - tanh * tanh) * (GELU_A + 3.0 * GELU_B * square)
        ghid[:, span] = (grad_act * slope).astype(BF)
    out = dot(act[...], down_ref[...])
    gin = dot(ghid[...], up_ref[...], 1, 1)
    if first:
        out_ref[...] = out
        gin_ref[...] = gin
    else:
        out_ref[...] = refs[4][...] + out
        gin_ref[...] = refs[5][...] + gin

    @pl.when(step == 0)
    def _():
        down_total[...] = dot(act[...], g, 0, 0)
        up_total[...] = dot(x, ghid[...], 0, 0)

    @pl.when(step > 0)
    def _():
        down_total[...] += dot(act[...], g, 0, 0)
        up_total[...] += dot(x, ghid[...], 0, 0)

    @pl.when(step == pl.num_programs(0) - 1)
    def _():
        ddown_ref[...] = down_total[...].astype(BF)
        dup_ref[...] = up_total[...].astype(BF)


def mlp_call(x, g, up, down, sums, deps=()):
    rows, width = x.shape
    hidden = up.shape[1]
    block = 512 if rows % 512 == 0 else WIN_TOK
    row = row_spec(block, width)
    first = sums is None
    extra = () if first else tuple(sums)
    halves = [down.shape, up.shape]
    out = call_after(
        functools.partial(mlp_kernel, chunk=min(512, hidden), first=first),
        deps,
        grid=(rows // block,),
        in_specs=[row, row, whole_spec(up.shape), whole_spec(down.shape)] + [row] * len(extra),
        out_specs=[row, row] + [whole_spec(shape) for shape in halves],
        out_shape=[shaped((rows, width), F32)] * 2 + [shaped(shape, BF) for shape in halves],
        scratch_shapes=[
            pltpu.VMEM(down.shape, F32),
            pltpu.VMEM(up.shape, F32),
            pltpu.VMEM((block, hidden), BF),
            pltpu.VMEM((block, hidden), BF),
        ],
        input_output_aliases={} if first else {4: 0, 5: 1},
        compiler_params=params(),
        cost_estimate=cost(46),
        name="mlp",
    )(x, g, up, down, *extra)
    return out[0], out[1], out[2:]


def middle_back_kernel(
    tokens_ref, cot_ref, attn_out_ref, mlp_out_ref, gin_ref, mod_ref, out_ref, gres_ref, gattn_ref, sums_ref
):
    cot = cot_ref[...].astype(F32)
    attn_out = attn_out_ref[...]
    mlp_out = mlp_out_ref[...]
    gin = gin_ref[...]
    resid = tokens_ref[...].astype(F32) + mod_ref[2:3] * attn_out
    out_ref[...] = (resid + mod_ref[5:6] * mlp_out).astype(BF)
    normed, inverse = normalise(resid)
    gres = cot + normalise_back(normed, inverse, gin * (1.0 + mod_ref[4:5]))
    gres_ref[...] = gres
    gattn_ref[...] = (mod_ref[2:3] * gres).astype(BF)
    sums_ref[0:1] = jnp.sum(gres * attn_out, axis=0, keepdims=True)
    sums_ref[1:2] = jnp.sum(gin, axis=0, keepdims=True)
    sums_ref[2:3] = jnp.sum(gin * normed, axis=0, keepdims=True)
    sums_ref[3:4] = jnp.sum(cot * mlp_out, axis=0, keepdims=True)


def middle_back_call(tokens, cotangent, attn_out, mlp_out, gin, mods, deps=()):
    rows, width = tokens.shape
    row = row_spec(WIN_TOK, width)
    windows = rows // WIN_TOK
    return call_after(
        middle_back_kernel,
        deps,
        grid=(windows,),
        in_specs=[row] * 5 + [mod_spec(mods.shape[1], width)],
        out_specs=[row, row, row, mod_spec(4, width)],
        out_shape=[
            shaped((rows, width), BF),
            shaped((rows, width), F32),
            shaped((rows, width), BF),
            shaped((windows, 4, width), F32),
        ],
        compiler_params=params(),
        cost_estimate=cost(24),
        name="middle_back",
    )(tokens, cotangent, attn_out, mlp_out, gin, mods)


def last_kernel(*refs, count):
    dqkv_refs = refs[:count]
    weight_refs = refs[count : 2 * count]
    tokens_ref, gres_ref, mod_ref, out_ref, sums_ref = refs[2 * count :]
    gin = None
    for dqkv_ref, weight_ref in zip(dqkv_refs, weight_refs):
        for part in range(3):
            term = dot(dqkv_ref[part], weight_ref[part], 1, 1)
            gin = term if gin is None else gin + term
    normed, inverse = normalise(tokens_ref[...].astype(F32))
    out_ref[...] = (
        gres_ref[...] + normalise_back(normed, inverse, gin * (1.0 + mod_ref[1:2]))
    ).astype(BF)
    sums_ref[0:1] = jnp.sum(gin, axis=0, keepdims=True)
    sums_ref[1:2] = jnp.sum(gin * normed, axis=0, keepdims=True)


def last_call(dqkv, weights, tokens, gres, mods, deps=()):
    rows, width = tokens.shape
    count = len(dqkv)
    row = row_spec(WIN_TOK, width)
    windows = rows // WIN_TOK
    return call_after(
        functools.partial(last_kernel, count=count),
        deps,
        grid=(windows,),
        in_specs=[part_spec(WIN_TOK, part.shape[2]) for part in dqkv]
        + [whole_spec(part.shape) for part in weights]
        + [row, row, mod_spec(mods.shape[1], width)],
        out_specs=[row, mod_spec(2, width)],
        out_shape=[shaped((rows, width), BF), shaped((windows, 2, width), F32)],
        compiler_params=params(),
        cost_estimate=cost(28),
        name="last",
    )(*dqkv, *weights, tokens, gres, mods)


def body(
    n_dp,
    n_mp,
    tokens,
    cotangent,
    qkv_weight,
    out_weight,
    up_weight,
    down_weight,
    rel_bias,
    ada_weight,
    ada_bias,
    class_embed,
    window_clip,
    timesteps,
    class_ids,
):
    mp_index = lax.axis_index("mp")
    micro, local_rows, width = tokens.shape
    local_cols = class_embed.shape[1]
    clips = timesteps.shape[1]
    own_windows = local_rows // WIN_TOK
    rows = micro * local_rows
    tokens_flat = tokens.reshape(rows, width)
    cot_flat = cotangent.reshape(rows, width)
    masks = range(n_mp)

    columns = mp_index * local_cols + jnp.arange(local_cols)
    half_width = width // 2
    freq_index = (columns % half_width).astype(F32)
    frequency = jnp.exp(-math.log(10000.0) * freq_index / half_width)
    angle = timesteps.astype(F32)[..., None] * frequency
    step_embed = jnp.where(columns < half_width, jnp.sin(angle), jnp.cos(angle))
    class_hot = (class_ids[..., None] == jnp.arange(class_embed.shape[0])).astype(F32)
    condition = step_embed + jnp.einsum("mck,kd->mcd", class_hot, class_embed, precision=highest)
    lowered = jax.nn.silu(condition).astype(BF)
    mod_terms = jnp.einsum("mcd,de->mce", lowered, ada_weight, preferred_element_type=F32)
    near_terms = add_low(mod_terms, swap(mod_terms, "mp", n_mp, 1))
    modulation = near_terms
    for bit in bits_of(n_mp)[1:]:
        modulation = add_low(modulation, swap(modulation, "mp", n_mp, bit))
    modulation = modulation + ada_bias
    own_clip = lax.dynamic_slice_in_dim(window_clip, mp_index * own_windows, own_windows, 1)
    clip_hot = (own_clip[..., None] == jnp.arange(clips)).astype(F32)
    mods = jnp.einsum("mwc,mce->mwe", clip_hot, modulation, precision=highest)
    mods = mods.reshape(micro * own_windows, 6, width)

    steps = Steps()
    rel_tables = gather_shards(rel_bias, "mp", n_mp)
    blocks = bias_blocks(jnp.concatenate([rel_tables[m] for m in masks], axis=0))
    heads = rel_bias.shape[0]

    def gather(own, hold):
        shards = {}
        steps.jobs.append(gather_job(steps, own, shards, "mp", n_mp, hold))
        return shards

    def need(shards, mask, ties, token):
        while mask not in shards:
            ties = ties + steps.step(token)
        return ties

    qkv_w = gather(qkv_weight, 3)
    steps.step(modulation)
    attn_in = norm_call(tokens_flat, mods)
    out_w = gather(out_weight, 3)
    ties = steps.step(attn_in)
    qkv, mixed, lse = {}, {}, {}
    for m in masks:
        ties = need(qkv_w, m, ties, attn_in)
        qkv[m], mixed[m], lse[m] = attend_call(attn_in, qkv_w[m], (blocks, m, heads), ties)
        if m == 0:
            down_w = gather(down_weight, 4)
        elif m == 2 or m == n_mp - 1 == 1:
            up_w = gather(up_weight, 3)
        ties = steps.step(mixed[m])
    for m in masks:
        ties = need(out_w, m, ties, mixed[0])
    attn_out, mlp_in, grad_mlp = middle_call(
        [mixed[m] for m in masks], [out_w[m] for m in masks], tokens_flat, cot_flat, mods, ties
    )
    ties = steps.step(mlp_in)
    wide_sums = [Sums(steps, n_mp, 0, 1), Sums(steps, n_mp, 1, 2)]
    grads = {}
    steps.jobs.append(spread_job(steps, wide_sums[0], n_dp, True, grads, "down"))
    steps.jobs.append(spread_job(steps, wide_sums[1], n_dp, False, grads, "up"))
    sums = None
    for m in [m for m in masks if m % 2] + [m for m in reversed(masks) if m % 2 == 0]:
        ties = need(down_w, m, need(up_w, m, ties, mlp_in), mlp_in)
        mlp_out, gin, wide_terms = mlp_call(mlp_in, grad_mlp, up_w[m], down_w[m], sums, ties)
        sums = (mlp_out, gin)
        for wide_sum, term in zip(wide_sums, wide_terms):
            wide_sum.add(m, term)
        ties = steps.step(wide_terms[0])
    block_out, grad_resid, grad_attn, late_sums = middle_back_call(
        tokens_flat, cot_flat, attn_out, mlp_out, gin, mods, ties
    )

    def clip_sums(window_sums):
        grouped = window_sums.reshape(micro, own_windows, -1)
        return jnp.einsum("mwc,mwe->mce", clip_hot, grouped, precision=highest).astype(BF)

    out_sum = Sums(steps, n_mp, 0, 1)
    qkv_sum = Sums(steps, n_mp, 0, 1)
    steps.jobs.append(psum_job(out_sum, "down", grads, "out"))
    steps.jobs.append(spread_job(steps, qkv_sum, n_dp, False, grads, "qkv"))
    dqkv, block_grads = {}, {}
    for m, out_term in zip(masks, out_grad_call([mixed[m] for m in masks], grad_attn)):
        out_sum.add(m, out_term)
    ties = steps.step(grad_attn)
    for m in reversed(masks):
        dqkv[m], block_grads[m], qkv_term = attend_back_call(
            grad_attn, out_w[m], qkv[m], mixed[m], lse[m], (blocks, m, heads), attn_in, ties
        )
        qkv_sum.add(m, qkv_term.reshape(-1, qkv_term.shape[2]))
        ties = steps.step(qkv_term)
    token_grad, early_sums = last_call(
        [dqkv[m] for m in masks], [qkv_w[m] for m in masks], tokens_flat, grad_resid, mods, ties
    )
    window_sums = jnp.concatenate([early_sums, late_sums], axis=1)
    steps.jobs.append(all_job(steps, clip_sums(window_sums), n_mp, n_dp, grads, "mod"))
    steps.step(token_grad)
    steps.finish()

    def gathered(name, shape):
        pieces = after(grads[name], token_grad)
        return jnp.swapaxes(pieces, 0, 1).astype(F32).reshape(shape)

    down_grad = gathered("down", down_weight.shape)
    up_grad = grads["up"]
    out_grad = after(grads["out"], token_grad).astype(F32)
    qkv_grad = grads["qkv"].reshape(qkv_weight.shape)
    rel_grads = collect_blocks(jnp.concatenate([block_grads[m] for m in masks], axis=0)).astype(BF)
    rel_terms = {m: rel_grads[m * heads : (m + 1) * heads] for m in masks}
    rel_grad = reduce_all(reduce_shards(rel_terms, "mp", n_mp), "dp", n_dp).astype(F32)

    mod_total = grads["mod"].astype(F32)
    ada_bias_grad = jnp.sum(mod_total, axis=(0, 1))
    ada_weight_grad = jnp.einsum(
        "mcd,mce->de", lowered.astype(F32), mod_total, precision=highest
    )
    grad_lowered = jnp.einsum(
        "mce,de->mcd", mod_total, ada_weight.astype(F32), precision=highest
    )
    grad_condition = jax.vjp(jax.nn.silu, condition)[1](grad_lowered)[0]
    class_grad = jnp.einsum("mck,mcd->kd", class_hot, grad_condition, precision=highest)
    return (
        block_out.reshape(tokens.shape),
        token_grad.reshape(tokens.shape),
        qkv_grad,
        out_grad,
        up_grad,
        down_grad,
        rel_grad,
        ada_weight_grad,
        ada_bias_grad,
        class_grad,
    )


def solution(mesh):
    rows = P(None, ("dp", "mp"), None)
    in_specs = (
        rows,
        rows,
        P(None, None, "mp"),
        P("mp", None),
        P(None, "mp"),
        P("mp", None),
        P("mp", None),
        P("mp", None),
        P(),
        P(None, "mp"),
        P(None, "dp"),
        P(),
        P(),
    )
    out_specs = (
        rows,
        rows,
        P(None, None, "mp"),
        P("mp", None),
        P(None, "mp"),
        P("mp", None),
        P("mp", None),
        P("mp", None),
        P(),
        P(None, "mp"),
    )
    step = functools.partial(body, mesh.shape["dp"], mesh.shape["mp"])
    return jax.shard_map(step, mesh=mesh, in_specs=in_specs, out_specs=out_specs, check_vma=False)
```

```python
import functools
import math

import jax
import jax.numpy as jnp
from jax import lax
from jax.experimental import pallas as pl
from jax.experimental.pallas import tpu as pltpu
from jax.sharding import PartitionSpec as P

WIN_T = 5
WIN_H = 8
WIN_W = 8
WIN_TOK = WIN_T * WIN_H * WIN_W
FRAME = WIN_H * WIN_W
PAD_TOK = 384
HEAD_DIM = 64
N_TIME, N_ROW, N_COL = 2 * WIN_T - 1, 2 * WIN_H - 1, 2 * WIN_W - 1

BF = jnp.bfloat16
F32 = jnp.float32
epsilon = 1e-06
highest = lax.Precision.HIGHEST
GELU_A = 0.7978845608028654
GELU_B = GELU_A * 0.044715
VMEM_LIMIT = 63 * 1024 * 1024


def dot(left, right, left_dim=1, right_dim=0):
    return lax.dot_general(
        left, right, (((left_dim,), (right_dim,)), ((), ())), preferred_element_type=F32
    )


def params():
    return pltpu.CompilerParams(vmem_limit_bytes=VMEM_LIMIT)


def shaped(shape, dtype):
    return jax.ShapeDtypeStruct(shape, dtype)


def row_spec(rows, cols):
    return pl.BlockSpec((rows, cols), lambda i: (i, 0))


def part_spec(rows, cols):
    return pl.BlockSpec((3, rows, cols), lambda i: (0, i, 0))


def per_step(rows):
    return 2 if rows % (2 * WIN_TOK) == 0 else 1


def window_span(window):
    return slice(window * WIN_TOK, (window + 1) * WIN_TOK)


def whole_spec(shape):
    return pl.BlockSpec(shape, lambda i: (0,) * len(shape))


def mod_spec(per, count, cols):
    return pl.BlockSpec((per, count, cols), lambda i: (i, 0, 0))


def cost(micros):
    return pl.CostEstimate(
        flops=int(micros * 1e9), bytes_accessed=int(micros * 3.5e6), transcendentals=0
    )


def call_after(kernel, deps, *, in_specs, **rest):
    deps = tuple(deps)
    count = len(in_specs)

    def run(*refs):
        kernel(*refs[:count], *refs[count + len(deps) :])

    call = pl.pallas_call(
        run, in_specs=list(in_specs) + [pl.BlockSpec(memory_space=pl.ANY)] * len(deps), **rest
    )
    return lambda *args: call(*args, *deps)


def after(value, *deps):
    return lax.optimization_barrier((value, *deps))[0]


def normalise(values):
    centred = values - jnp.mean(values, axis=-1, keepdims=True)
    inverse = lax.rsqrt(jnp.mean(centred * centred, axis=-1, keepdims=True) + epsilon)
    return centred * inverse, inverse


def normalise_back(normed, inverse, grad_in):
    return inverse * (
        grad_in
        - jnp.mean(grad_in, axis=-1, keepdims=True)
        - normed * jnp.mean(grad_in * normed, axis=-1, keepdims=True)
    )


def swap(value, axis, size, bit):
    return lax.ppermute(value, axis, [(i, i ^ bit) for i in range(size)])


def bits_of(size):
    return [1 << b for b in range(size.bit_length() - 1)]


def add_low(left, right):
    return (left.astype(F32) + right.astype(F32)).astype(left.dtype)


def gather_shards(own, axis, size):
    shards = {0: own}
    for bit in reversed(bits_of(size)):
        for mask in list(shards):
            shards[mask ^ bit] = swap(shards[mask], axis, size, bit)
    return shards


def reduce_all(value, axis, size):
    for bit in bits_of(size):
        value = add_low(value, swap(value, axis, size, bit))
    return value


def reduce_shards(terms, axis, size):
    terms = dict(terms)
    for bit in bits_of(size):
        for mask in [m for m in terms if m & bit]:
            terms[mask ^ bit] = add_low(terms[mask ^ bit], swap(terms.pop(mask), axis, size, bit))
    return terms[0]


def sum_kernel(*refs, groups):
    outs = refs[sum(groups) :]
    for out, group in zip(outs, groups):
        total = refs[0][...].astype(F32)
        for ref in refs[1:group]:
            total = total + ref[...].astype(F32)
        out[...] = total.astype(BF)
        refs = refs[group:]


def add_groups(groups):
    if all(len(group) == 1 for group in groups):
        return [group[0] for group in groups]
    shapes = [group[0].shape for group in groups]
    turns = 4 if all(shape[0] % 64 == 0 and shape[0] >= 512 for shape in shapes) else 1
    spec = lambda shape: row_spec(shape[0] // turns, shape[1])
    return pl.pallas_call(
        functools.partial(sum_kernel, groups=[len(group) for group in groups]),
        grid=(turns,),
        in_specs=[spec(array.shape) for group in groups for array in group],
        out_specs=[spec(shape) for shape in shapes],
        out_shape=[shaped(shape, BF) for shape in shapes],
        compiler_params=params(),
        cost_estimate=cost(0.001),
        name="add",
    )(*[array for group in groups for array in group])


def split_kernel(index_ref, *refs, count, groups, deps):
    outs = refs[sum(groups) + deps :]
    totals = []
    for group in groups:
        total = refs[0][...].astype(F32)
        for ref in refs[1:group]:
            total = total + ref[...].astype(F32)
        totals.append(total.astype(BF))
        refs = refs[group:]
    size = totals[0].shape[0]
    for k in range(count):

        @pl.when(pl.program_id(0) == k)
        def _():
            for place, total in enumerate(totals):
                outs[k][place * size : (place + 1) * size, :] = total


def split_call(groups, index, count, deps=()):
    rows, cols = groups[0][0].shape
    part = (rows // count, cols)
    piece = (len(groups) * part[0], cols)
    parts = [array for group in groups for array in group]
    spec = pltpu.PrefetchScalarGridSpec(
        num_scalar_prefetch=1,
        grid=(count,),
        in_specs=[pl.BlockSpec(part, lambda k, f: (f[0] ^ k, 0))] * len(parts)
        + [pl.BlockSpec(memory_space=pl.ANY)] * len(deps),
        out_specs=[pl.BlockSpec(piece, lambda k, f: (0, 0))] * count,
    )
    return pl.pallas_call(
        functools.partial(
            split_kernel, count=count, groups=[len(group) for group in groups], deps=len(deps)
        ),
        grid_spec=spec,
        out_shape=[shaped(piece, BF)] * count,
        compiler_params=params(),
        cost_estimate=cost(0.001),
        name="split",
    )(jnp.reshape(index, (1,)).astype(jnp.int32), *parts, *deps)


def assemble_kernel(index_ref, *refs, groups):
    step = pl.program_id(0)
    size = refs[-1].shape[0]
    rows = pl.ds(pl.multiple_of(step % groups * size, size), size)
    for k, ref in enumerate(refs[:-1]):

        @pl.when(step // groups == k)
        def _():
            refs[-1][...] = ref[rows, :].astype(refs[-1].dtype)


def assemble_call(pieces, index, dtype, groups=1):
    count = len(pieces)
    rows, cols = pieces[0].shape
    spec = pltpu.PrefetchScalarGridSpec(
        num_scalar_prefetch=1,
        grid=(count * groups,),
        in_specs=[pl.BlockSpec((rows, cols), lambda i, f: (0, 0))] * count,
        out_specs=pl.BlockSpec(
            (rows // groups, cols), lambda i, f: (i % groups * count + (f[0] ^ (i // groups)), 0)
        ),
    )
    return pl.pallas_call(
        functools.partial(assemble_kernel, groups=groups),
        grid_spec=spec,
        out_shape=shaped((rows * count, cols), dtype),
        compiler_params=params(),
        cost_estimate=cost(0.001),
        name="assemble",
    )(jnp.reshape(index, (1,)).astype(jnp.int32), *pieces)


def unfold_kernel(part_ref, out_ref):
    out_ref[...] = part_ref[...].astype(F32)


def unfold_call(parts, groups, deps):
    count, rows, cols = parts.shape
    far = count // 2
    own = far // groups

    def place(i):
        group, near, piece = i // (2 * own), i // own % 2, i % own
        return (2 * (group * own + piece) + near, 0, 0)

    return call_after(
        unfold_kernel,
        deps,
        grid=(count,),
        in_specs=[pl.BlockSpec((None, rows, cols), place)],
        out_specs=row_spec(rows, cols),
        out_shape=shaped((count * rows, cols), F32),
        compiler_params=params(),
        cost_estimate=cost(0.001),
        name="unfold",
    )(parts)


class Steps:
    def __init__(self):
        self.jobs, self.token, self.ties = [], None, []

    def swap(self, value, axis, size, bit):
        if self.token is not None:
            value = after(value, self.token)
        return swap(value, axis, size, bit)

    def arrive(self, value):
        return value if self.token is None else after(value, self.token)

    def step(self, token=None):
        self.token = token
        self.ties, jobs = [], []
        for job in self.jobs:
            try:
                self.ties = self.ties + next(job)
            except StopIteration:
                continue
            jobs.append(job)
        self.jobs = jobs
        return self.ties if token is None else self.ties + [token]

    def finish(self):
        while self.jobs:
            self.step()


def gather_job(steps, own, shards, axis, size, hold):
    shards[0] = own
    even = {0: own}
    shards[1] = steps.swap(own, axis, size, 1)
    for bit in reversed(bits_of(size)[1:]):
        new = {mask ^ bit: steps.swap(part, axis, size, bit) for mask, part in even.items()}
        for _ in range(hold):
            yield []
        new = {mask: steps.arrive(part) for mask, part in new.items()}
        even.update(new)
        for mask, part in new.items():
            shards[mask] = part
            shards[mask ^ 1] = steps.swap(part, axis, size, 1)
        yield list(new.values())


class Sums:
    def __init__(self, steps, size, lags):
        self.steps, self.size, self.lags = steps, size, lags
        self.parts = {mask: [[] for _ in lags] for mask in range(size)}
        nearest_first = sorted(range(1, size), key=lambda mask: (mask & -mask, mask))
        steps.jobs += [self.send(mask) for mask in nearest_first]

    def full(self, mask, places):
        low = mask & -mask if mask else self.size
        return all(len(self.parts[mask][i]) == low.bit_length() for i in places)

    def add(self, mask, terms):
        for part, term in zip(self.parts[mask], terms):
            part.append(term)

    def send(self, mask):
        every = range(len(self.lags))
        while not self.full(mask, every):
            yield []
        bit = mask & -mask
        values = list(add_groups(self.parts[mask]))
        lags = self.lags if bit > 1 else [0] * len(values)
        flying, ready = {}, values if bit > 1 else []
        for turn in range(max(lags) + 2):
            for i in every:
                if turn == lags[i] + 1:
                    other = self.steps.arrive(flying[i])
                    self.parts[mask ^ bit][i].append(other)
                    ready = ready + [other]
                if turn == lags[i]:
                    flying[i] = self.steps.swap(values[i], "mp", self.size, bit)
            yield ready
            ready = []


def sum_everywhere(shared, by_shard, n_mp, n_dp):
    rows = shared.shape[0]
    for axis, size in (("mp", n_mp), ("dp", n_dp)):
        for bit in bits_of(size):
            sent = by_shard
            if axis == "mp":
                pairs = (size // (2 * bit), 2, bit * by_shard.shape[1], by_shard.shape[2])
                sent = by_shard.reshape(pairs)[:, ::-1]
            sent = jnp.concatenate([shared, sent.reshape(-1, shared.shape[1])], axis=0)
            other = swap(sent, axis, size, bit)
            shared = add_low(shared, other[:rows])
            by_shard = add_low(by_shard, other[rows:].reshape(by_shard.shape))
    return shared, by_shard[0]


def spread_job(steps, sums, places, n_dp, offload, out, name):
    while not sums.full(0, places):
        yield []
    index = lax.axis_index("dp")
    count = n_dp // 2
    keep, send = split_call([sums.parts[0][i] for i in places], index % 2, 2)
    other = steps.swap(send, "dp", n_dp, 1)
    yield [send]
    pieces = split_call([[keep, steps.arrive(other)]], index // 2, count, steps.ties)
    others = [steps.swap(pieces[k], "dp", n_dp, 2 * k) for k in range(1, count)]
    yield [other, *pieces]
    (total,) = add_groups([[pieces[0]] + [steps.arrive(part) for part in others]])
    if offload:
        whole = lax.all_gather(total, "dp", axis=0)
        yield [total]
        yield []
        out[name] = steps.arrive(whole)
        yield [whole]
        return
    others = [steps.swap(total, "dp", n_dp, 2 * k) for k in range(1, count)]
    yield others[:1] if steps.token is None else [total]
    half = assemble_call([total] + [steps.arrive(part) for part in others], index // 2, BF)
    other = steps.swap(half, "dp", n_dp, 1)
    yield [half]
    other = steps.arrive(other)
    out[name] = assemble_call([half, other], index % 2, F32, len(places))
    yield [other]


def place_hot():
    place = jnp.arange(FRAME)
    row, col = place // WIN_W, place % WIN_W
    offset = (row[:, None] - row[None, :] + WIN_H - 1) * N_COL + (
        col[:, None] - col[None, :] + WIN_W - 1
    )
    return (offset.reshape(1, -1) == jnp.arange(N_ROW * N_COL)[:, None]).astype(F32)


def bias_blocks(rel_table):
    heads = rel_table.shape[0]
    cube = rel_table.reshape(heads * N_TIME, N_ROW * N_COL)
    return lax.dot(cube, place_hot(), precision=highest).reshape(heads, N_TIME, FRAME, FRAME)


def collect_blocks(block_grad):
    heads = block_grad.shape[0]
    flat = block_grad.reshape(heads * N_TIME, FRAME * FRAME)
    cube = lax.dot_general(flat, place_hot(), (((1,), (1,)), ((), ())), precision=highest)
    return cube[:, ::-1].reshape(heads, -1)


def block_spec(heads, place):
    return pl.BlockSpec((heads, N_TIME, FRAME, FRAME), lambda i: (place, 0, 0, 0))


def frame_span(frame):
    return slice(frame * FRAME, (frame + 1) * FRAME)


def spread_blocks(blocks_ref, table, fill, transposed):
    for head in range(table.shape[0]):
        for offset in range(N_TIME):
            block = blocks_ref[head, offset]
            if transposed:
                block = block.T
            for query in range(WIN_T):
                key = query - (offset - WIN_T + 1)
                if 0 <= key < WIN_T:
                    row, col = (key, query) if transposed else (query, key)
                    table[head, frame_span(row), frame_span(col)] = block
        table[head, :, WIN_TOK:] = jnp.full((WIN_TOK, PAD_TOK - WIN_TOK), fill, F32)


def norm_kernel(tokens_ref, mod_ref, attn_in_ref):
    normed, _ = normalise(tokens_ref[...].astype(F32))
    attn_in_ref[...] = (normed * (1.0 + mod_ref[0, 1:2]) + mod_ref[0, 0:1]).astype(BF)


def norm_call(tokens, mods, deps=()):
    rows, width = tokens.shape
    return call_after(
        norm_kernel,
        deps,
        grid=(rows // WIN_TOK,),
        in_specs=[row_spec(WIN_TOK, width), mod_spec(1, mods.shape[1], width)],
        out_specs=row_spec(WIN_TOK, width),
        out_shape=shaped((rows, width), BF),
        compiler_params=params(),
        cost_estimate=cost(8),
        name="norm_in",
    )(tokens, mods)


def head_copies(value, heads):
    if heads == 1:
        return [value]
    lane = lax.broadcasted_iota(jnp.int32, value.shape, 1) // HEAD_DIM
    return [jnp.where(lane == head, value, jnp.zeros_like(value)) for head in range(heads)]


def pad_rows(value):
    return jnp.concatenate(
        [value, jnp.zeros((PAD_TOK - WIN_TOK, value.shape[1]), value.dtype)], axis=0
    )


def attend_kernel(x_ref, w_ref, blocks_ref, qkv_ref, mixed_ref, lse_ref, table, columns):
    heads = blocks_ref.shape[0]

    @pl.when(pl.program_id(0) == 0)
    def _():
        spread_blocks(blocks_ref, table, -1e30, False)
        columns[...] = jnp.zeros_like(columns)

    x = x_ref[...]
    queries = dot(x, w_ref[0]).astype(BF)
    keys = dot(x, w_ref[1]).astype(BF)
    values = dot(x, w_ref[2]).astype(BF)
    qkv_ref[0] = queries
    qkv_ref[1] = keys
    qkv_ref[2] = values
    scaled = queries * jnp.asarray(HEAD_DIM**-0.5, BF)
    for window in range(x.shape[0] // WIN_TOK):
        span = window_span(window)
        scores = dot(
            jnp.concatenate(head_copies(scaled[span], heads), axis=0), pad_rows(keys[span]), 1, 1
        )
        probs = []
        for head in range(heads):
            score = scores[window_span(head)] + table[head]
            top = jnp.max(score, axis=1, keepdims=True)
            exponent = jnp.exp(score - top)
            total = jnp.sum(exponent, axis=1, keepdims=True)
            probs.append((exponent * (1.0 / total)).astype(BF))
            columns[window, :WIN_TOK, head : head + 1] = top + jnp.log(total)
        value = jnp.concatenate([pad_rows(part) for part in head_copies(values[span], heads)], axis=0)
        mixed_ref[span, :] = dot(jnp.concatenate(probs, axis=1), value).astype(BF)
        lse_ref[window] = columns[window].T[: lse_ref.shape[1]]


def attend_call(attn_in, weight, blocks, deps=()):
    rows, width = attn_in.shape
    cols = weight.shape[2]
    blocks, place, heads = blocks
    windows = rows // WIN_TOK
    per = per_step(rows)
    block = per * WIN_TOK
    stat_rows = -(-heads // 8) * 8
    return call_after(
        attend_kernel,
        deps,
        grid=(windows // per,),
        in_specs=[row_spec(block, width), whole_spec(weight.shape), block_spec(heads, place)],
        out_specs=[
            part_spec(block, cols),
            row_spec(block, cols),
            mod_spec(per, stat_rows, PAD_TOK),
        ],
        out_shape=[
            shaped((3, rows, cols), BF),
            shaped((rows, cols), BF),
            shaped((windows, stat_rows, PAD_TOK), F32),
        ],
        scratch_shapes=[
            pltpu.VMEM((heads, WIN_TOK, PAD_TOK), F32),
            pltpu.VMEM((per, PAD_TOK, 128), F32),
        ],
        compiler_params=params(),
        cost_estimate=cost(19),
        name="attend",
    )(attn_in, weight, blocks)


def attend_back_kernel(
    grad_ref, out_w_ref, qkv_ref, mixed_ref, lse_ref, blocks_ref, x_ref, dqkv_ref, dblocks_ref, dw_ref, table, total, x_all, grad_all, d_all
):
    heads = blocks_ref.shape[0]
    cols = out_w_ref.shape[0]
    step = pl.program_id(0)

    @pl.when(step == 0)
    def _():
        spread_blocks(blocks_ref, table, 0.0, True)
        total[...] = jnp.zeros_like(total)

    grads_mixed = dot(grad_ref[...], out_w_ref[...], 1, 1).astype(BF)
    scale = jnp.asarray(HEAD_DIM**-0.5, BF)
    head_rows = (lse_ref.shape[1], cols)
    head_hot = (
        lax.broadcasted_iota(jnp.int32, head_rows, 1) // HEAD_DIM
        == lax.broadcasted_iota(jnp.int32, head_rows, 0)
    ).astype(BF)
    block = grad_ref.shape[0]
    rows = pl.ds(pl.multiple_of(step * block, block), block)
    x_all[rows, :] = x_ref[...]
    grad_all[rows, :] = grad_ref[...]
    d_all[3, rows, :] = mixed_ref[...]
    for window in range(block // WIN_TOK):
        place = window_span(window)
        grad_mixed = grads_mixed[place]
        query = qkv_ref[0, place, :]
        key = qkv_ref[1, place, :]
        value = qkv_ref[2, place, :]
        product = grad_mixed.astype(F32) * mixed_ref[place, :].astype(F32)
        upper = product.astype(BF)
        lower = (product - upper.astype(F32)).astype(BF)
        inner = dot(head_hot, pad_rows(upper), 1, 1) + dot(head_hot, pad_rows(lower), 1, 1)
        keys = jnp.concatenate(head_copies(key * scale, heads), axis=0)
        values = jnp.concatenate(head_copies(value, heads), axis=0)
        query_pad = pad_rows(query)
        grad_pad = pad_rows(grad_mixed)
        scores = dot(keys, query_pad, 1, 1)
        grad_probs = dot(values, grad_pad, 1, 1)
        probs = []
        grad_scores = []
        for head in range(heads):
            span = window_span(head)
            prob = jnp.exp(scores[span] + table[head] - lse_ref[window, head : head + 1, :])
            grad_score = (prob * (grad_probs[span] - inner[head : head + 1, :])).astype(BF)
            probs.append(prob.astype(BF))
            grad_scores.append(grad_score)
            total[head] += grad_score.astype(F32)
        wide = jnp.concatenate(grad_scores, axis=1)
        grad_value = dot(
            jnp.concatenate(probs, axis=1), jnp.concatenate(head_copies(grad_pad, heads), axis=0)
        )
        grad_key = dot(wide, jnp.concatenate(head_copies(query_pad * scale, heads), axis=0))
        grad_query = dot(jnp.concatenate(grad_scores, axis=0), keys, 0, 0)[:WIN_TOK]
        own = pl.ds(pl.multiple_of(step * block + window * WIN_TOK, WIN_TOK), WIN_TOK)
        for part, grad in enumerate((grad_query, grad_key, grad_value)):
            grad = grad.astype(BF)
            dqkv_ref[part, place, :] = grad
            d_all[part, own, :] = grad

    @pl.when(step == pl.num_programs(0) - 1)
    def _():
        for part in range(4):
            left = grad_all if part == 3 else x_all
            dw_ref[part] = dot(left[...], d_all[part], 0, 0).astype(BF)
        for head in range(heads):
            for offset in range(N_TIME):
                block = None
                for query in range(WIN_T):
                    key = query - (offset - WIN_T + 1)
                    if 0 <= key < WIN_T:
                        part = total[head, frame_span(key), frame_span(query)]
                        block = part if block is None else block + part
                dblocks_ref[head, offset] = block


def attend_back_call(grad_attn, out_weight, qkv, mixed, lse, blocks, attn_in, deps=()):
    rows, width = grad_attn.shape
    cols = out_weight.shape[0]
    blocks, place, heads = blocks
    per = per_step(rows)
    block = per * WIN_TOK
    return call_after(
        attend_back_kernel,
        deps,
        grid=(rows // block,),
        in_specs=[
            row_spec(block, width),
            whole_spec(out_weight.shape),
            part_spec(block, cols),
            row_spec(block, cols),
            mod_spec(per, lse.shape[1], PAD_TOK),
            block_spec(heads, place),
            row_spec(block, width),
        ],
        out_specs=[
            part_spec(block, cols),
            block_spec(heads, 0),
            whole_spec((4, width, cols)),
        ],
        out_shape=[
            shaped((3, rows, cols), BF),
            shaped((heads,) + blocks.shape[1:], F32),
            shaped((4, width, cols), BF),
        ],
        scratch_shapes=[pltpu.VMEM((heads, WIN_TOK, PAD_TOK), F32)] * 2
        + [pltpu.VMEM((rows, width), BF)] * 2
        + [pltpu.VMEM((4, rows, cols), BF)],
        compiler_params=params(),
        cost_estimate=cost(30),
        name="attend_back",
    )(grad_attn, out_weight, qkv, mixed, lse, blocks, attn_in)


def middle_kernel(*refs, count):
    mixed_refs = refs[:count]
    weight_refs = refs[count : 2 * count]
    tokens_ref, cot_ref, mod_ref, attn_out_ref, mlp_in_ref, grad_mlp_ref = refs[2 * count :]
    attn_out = dot(mixed_refs[0][...], weight_refs[0][...])
    for mixed_ref, weight_ref in zip(mixed_refs[1:], weight_refs[1:]):
        attn_out = attn_out + dot(mixed_ref[...], weight_ref[...])
    attn_out_ref[...] = attn_out.astype(BF)
    for window in range(attn_out.shape[0] // WIN_TOK):
        span = window_span(window)
        mod = mod_ref[window]
        resid = tokens_ref[span, :].astype(F32) + mod[2:3] * attn_out[span]
        normed, _ = normalise(resid)
        mlp_in_ref[span, :] = (normed * (1.0 + mod[4:5]) + mod[3:4]).astype(BF)
        grad_mlp_ref[span, :] = (mod[5:6] * cot_ref[span, :].astype(F32)).astype(BF)


def middle_call(mixed, weights, tokens, cotangent, mods, deps=()):
    rows, width = tokens.shape
    count = len(mixed)
    per = per_step(rows)
    block = per * WIN_TOK
    row = row_spec(block, width)
    return call_after(
        functools.partial(middle_kernel, count=count),
        deps,
        grid=(rows // block,),
        in_specs=[row_spec(block, part.shape[1]) for part in mixed]
        + [whole_spec(part.shape) for part in weights]
        + [row, row, mod_spec(per, mods.shape[1], width)],
        out_specs=[row, row, row],
        out_shape=[
            shaped((rows, width), BF),
            shaped((rows, width), BF),
            shaped((rows, width), BF),
        ],
        compiler_params=params(),
        cost_estimate=cost(16),
        name="middle",
    )(*mixed, *weights, tokens, cotangent, mods)


def mlp_kernel(
    x_ref, g_ref, up_ref, down_ref, act_ref, ghid_ref, *rest, chunk
):
    down_total, up_total = rest[4:]
    step = pl.program_id(0)
    x = x_ref[...]
    g = g_ref[...]
    for start in range(0, up_ref.shape[1], chunk):
        span = slice(start, start + chunk)
        hidden = dot(x, up_ref[:, span])
        grad_act = dot(g, down_ref[span, :], 1, 1)
        cubic = GELU_B * (hidden * hidden)
        gate = 0.5 + 0.5 * jnp.tanh(hidden * (GELU_A + cubic))
        act_ref[:, span] = (hidden * gate).astype(BF)
        slope = gate + gate * ((1.0 - gate) * (hidden * (2.0 * GELU_A + 6.0 * cubic)))
        ghid_ref[:, span] = (grad_act * slope).astype(BF)

    @pl.when(step == 0)
    def _():
        down_total[...] = dot(act_ref[...], g, 0, 0)
        up_total[...] = dot(x, ghid_ref[...], 0, 0)

    @pl.when(step > 0)
    def _():
        down_total[...] += dot(act_ref[...], g, 0, 0)
        up_total[...] += dot(x, ghid_ref[...], 0, 0)

    @pl.when(step == pl.num_programs(0) - 1)
    def _():
        for place, total in enumerate((down_total, up_total)):
            size = total.shape[0] // 2
            rest[2 * place][...] = total[:size].astype(BF)
            rest[2 * place + 1][...] = total[size:].astype(BF)


MLP_BLOCK = 1280
MLP_CHUNK = 512


def mlp_call(x, g, up, down, deps=()):
    rows, width = x.shape
    hidden = up.shape[1]
    block = MLP_BLOCK if rows % MLP_BLOCK == 0 else WIN_TOK
    row = row_spec(block, width)
    wide = row_spec(block, hidden)
    halves = [(hidden // 2, width)] * 2 + [(width // 2, hidden)] * 2
    return call_after(
        functools.partial(mlp_kernel, chunk=min(MLP_CHUNK, hidden)),
        deps,
        grid=(rows // block,),
        in_specs=[row, row, whole_spec(up.shape), whole_spec(down.shape)],
        out_specs=[wide, wide] + [whole_spec(shape) for shape in halves],
        out_shape=[
            shaped((rows, hidden), BF),
            shaped((rows, hidden), BF),
        ]
        + [shaped(shape, BF) for shape in halves],
        scratch_shapes=[pltpu.VMEM(down.shape, F32), pltpu.VMEM(up.shape, F32)],
        compiler_params=params(),
        cost_estimate=cost(30),
        name="mlp",
    )(x, g, up, down)


def mlp_out_kernel(*refs, count):
    act_refs, ghid_refs, down_refs, up_refs = [
        refs[place * count : (place + 1) * count] for place in range(4)
    ]
    tokens_ref, cot_ref, attn_out_ref, mod_ref, out_ref, gres_ref, gattn_ref, sums_ref = refs[
        4 * count :
    ]
    join = lambda parts, axis: jnp.concatenate([part[...] for part in parts], axis=axis)
    mlp_outs = dot(join(act_refs, 1), join(down_refs, 0))
    gins = dot(join(ghid_refs, 1), join(up_refs, 1), 1, 1)
    for window in range(gins.shape[0] // WIN_TOK):
        span = window_span(window)
        mod = mod_ref[window]
        mlp_out, gin = mlp_outs[span], gins[span]
        cot = cot_ref[span, :].astype(F32)
        attn_out = attn_out_ref[span, :].astype(F32)
        resid = tokens_ref[span, :].astype(F32) + mod[2:3] * attn_out
        out_ref[span, :] = (resid + mod[5:6] * mlp_out).astype(BF)
        normed, inverse = normalise(resid)
        gres = cot + normalise_back(normed, inverse, gin * (1.0 + mod[4:5]))
        gres_ref[span, :] = gres.astype(BF)
        gattn_ref[span, :] = (mod[2:3] * gres).astype(BF)
        sums_ref[window, 0:1] = jnp.sum(gres * attn_out, axis=0, keepdims=True)
        sums_ref[window, 1:2] = jnp.sum(gin, axis=0, keepdims=True)
        sums_ref[window, 2:3] = jnp.sum(gin * normed, axis=0, keepdims=True)
        sums_ref[window, 3:4] = jnp.sum(cot * mlp_out, axis=0, keepdims=True)


def kept_spec(shape):
    return pl.BlockSpec(shape, lambda i: (0,) * len(shape), pipeline_mode=pl.Buffered(1))


def mlp_out_call(act, ghid, down, up, tokens, cotangent, attn_out, mods, deps=()):
    rows, width = tokens.shape
    per = 1
    block = per * WIN_TOK
    row = row_spec(block, width)
    windows = rows // WIN_TOK
    return call_after(
        functools.partial(mlp_out_kernel, count=len(act)),
        deps,
        grid=(windows // per,),
        in_specs=[row_spec(block, part.shape[1]) for part in act + ghid]
        + [kept_spec(part.shape) for part in down + up]
        + [row, row, row, mod_spec(per, mods.shape[1], width)],
        out_specs=[row, row, row, mod_spec(per, 4, width)],
        out_shape=[
            shaped((rows, width), BF),
            shaped((rows, width), BF),
            shaped((rows, width), BF),
            shaped((windows, 4, width), F32),
        ],
        compiler_params=params(),
        cost_estimate=cost(55),
        name="mlp_out",
    )(*act, *ghid, *down, *up, tokens, cotangent, attn_out, mods)


def last_kernel(*refs, count):
    dqkv_refs = refs[:count]
    weight_refs = refs[count : 2 * count]
    tokens_ref, gres_ref, mod_ref, out_ref, sums_ref = refs[2 * count :]
    join = lambda refs: jnp.concatenate([ref[part] for ref in refs for part in range(3)], axis=1)
    gin = dot(join(dqkv_refs), join(weight_refs), 1, 1)
    for window in range(gin.shape[0] // WIN_TOK):
        span = window_span(window)
        normed, inverse = normalise(tokens_ref[span, :].astype(F32))
        grad = gin[span]
        out_ref[span, :] = (
            gres_ref[span, :].astype(F32) + normalise_back(normed, inverse, grad * (1.0 + mod_ref[window, 1:2]))
        ).astype(BF)
        sums_ref[window, 0:1] = jnp.sum(grad, axis=0, keepdims=True)
        sums_ref[window, 1:2] = jnp.sum(grad * normed, axis=0, keepdims=True)


def last_call(dqkv, weights, tokens, gres, mods, deps=()):
    rows, width = tokens.shape
    count = len(dqkv)
    per = 1
    block = per * WIN_TOK
    row = row_spec(block, width)
    windows = rows // WIN_TOK
    return call_after(
        functools.partial(last_kernel, count=count),
        deps,
        grid=(windows // per,),
        in_specs=[part_spec(block, part.shape[2]) for part in dqkv]
        + [kept_spec(part.shape) for part in weights]
        + [row, row, mod_spec(per, mods.shape[1], width)],
        out_specs=[row, mod_spec(per, 2, width)],
        out_shape=[shaped((rows, width), BF), shaped((windows, 2, width), F32)],
        compiler_params=params(),
        cost_estimate=cost(28),
        name="last",
    )(*dqkv, *weights, tokens, gres, mods)


def body(
    n_dp,
    n_mp,
    tokens,
    cotangent,
    qkv_weight,
    out_weight,
    up_weight,
    down_weight,
    rel_bias,
    ada_weight,
    ada_bias,
    class_embed,
    window_clip,
    timesteps,
    class_ids,
):
    mp_index = lax.axis_index("mp")
    micro, local_rows, width = tokens.shape
    local_cols = class_embed.shape[1]
    clips = timesteps.shape[1]
    own_windows = local_rows // WIN_TOK
    rows = micro * local_rows
    tokens_flat = tokens.reshape(rows, width)
    cot_flat = cotangent.reshape(rows, width)
    masks = range(n_mp)

    columns = mp_index * local_cols + jnp.arange(local_cols)
    half_width = width // 2
    freq_index = (columns % half_width).astype(F32)
    frequency = jnp.exp(-math.log(10000.0) * freq_index / half_width)
    angle = timesteps.astype(F32)[..., None] * frequency
    step_embed = jnp.where(columns < half_width, jnp.sin(angle), jnp.cos(angle))
    class_hot = (class_ids[..., None] == jnp.arange(class_embed.shape[0])).astype(F32)
    condition = step_embed + jnp.einsum("mck,kd->mcd", class_hot, class_embed, precision=highest)
    lowered = jax.nn.silu(condition).astype(BF)
    mod_terms = jnp.einsum("mcd,de->mce", lowered, ada_weight, preferred_element_type=F32)
    near_terms = add_low(mod_terms, swap(mod_terms, "mp", n_mp, 1))
    modulation = near_terms
    for bit in bits_of(n_mp)[1:]:
        modulation = add_low(modulation, swap(modulation, "mp", n_mp, bit))
    modulation = modulation + ada_bias
    own_clip = lax.dynamic_slice_in_dim(window_clip, mp_index * own_windows, own_windows, 1)
    clip_hot = (own_clip[..., None] == jnp.arange(clips)).astype(F32)
    mods = jnp.einsum("mwc,mce->mwe", clip_hot, modulation, precision=highest)
    mods = mods.reshape(micro * own_windows, 6, width)

    steps = Steps()
    rel_tables = gather_shards(rel_bias, "mp", n_mp)
    blocks = bias_blocks(jnp.concatenate([rel_tables[m] for m in masks], axis=0))
    heads = rel_bias.shape[0]

    def gather(own, hold):
        shards = {}
        steps.jobs.append(gather_job(steps, own, shards, "mp", n_mp, hold))
        return shards

    def need(shards, mask, ties, token):
        while mask not in shards:
            ties = ties + steps.step(token)
        return ties

    qkv_w = gather(qkv_weight, 3)
    steps.step(modulation)
    attn_in = norm_call(tokens_flat, mods)
    out_w = gather(out_weight, 3)
    ties = steps.step(attn_in)
    qkv, mixed, lse = {}, {}, {}
    for m in masks:
        ties = need(qkv_w, m, ties, attn_in)
        qkv[m], mixed[m], lse[m] = attend_call(attn_in, qkv_w[m], (blocks, m, heads), ties)
        if m == 0:
            down_w = gather(down_weight, 4)
        elif m == 2 or m == n_mp - 1 == 1:
            up_w = gather(up_weight, 3)
        ties = steps.step(mixed[m])
    for m in masks:
        ties = need(out_w, m, ties, mixed[0])
    attn_out, mlp_in, grad_mlp = middle_call(
        [mixed[m] for m in masks], [out_w[m] for m in masks], tokens_flat, cot_flat, mods, ties
    )
    ties = steps.step(mlp_in)
    wide_sums = Sums(steps, n_mp, [0, 1, 1, 2])
    grads = {}
    steps.jobs.append(spread_job(steps, wide_sums, [0, 1], n_dp, True, grads, "down"))
    steps.jobs.append(spread_job(steps, wide_sums, [2, 3], n_dp, False, grads, "up"))
    act, grad_hidden = {}, {}
    for m in [m for m in masks if m % 2] + [m for m in reversed(masks) if m % 2 == 0]:
        ties = need(down_w, m, need(up_w, m, ties, mlp_in), mlp_in)
        act[m], grad_hidden[m], *wide_terms = mlp_call(mlp_in, grad_mlp, up_w[m], down_w[m], ties)
        wide_sums.add(m, wide_terms)
        ties = steps.step(wide_terms[0])
    block_out, grad_resid, grad_attn, late_sums = mlp_out_call(
        *[[part[m] for m in masks] for part in (act, grad_hidden, down_w, up_w)],
        tokens_flat,
        cot_flat,
        attn_out,
        mods,
        ties,
    )

    def clip_sums(window_sums):
        grouped = window_sums.reshape(micro, own_windows, -1)
        return jnp.einsum("mwc,mwe->mce", clip_hot, grouped, precision=highest).astype(BF)

    attn_sums = Sums(steps, n_mp, [0])
    steps.jobs.append(spread_job(steps, attn_sums, [0], n_dp, False, grads, "qkv"))
    dqkv, block_grads = {}, {}
    ties = steps.step(grad_attn)
    for m in reversed(masks):
        dqkv[m], block_grads[m], qkv_term = attend_back_call(
            grad_attn, out_w[m], qkv[m], mixed[m], lse[m], (blocks, m, heads), attn_in, ties
        )
        attn_sums.add(m, [qkv_term.reshape(-1, qkv_term.shape[2])])
        ties = steps.step(qkv_term)
    token_grad, early_sums = last_call(
        [dqkv[m] for m in masks], [qkv_w[m] for m in masks], tokens_flat, grad_resid, mods, ties
    )
    ties = steps.step(token_grad)
    window_sums = after(jnp.concatenate([early_sums, late_sums], axis=1), *ties)
    rel_sums = after(jnp.concatenate([block_grads[m] for m in masks], axis=0), *ties)
    rel_sums = collect_blocks(rel_sums).astype(BF).reshape(n_mp, -1)
    table_size = rel_sums.shape[1]
    rel_sums = jnp.pad(rel_sums, ((0, 0), (0, -table_size % width))).reshape(n_mp, -1, width)
    clip_terms = clip_sums(window_sums).reshape(-1, width)
    ties = steps.step()
    mod_total, rel_total = sum_everywhere(
        after(clip_terms, *ties), after(rel_sums, *ties), n_mp, n_dp
    )
    rel_grad = rel_total.reshape(-1)[:table_size].reshape(rel_bias.shape).astype(F32)
    steps.finish()

    down_grad = unfold_call(grads["down"], 2, ties)
    up_grad = grads["up"]
    qkv_grad = grads["qkv"][: 3 * width].reshape(qkv_weight.shape)
    out_grad = grads["qkv"][3 * width :].T
    mod_total = mod_total.astype(F32).reshape(micro, clips, 6 * width)
    ada_bias_grad = jnp.sum(mod_total, axis=(0, 1))
    ada_weight_grad = jnp.einsum(
        "mcd,mce->de", lowered.astype(F32), mod_total, precision=highest
    )
    grad_lowered = jnp.einsum(
        "mce,de->mcd", mod_total, ada_weight.astype(F32), precision=highest
    )
    grad_condition = jax.vjp(jax.nn.silu, condition)[1](grad_lowered)[0]
    class_grad = jnp.einsum("mck,mcd->kd", class_hot, grad_condition, precision=highest)
    return (
        block_out.reshape(tokens.shape),
        token_grad.reshape(tokens.shape),
        qkv_grad,
        out_grad,
        up_grad,
        down_grad,
        rel_grad,
        ada_weight_grad,
        ada_bias_grad,
        class_grad,
    )


def solution(mesh):
    rows = P(None, ("dp", "mp"), None)
    in_specs = (
        rows,
        rows,
        P(None, None, "mp"),
        P("mp", None),
        P(None, "mp"),
        P("mp", None),
        P("mp", None),
        P("mp", None),
        P(),
        P(None, "mp"),
        P(None, "dp"),
        P(),
        P(),
    )
    out_specs = (
        rows,
        rows,
        P(None, None, "mp"),
        P("mp", None),
        P(None, "mp"),
        P("mp", None),
        P("mp", None),
        P("mp", None),
        P(),
        P(None, "mp"),
    )
    step = functools.partial(body, mesh.shape["dp"], mesh.shape["mp"])
    return jax.shard_map(step, mesh=mesh, in_specs=in_specs, out_specs=out_specs, check_vma=False)
```

```python
import functools
import math

import jax
import jax.numpy as jnp
from jax import lax
from jax.experimental import pallas as pl
from jax.experimental.pallas import tpu as pltpu
from jax.sharding import PartitionSpec as P

WIN_T = 5
WIN_H = 8
WIN_W = 8
WIN_TOK = WIN_T * WIN_H * WIN_W
FRAME = WIN_H * WIN_W
PAD_TOK = 384
HEAD_DIM = 64
N_TIME, N_ROW, N_COL = 2 * WIN_T - 1, 2 * WIN_H - 1, 2 * WIN_W - 1

BF = jnp.bfloat16
F32 = jnp.float32
epsilon = 1e-06
highest = lax.Precision.HIGHEST
GELU_A = 0.7978845608028654
GELU_B = GELU_A * 0.044715
VMEM_LIMIT = 63 * 1024 * 1024


def dot(left, right, left_dim=1, right_dim=0):
    return lax.dot_general(
        left, right, (((left_dim,), (right_dim,)), ((), ())), preferred_element_type=F32
    )


def params():
    return pltpu.CompilerParams(vmem_limit_bytes=VMEM_LIMIT)


def shaped(shape, dtype):
    return jax.ShapeDtypeStruct(shape, dtype)


def row_spec(rows, cols):
    return pl.BlockSpec((rows, cols), lambda i: (i, 0))


def part_spec(rows, cols):
    return pl.BlockSpec((3, rows, cols), lambda i: (0, i, 0))


def per_step(rows):
    return 2 if rows % (2 * WIN_TOK) == 0 else 1


def window_span(window):
    return slice(window * WIN_TOK, (window + 1) * WIN_TOK)


def whole_spec(shape):
    return pl.BlockSpec(shape, lambda i: (0,) * len(shape))


def mod_spec(per, count, cols):
    return pl.BlockSpec((per, count, cols), lambda i: (i, 0, 0))


def cost(micros):
    return pl.CostEstimate(
        flops=int(micros * 1e9), bytes_accessed=int(micros * 3.5e6), transcendentals=0
    )


def call_after(kernel, deps, *, in_specs, **rest):
    deps = tuple(deps)
    count = len(in_specs)

    def run(*refs):
        kernel(*refs[:count], *refs[count + len(deps) :])

    call = pl.pallas_call(
        run, in_specs=list(in_specs) + [pl.BlockSpec(memory_space=pl.ANY)] * len(deps), **rest
    )
    return lambda *args: call(*args, *deps)


def after(value, *deps):
    return lax.optimization_barrier((value, *deps))[0]


def normalise(values):
    centred = values - jnp.mean(values, axis=-1, keepdims=True)
    inverse = lax.rsqrt(jnp.mean(centred * centred, axis=-1, keepdims=True) + epsilon)
    return centred * inverse, inverse


def normalise_back(normed, inverse, grad_in):
    return inverse * (
        grad_in
        - jnp.mean(grad_in, axis=-1, keepdims=True)
        - normed * jnp.mean(grad_in * normed, axis=-1, keepdims=True)
    )


def swap(value, axis, size, bit):
    return lax.ppermute(value, axis, [(i, i ^ bit) for i in range(size)])


def bits_of(size):
    return [1 << b for b in range(size.bit_length() - 1)]


def add_low(left, right):
    return (left.astype(F32) + right.astype(F32)).astype(left.dtype)


def gather_shards(own, axis, size):
    shards = {0: own}
    for bit in reversed(bits_of(size)):
        for mask in list(shards):
            shards[mask ^ bit] = swap(shards[mask], axis, size, bit)
    return shards


def reduce_all(value, axis, size):
    for bit in bits_of(size):
        value = add_low(value, swap(value, axis, size, bit))
    return value


def reduce_shards(terms, axis, size):
    terms = dict(terms)
    for bit in bits_of(size):
        for mask in [m for m in terms if m & bit]:
            terms[mask ^ bit] = add_low(terms[mask ^ bit], swap(terms.pop(mask), axis, size, bit))
    return terms[0]


def sum_kernel(*refs, groups):
    outs = refs[sum(groups) :]
    for out, group in zip(outs, groups):
        total = refs[0][...].astype(F32)
        for ref in refs[1:group]:
            total = total + ref[...].astype(F32)
        out[...] = total.astype(BF)
        refs = refs[group:]


def add_groups(groups):
    if all(len(group) == 1 for group in groups):
        return [group[0] for group in groups]
    shapes = [group[0].shape for group in groups]
    turns = 4 if all(shape[0] % 64 == 0 and shape[0] >= 512 for shape in shapes) else 1
    spec = lambda shape: row_spec(shape[0] // turns, shape[1])
    return pl.pallas_call(
        functools.partial(sum_kernel, groups=[len(group) for group in groups]),
        grid=(turns,),
        in_specs=[spec(array.shape) for group in groups for array in group],
        out_specs=[spec(shape) for shape in shapes],
        out_shape=[shaped(shape, BF) for shape in shapes],
        compiler_params=params(),
        cost_estimate=cost(0.001),
        name="add",
    )(*[array for group in groups for array in group])


def split_kernel(index_ref, *refs, count, groups, deps):
    outs = refs[sum(groups) + deps :]
    totals = []
    for group in groups:
        total = refs[0][...].astype(F32)
        for ref in refs[1:group]:
            total = total + ref[...].astype(F32)
        totals.append(total.astype(BF))
        refs = refs[group:]
    size = totals[0].shape[0]
    for k in range(count):

        @pl.when(pl.program_id(0) == k)
        def _():
            for place, total in enumerate(totals):
                outs[k][place * size : (place + 1) * size, :] = total


def split_call(groups, index, count, deps=()):
    rows, cols = groups[0][0].shape
    part = (rows // count, cols)
    piece = (len(groups) * part[0], cols)
    parts = [array for group in groups for array in group]
    spec = pltpu.PrefetchScalarGridSpec(
        num_scalar_prefetch=1,
        grid=(count,),
        in_specs=[pl.BlockSpec(part, lambda k, f: (f[0] ^ k, 0))] * len(parts)
        + [pl.BlockSpec(memory_space=pl.ANY)] * len(deps),
        out_specs=[pl.BlockSpec(piece, lambda k, f: (0, 0))] * count,
    )
    return pl.pallas_call(
        functools.partial(
            split_kernel, count=count, groups=[len(group) for group in groups], deps=len(deps)
        ),
        grid_spec=spec,
        out_shape=[shaped(piece, BF)] * count,
        compiler_params=params(),
        cost_estimate=cost(0.001),
        name="split",
    )(jnp.reshape(index, (1,)).astype(jnp.int32), *parts, *deps)


def assemble_kernel(index_ref, *refs, groups):
    step = pl.program_id(0)
    size = refs[-1].shape[0]
    rows = pl.ds(pl.multiple_of(step % groups * size, size), size)
    for k, ref in enumerate(refs[:-1]):

        @pl.when(step // groups == k)
        def _():
            refs[-1][...] = ref[rows, :].astype(refs[-1].dtype)


def assemble_call(pieces, index, dtype, groups=1):
    count = len(pieces)
    rows, cols = pieces[0].shape
    spec = pltpu.PrefetchScalarGridSpec(
        num_scalar_prefetch=1,
        grid=(count * groups,),
        in_specs=[pl.BlockSpec((rows, cols), lambda i, f: (0, 0))] * count,
        out_specs=pl.BlockSpec(
            (rows // groups, cols), lambda i, f: (i % groups * count + (f[0] ^ (i // groups)), 0)
        ),
    )
    return pl.pallas_call(
        functools.partial(assemble_kernel, groups=groups),
        grid_spec=spec,
        out_shape=shaped((rows * count, cols), dtype),
        compiler_params=params(),
        cost_estimate=cost(0.001),
        name="assemble",
    )(jnp.reshape(index, (1,)).astype(jnp.int32), *pieces)


def attention_grads_kernel(index_ref, own_ref, other_ref, qkv_ref, out_ref):
    step = pl.program_id(0)
    place = 2 * (index_ref[0] ^ (step // 2)) + step % 2
    size = qkv_ref.shape[0]
    rows = pl.ds(pl.multiple_of(step % 2 * size, size), size)
    for k, ref in enumerate((own_ref, other_ref)):

        @pl.when((step // 2 == k) & (place < 3))
        def _():
            qkv_ref[...] = ref[rows, :].astype(F32)

        @pl.when((step // 2 == k) & (place == 3))
        def _():
            out_ref[...] = ref[rows, :].astype(F32).T


def attention_grads_call(halves, index, dtype, groups):
    rows, cols = halves[0].shape
    size = rows // 2
    place = lambda i, f: (jnp.minimum(2 * (f[0] ^ (i // 2)) + i % 2, 2), 0)
    spec = pltpu.PrefetchScalarGridSpec(
        num_scalar_prefetch=1,
        grid=(4,),
        in_specs=[pl.BlockSpec((rows, cols), lambda i, f: (0, 0))] * 2,
        out_specs=[
            pl.BlockSpec((size, cols), place),
            pl.BlockSpec((cols, size), lambda i, f: (0, 0)),
        ],
    )
    return pl.pallas_call(
        attention_grads_kernel,
        grid_spec=spec,
        out_shape=[shaped((3 * size, cols), dtype), shaped((cols, size), dtype)],
        compiler_params=params(),
        cost_estimate=cost(0.001),
        name="attention_grads",
    )(jnp.reshape(index, (1,)).astype(jnp.int32), *halves)


def unfold_kernel(part_ref, out_ref):
    out_ref[...] = part_ref[...].astype(F32)


def unfold_call(parts, groups, deps):
    count, rows, cols = parts.shape
    far = count // 2
    own = far // groups

    def place(i):
        group, near, piece = i // (2 * own), i // own % 2, i % own
        return (2 * (group * own + piece) + near, 0, 0)

    return call_after(
        unfold_kernel,
        deps,
        grid=(count,),
        in_specs=[pl.BlockSpec((None, rows, cols), place)],
        out_specs=row_spec(rows, cols),
        out_shape=shaped((count * rows, cols), F32),
        compiler_params=params(),
        cost_estimate=cost(0.001),
        name="unfold",
    )(parts)


class Steps:
    def __init__(self):
        self.jobs, self.token, self.ties = [], None, []

    def swap(self, value, axis, size, bit):
        if self.token is not None:
            value = after(value, self.token)
        return swap(value, axis, size, bit)

    def arrive(self, value):
        return value if self.token is None else after(value, self.token)

    def step(self, token=None):
        self.token = token
        self.ties, jobs = [], []
        for job in self.jobs:
            try:
                self.ties = self.ties + next(job)
            except StopIteration:
                continue
            jobs.append(job)
        self.jobs = jobs
        return self.ties if token is None else self.ties + [token]

    def finish(self):
        while self.jobs:
            self.step()


def gather_job(steps, own, shards, axis, size, hold):
    shards[0] = own
    even = {0: own}
    shards[1] = steps.swap(own, axis, size, 1)
    for bit in reversed(bits_of(size)[1:]):
        new = {mask ^ bit: steps.swap(part, axis, size, bit) for mask, part in even.items()}
        for _ in range(hold):
            yield []
        new = {mask: steps.arrive(part) for mask, part in new.items()}
        even.update(new)
        for mask, part in new.items():
            shards[mask] = part
            shards[mask ^ 1] = steps.swap(part, axis, size, 1)
        yield list(new.values())


class Sums:
    def __init__(self, steps, size, lags):
        self.steps, self.size, self.lags = steps, size, lags
        self.parts = {mask: [[] for _ in lags] for mask in range(size)}
        nearest_first = sorted(range(1, size), key=lambda mask: (mask & -mask, mask))
        steps.jobs += [self.send(mask) for mask in nearest_first]

    def full(self, mask, places):
        low = mask & -mask if mask else self.size
        return all(len(self.parts[mask][i]) == low.bit_length() for i in places)

    def add(self, mask, terms):
        for part, term in zip(self.parts[mask], terms):
            part.append(term)

    def send(self, mask):
        every = range(len(self.lags))
        while not self.full(mask, every):
            yield []
        bit = mask & -mask
        values = list(add_groups(self.parts[mask]))
        lags = self.lags if bit > 1 else [0] * len(values)
        flying, ready = {}, values if bit > 1 else []
        for turn in range(max(lags) + 2):
            for i in every:
                if turn == lags[i] + 1:
                    other = self.steps.arrive(flying[i])
                    self.parts[mask ^ bit][i].append(other)
                    ready = ready + [other]
                if turn == lags[i]:
                    flying[i] = self.steps.swap(values[i], "mp", self.size, bit)
            yield ready
            ready = []


def sum_everywhere(shared, by_shard, n_mp, n_dp):
    rows = shared.shape[0]
    for axis, size in (("mp", n_mp), ("dp", n_dp)):
        for bit in bits_of(size):
            sent = by_shard
            if axis == "mp":
                pairs = (size // (2 * bit), 2, bit * by_shard.shape[1], by_shard.shape[2])
                sent = by_shard.reshape(pairs)[:, ::-1]
            sent = jnp.concatenate([shared, sent.reshape(-1, shared.shape[1])], axis=0)
            other = swap(sent, axis, size, bit)
            shared = add_low(shared, other[:rows])
            by_shard = add_low(by_shard, other[rows:].reshape(by_shard.shape))
    return shared, by_shard[0]


def spread_job(steps, sums, places, n_dp, offload, out, name):
    while not sums.full(0, places):
        yield []
    index = lax.axis_index("dp")
    count = n_dp // 2
    keep, send = split_call([sums.parts[0][i] for i in places], index % 2, 2)
    other = steps.swap(send, "dp", n_dp, 1)
    yield [send]
    pieces = split_call([[keep, steps.arrive(other)]], index // 2, count, steps.ties)
    others = [steps.swap(pieces[k], "dp", n_dp, 2 * k) for k in range(1, count)]
    yield [other, *pieces]
    (total,) = add_groups([[pieces[0]] + [steps.arrive(part) for part in others]])
    if offload:
        whole = lax.all_gather(total, "dp", axis=0)
        yield [total]
        yield []
        out[name] = steps.arrive(whole)
        yield [whole]
        return
    others = [steps.swap(total, "dp", n_dp, 2 * k) for k in range(1, count)]
    yield [total]
    half = assemble_call([total] + [steps.arrive(part) for part in others], index // 2, BF)
    other = steps.swap(half, "dp", n_dp, 1)
    yield [half]
    other = steps.arrive(other)
    finish = attention_grads_call if name == "attention" else assemble_call
    out[name] = finish([half, other], index % 2, F32, len(places))
    yield [other]


def place_hot():
    place = jnp.arange(FRAME)
    row, col = place // WIN_W, place % WIN_W
    offset = (row[:, None] - row[None, :] + WIN_H - 1) * N_COL + (
        col[:, None] - col[None, :] + WIN_W - 1
    )
    return (offset.reshape(1, -1) == jnp.arange(N_ROW * N_COL)[:, None]).astype(F32)


def bias_blocks(rel_table):
    heads = rel_table.shape[0]
    cube = rel_table.reshape(heads * N_TIME, N_ROW * N_COL)
    return lax.dot(cube, place_hot(), precision=highest).reshape(heads, N_TIME, FRAME, FRAME)


def collect_blocks(block_grad):
    heads = block_grad.shape[0]
    flat = block_grad.reshape(heads * N_TIME, FRAME * FRAME)
    cube = lax.dot_general(flat, place_hot(), (((1,), (1,)), ((), ())), precision=highest)
    return cube[:, ::-1].reshape(heads, -1)


def block_spec(heads, place):
    return pl.BlockSpec((heads, N_TIME, FRAME, FRAME), lambda i: (place, 0, 0, 0))


def frame_span(frame):
    return slice(frame * FRAME, (frame + 1) * FRAME)


def spread_blocks(blocks_ref, table, fill, transposed):
    for head in range(table.shape[0]):
        for offset in range(N_TIME):
            block = blocks_ref[head, offset]
            if transposed:
                block = block.T
            for query in range(WIN_T):
                key = query - (offset - WIN_T + 1)
                if 0 <= key < WIN_T:
                    row, col = (key, query) if transposed else (query, key)
                    table[head, frame_span(row), frame_span(col)] = block
        table[head, :, WIN_TOK:] = jnp.full((WIN_TOK, PAD_TOK - WIN_TOK), fill, F32)


def norm_kernel(tokens_ref, mod_ref, attn_in_ref):
    normed, _ = normalise(tokens_ref[...].astype(F32))
    attn_in_ref[...] = (normed * (1.0 + mod_ref[0, 1:2]) + mod_ref[0, 0:1]).astype(BF)


def norm_call(tokens, mods, deps=()):
    rows, width = tokens.shape
    return call_after(
        norm_kernel,
        deps,
        grid=(rows // WIN_TOK,),
        in_specs=[row_spec(WIN_TOK, width), mod_spec(1, mods.shape[1], width)],
        out_specs=row_spec(WIN_TOK, width),
        out_shape=shaped((rows, width), BF),
        compiler_params=params(),
        cost_estimate=cost(8),
        name="norm_in",
    )(tokens, mods)


def head_copies(value, heads):
    if heads == 1:
        return [value]
    lane = lax.broadcasted_iota(jnp.int32, value.shape, 1) // HEAD_DIM
    return [jnp.where(lane == head, value, jnp.zeros_like(value)) for head in range(heads)]


def pad_rows(value):
    return jnp.concatenate(
        [value, jnp.zeros((PAD_TOK - WIN_TOK, value.shape[1]), value.dtype)], axis=0
    )


def attend_kernel(x_ref, w_ref, blocks_ref, qkv_ref, mixed_ref, lse_ref, table, columns):
    heads = blocks_ref.shape[0]

    @pl.when(pl.program_id(0) == 0)
    def _():
        spread_blocks(blocks_ref, table, -1e30, False)
        columns[...] = jnp.zeros_like(columns)

    x = x_ref[...]
    queries = dot(x, w_ref[0]).astype(BF)
    keys = dot(x, w_ref[1]).astype(BF)
    values = dot(x, w_ref[2]).astype(BF)
    qkv_ref[0] = queries
    qkv_ref[1] = keys
    qkv_ref[2] = values
    scaled = queries * jnp.asarray(HEAD_DIM**-0.5, BF)
    for window in range(x.shape[0] // WIN_TOK):
        span = window_span(window)
        scores = dot(
            jnp.concatenate(head_copies(scaled[span], heads), axis=0), pad_rows(keys[span]), 1, 1
        )
        probs = []
        for head in range(heads):
            score = scores[window_span(head)] + table[head]
            top = jnp.max(score, axis=1, keepdims=True)
            exponent = jnp.exp(score - top)
            total = jnp.sum(exponent, axis=1, keepdims=True)
            probs.append((exponent * (1.0 / total)).astype(BF))
            columns[window, :WIN_TOK, head : head + 1] = top + jnp.log(total)
        value = jnp.concatenate([pad_rows(part) for part in head_copies(values[span], heads)], axis=0)
        mixed_ref[span, :] = dot(jnp.concatenate(probs, axis=1), value).astype(BF)
        lse_ref[window] = columns[window].T[: lse_ref.shape[1]]


def attend_call(attn_in, weight, blocks, deps=()):
    rows, width = attn_in.shape
    cols = weight.shape[2]
    blocks, place, heads = blocks
    windows = rows // WIN_TOK
    per = per_step(rows)
    block = per * WIN_TOK
    stat_rows = -(-heads // 8) * 8
    return call_after(
        attend_kernel,
        deps,
        grid=(windows // per,),
        in_specs=[row_spec(block, width), whole_spec(weight.shape), block_spec(heads, place)],
        out_specs=[
            part_spec(block, cols),
            row_spec(block, cols),
            mod_spec(per, stat_rows, PAD_TOK),
        ],
        out_shape=[
            shaped((3, rows, cols), BF),
            shaped((rows, cols), BF),
            shaped((windows, stat_rows, PAD_TOK), F32),
        ],
        scratch_shapes=[
            pltpu.VMEM((heads, WIN_TOK, PAD_TOK), F32),
            pltpu.VMEM((per, PAD_TOK, 128), F32),
        ],
        compiler_params=params(),
        cost_estimate=cost(19),
        name="attend",
    )(attn_in, weight, blocks)


def attend_back_kernel(*refs, held):
    grad_ref, out_w_ref, qkv_ref, mixed_ref, lse_ref, blocks_ref, x_ref = refs[:7]
    dqkv_ref, dblocks_ref, dw_ref, table, total, x_all, grad_all, d_all = refs[7 + held :]
    heads = blocks_ref.shape[0]
    cols = out_w_ref.shape[0]
    step = pl.program_id(0)

    @pl.when(step == 0)
    def _():
        spread_blocks(blocks_ref, table, 0.0, True)
        total[...] = jnp.zeros_like(total)

    grads_mixed = dot(grad_ref[...], out_w_ref[...], 1, 1).astype(BF)
    scale = jnp.asarray(HEAD_DIM**-0.5, BF)
    head_rows = (lse_ref.shape[1], cols)
    head_hot = (
        lax.broadcasted_iota(jnp.int32, head_rows, 1) // HEAD_DIM
        == lax.broadcasted_iota(jnp.int32, head_rows, 0)
    ).astype(BF)
    block = grad_ref.shape[0]
    rows = pl.ds(pl.multiple_of(step * block, block), block)
    x_all[rows, :] = x_ref[...]
    grad_all[rows, :] = grad_ref[...]
    d_all[3, rows, :] = mixed_ref[...]
    for window in range(block // WIN_TOK):
        place = window_span(window)
        grad_mixed = grads_mixed[place]
        query = qkv_ref[0, place, :]
        key = qkv_ref[1, place, :]
        value = qkv_ref[2, place, :]
        product = grad_mixed.astype(F32) * mixed_ref[place, :].astype(F32)
        upper = product.astype(BF)
        lower = (product - upper.astype(F32)).astype(BF)
        inner = dot(head_hot, pad_rows(upper), 1, 1) + dot(head_hot, pad_rows(lower), 1, 1)
        keys = jnp.concatenate(head_copies(key * scale, heads), axis=0)
        values = jnp.concatenate(head_copies(value, heads), axis=0)
        query_pad = pad_rows(query)
        grad_pad = pad_rows(grad_mixed)
        scores = dot(keys, query_pad, 1, 1)
        grad_probs = dot(values, grad_pad, 1, 1)
        probs = []
        grad_scores = []
        for head in range(heads):
            span = window_span(head)
            prob = jnp.exp(scores[span] + table[head] - lse_ref[window, head : head + 1, :])
            grad_score = (prob * (grad_probs[span] - inner[head : head + 1, :])).astype(BF)
            probs.append(prob.astype(BF))
            grad_scores.append(grad_score)
            total[head] += grad_score.astype(F32)
        wide = jnp.concatenate(grad_scores, axis=1)
        grad_value = dot(
            jnp.concatenate(probs, axis=1), jnp.concatenate(head_copies(grad_pad, heads), axis=0)
        )
        grad_key = dot(wide, jnp.concatenate(head_copies(query_pad * scale, heads), axis=0))
        grad_query = dot(jnp.concatenate(grad_scores, axis=0), keys, 0, 0)[:WIN_TOK]
        own = pl.ds(pl.multiple_of(step * block + window * WIN_TOK, WIN_TOK), WIN_TOK)
        for part, grad in enumerate((grad_query, grad_key, grad_value)):
            grad = grad.astype(BF)
            dqkv_ref[part, place, :] = grad
            d_all[part, own, :] = grad

    @pl.when(step == pl.num_programs(0) - 1)
    def _():
        for part in range(4):
            left = grad_all if part == 3 else x_all
            dw_ref[part] = dot(left[...], d_all[part], 0, 0).astype(BF)
        for head in range(heads):
            for offset in range(N_TIME):
                block = None
                for query in range(WIN_T):
                    key = query - (offset - WIN_T + 1)
                    if 0 <= key < WIN_T:
                        part = total[head, frame_span(key), frame_span(query)]
                        block = part if block is None else block + part
                dblocks_ref[head, offset] = block


def attend_back_call(grad_attn, out_weight, qkv, mixed, lse, blocks, attn_in, block_grads, deps=()):
    rows, width = grad_attn.shape
    cols = out_weight.shape[0]
    blocks, place, heads = blocks
    per = per_step(rows)
    block = per * WIN_TOK
    held = () if block_grads is None else (block_grads,)
    return call_after(
        functools.partial(attend_back_kernel, held=len(held)),
        deps,
        grid=(rows // block,),
        in_specs=[
            row_spec(block, width),
            whole_spec(out_weight.shape),
            part_spec(block, cols),
            row_spec(block, cols),
            mod_spec(per, lse.shape[1], PAD_TOK),
            block_spec(heads, place),
            row_spec(block, width),
        ]
        + [pl.BlockSpec(memory_space=pl.ANY)] * len(held),
        out_specs=[
            part_spec(block, cols),
            block_spec(heads, place),
            whole_spec((4, width, cols)),
        ],
        out_shape=[
            shaped((3, rows, cols), BF),
            shaped(blocks.shape, F32),
            shaped((4, width, cols), BF),
        ],
        scratch_shapes=[pltpu.VMEM((heads, WIN_TOK, PAD_TOK), F32)] * 2
        + [pltpu.VMEM((rows, width), BF)] * 2
        + [pltpu.VMEM((4, rows, cols), BF)],
        input_output_aliases={7: 1} if held else {},
        compiler_params=params(),
        cost_estimate=cost(30),
        name="attend_back",
    )(grad_attn, out_weight, qkv, mixed, lse, blocks, attn_in, *held)


def middle_kernel(*refs, count):
    mixed_refs = refs[:count]
    weight_refs = refs[count : 2 * count]
    tokens_ref, cot_ref, mod_ref, attn_out_ref, mlp_in_ref, grad_mlp_ref = refs[2 * count :]
    attn_out = dot(mixed_refs[0][...], weight_refs[0][...])
    for mixed_ref, weight_ref in zip(mixed_refs[1:], weight_refs[1:]):
        attn_out = attn_out + dot(mixed_ref[...], weight_ref[...])
    attn_out_ref[...] = attn_out.astype(BF)
    for window in range(attn_out.shape[0] // WIN_TOK):
        span = window_span(window)
        mod = mod_ref[window]
        resid = tokens_ref[span, :].astype(F32) + mod[2:3] * attn_out[span]
        normed, _ = normalise(resid)
        mlp_in_ref[span, :] = (normed * (1.0 + mod[4:5]) + mod[3:4]).astype(BF)
        grad_mlp_ref[span, :] = (mod[5:6] * cot_ref[span, :].astype(F32)).astype(BF)


def middle_call(mixed, weights, tokens, cotangent, mods, deps=()):
    rows, width = tokens.shape
    count = len(mixed)
    per = per_step(rows)
    block = per * WIN_TOK
    row = row_spec(block, width)
    return call_after(
        functools.partial(middle_kernel, count=count),
        deps,
        grid=(rows // block,),
        in_specs=[row_spec(block, part.shape[1]) for part in mixed]
        + [whole_spec(part.shape) for part in weights]
        + [row, row, mod_spec(per, mods.shape[1], width)],
        out_specs=[row, row, row],
        out_shape=[
            shaped((rows, width), BF),
            shaped((rows, width), BF),
            shaped((rows, width), BF),
        ],
        compiler_params=params(),
        cost_estimate=cost(16),
        name="middle",
    )(*mixed, *weights, tokens, cotangent, mods)


def mlp_kernel(
    x_ref, g_ref, up_ref, down_ref, act_ref, ghid_ref, *rest, chunk
):
    down_total, up_total = rest[4:]
    step = pl.program_id(0)
    x = x_ref[...]
    g = g_ref[...]
    for start in range(0, up_ref.shape[1], chunk):
        span = slice(start, start + chunk)
        hidden = dot(x, up_ref[:, span])
        grad_act = dot(g, down_ref[span, :], 1, 1)
        cubic = GELU_B * (hidden * hidden)
        gate = 0.5 + 0.5 * jnp.tanh(hidden * (GELU_A + cubic))
        act_ref[:, span] = (hidden * gate).astype(BF)
        slope = gate + gate * ((1.0 - gate) * (hidden * (2.0 * GELU_A + 6.0 * cubic)))
        ghid_ref[:, span] = (grad_act * slope).astype(BF)

    @pl.when(step == 0)
    def _():
        down_total[...] = dot(act_ref[...], g, 0, 0)
        up_total[...] = dot(x, ghid_ref[...], 0, 0)

    @pl.when(step > 0)
    def _():
        down_total[...] += dot(act_ref[...], g, 0, 0)
        up_total[...] += dot(x, ghid_ref[...], 0, 0)

    @pl.when(step == pl.num_programs(0) - 1)
    def _():
        for place, total in enumerate((down_total, up_total)):
            size = total.shape[0] // 2
            rest[2 * place][...] = total[:size].astype(BF)
            rest[2 * place + 1][...] = total[size:].astype(BF)


MLP_BLOCK = 1280
MLP_CHUNK = 512


def mlp_call(x, g, up, down, deps=()):
    rows, width = x.shape
    hidden = up.shape[1]
    block = MLP_BLOCK if rows % MLP_BLOCK == 0 else WIN_TOK
    row = row_spec(block, width)
    wide = row_spec(block, hidden)
    halves = [(hidden // 2, width)] * 2 + [(width // 2, hidden)] * 2
    return call_after(
        functools.partial(mlp_kernel, chunk=min(MLP_CHUNK, hidden)),
        deps,
        grid=(rows // block,),
        in_specs=[row, row, whole_spec(up.shape), whole_spec(down.shape)],
        out_specs=[wide, wide] + [whole_spec(shape) for shape in halves],
        out_shape=[
            shaped((rows, hidden), BF),
            shaped((rows, hidden), BF),
        ]
        + [shaped(shape, BF) for shape in halves],
        scratch_shapes=[pltpu.VMEM(down.shape, F32), pltpu.VMEM(up.shape, F32)],
        compiler_params=params(),
        cost_estimate=cost(30),
        name="mlp",
    )(x, g, up, down)


def mlp_out_kernel(*refs, count):
    act_refs, ghid_refs, down_refs, up_refs = [
        refs[place * count : (place + 1) * count] for place in range(4)
    ]
    tokens_ref, cot_ref, attn_out_ref, mod_ref, out_ref, gres_ref, gattn_ref, sums_ref = refs[
        4 * count :
    ]
    join = lambda parts, axis: jnp.concatenate([part[...] for part in parts], axis=axis)
    mlp_outs = dot(join(act_refs, 1), join(down_refs, 0))
    gins = dot(join(ghid_refs, 1), join(up_refs, 1), 1, 1)
    for window in range(gins.shape[0] // WIN_TOK):
        span = window_span(window)
        mod = mod_ref[window]
        mlp_out, gin = mlp_outs[span], gins[span]
        cot = cot_ref[span, :].astype(F32)
        attn_out = attn_out_ref[span, :].astype(F32)
        resid = tokens_ref[span, :].astype(F32) + mod[2:3] * attn_out
        out_ref[span, :] = (resid + mod[5:6] * mlp_out).astype(BF)
        normed, inverse = normalise(resid)
        gres = cot + normalise_back(normed, inverse, gin * (1.0 + mod[4:5]))
        gres_ref[span, :] = gres.astype(BF)
        gattn_ref[span, :] = (mod[2:3] * gres).astype(BF)
        sums_ref[window, 0:1] = jnp.sum(gres * attn_out, axis=0, keepdims=True)
        sums_ref[window, 1:2] = jnp.sum(gin, axis=0, keepdims=True)
        sums_ref[window, 2:3] = jnp.sum(gin * normed, axis=0, keepdims=True)
        sums_ref[window, 3:4] = jnp.sum(cot * mlp_out, axis=0, keepdims=True)


def kept_spec(shape):
    return pl.BlockSpec(shape, lambda i: (0,) * len(shape), pipeline_mode=pl.Buffered(1))


def mlp_out_call(act, ghid, down, up, tokens, cotangent, attn_out, mods, deps=()):
    rows, width = tokens.shape
    per = 1
    block = per * WIN_TOK
    row = row_spec(block, width)
    windows = rows // WIN_TOK
    return call_after(
        functools.partial(mlp_out_kernel, count=len(act)),
        deps,
        grid=(windows // per,),
        in_specs=[row_spec(block, part.shape[1]) for part in act + ghid]
        + [kept_spec(part.shape) for part in down + up]
        + [row, row, row, mod_spec(per, mods.shape[1], width)],
        out_specs=[row, row, row, mod_spec(per, 4, width)],
        out_shape=[
            shaped((rows, width), BF),
            shaped((rows, width), BF),
            shaped((rows, width), BF),
            shaped((windows, 4, width), F32),
        ],
        compiler_params=params(),
        cost_estimate=cost(55),
        name="mlp_out",
    )(*act, *ghid, *down, *up, tokens, cotangent, attn_out, mods)


def last_kernel(*refs, count):
    dqkv_refs = refs[:count]
    weight_refs = refs[count : 2 * count]
    tokens_ref, gres_ref, mod_ref, out_ref, sums_ref = refs[2 * count :]
    join = lambda refs: jnp.concatenate([ref[part] for ref in refs for part in range(3)], axis=1)
    gin = dot(join(dqkv_refs), join(weight_refs), 1, 1)
    for window in range(gin.shape[0] // WIN_TOK):
        span = window_span(window)
        normed, inverse = normalise(tokens_ref[span, :].astype(F32))
        grad = gin[span]
        out_ref[span, :] = (
            gres_ref[span, :].astype(F32) + normalise_back(normed, inverse, grad * (1.0 + mod_ref[window, 1:2]))
        ).astype(BF)
        sums_ref[window, 0:1] = jnp.sum(grad, axis=0, keepdims=True)
        sums_ref[window, 1:2] = jnp.sum(grad * normed, axis=0, keepdims=True)


def last_call(dqkv, weights, tokens, gres, mods, deps=()):
    rows, width = tokens.shape
    count = len(dqkv)
    per = 1
    block = per * WIN_TOK
    row = row_spec(block, width)
    windows = rows // WIN_TOK
    return call_after(
        functools.partial(last_kernel, count=count),
        deps,
        grid=(windows // per,),
        in_specs=[part_spec(block, part.shape[2]) for part in dqkv]
        + [kept_spec(part.shape) for part in weights]
        + [row, row, mod_spec(per, mods.shape[1], width)],
        out_specs=[row, mod_spec(per, 2, width)],
        out_shape=[shaped((rows, width), BF), shaped((windows, 2, width), F32)],
        compiler_params=params(),
        cost_estimate=cost(28),
        name="last",
    )(*dqkv, *weights, tokens, gres, mods)


def body(
    n_dp,
    n_mp,
    tokens,
    cotangent,
    qkv_weight,
    out_weight,
    up_weight,
    down_weight,
    rel_bias,
    ada_weight,
    ada_bias,
    class_embed,
    window_clip,
    timesteps,
    class_ids,
):
    mp_index = lax.axis_index("mp")
    micro, local_rows, width = tokens.shape
    local_cols = class_embed.shape[1]
    clips = timesteps.shape[1]
    own_windows = local_rows // WIN_TOK
    rows = micro * local_rows
    tokens_flat = tokens.reshape(rows, width)
    cot_flat = cotangent.reshape(rows, width)
    masks = range(n_mp)

    columns = mp_index * local_cols + jnp.arange(local_cols)
    half_width = width // 2
    freq_index = (columns % half_width).astype(F32)
    frequency = jnp.exp(-math.log(10000.0) * freq_index / half_width)
    angle = timesteps.astype(F32)[..., None] * frequency
    step_embed = jnp.where(columns < half_width, jnp.sin(angle), jnp.cos(angle))
    class_hot = (class_ids[..., None] == jnp.arange(class_embed.shape[0])).astype(F32)
    condition = step_embed + jnp.einsum("mck,kd->mcd", class_hot, class_embed, precision=highest)
    lowered = jax.nn.silu(condition).astype(BF)
    mod_terms = jnp.einsum("mcd,de->mce", lowered, ada_weight, preferred_element_type=F32)
    near_terms = add_low(mod_terms, swap(mod_terms, "mp", n_mp, 1))
    modulation = near_terms
    for bit in bits_of(n_mp)[1:]:
        modulation = add_low(modulation, swap(modulation, "mp", n_mp, bit))
    modulation = modulation + ada_bias
    own_clip = lax.dynamic_slice_in_dim(window_clip, mp_index * own_windows, own_windows, 1)
    clip_hot = (own_clip[..., None] == jnp.arange(clips)).astype(F32)
    mods = jnp.einsum("mwc,mce->mwe", clip_hot, modulation, precision=highest)
    mods = mods.reshape(micro * own_windows, 6, width)

    steps = Steps()
    rel_tables = gather_shards(rel_bias, "mp", n_mp)
    blocks = bias_blocks(jnp.concatenate([rel_tables[m] for m in masks], axis=0))
    heads = rel_bias.shape[0]

    def gather(own, hold):
        shards = {}
        steps.jobs.append(gather_job(steps, own, shards, "mp", n_mp, hold))
        return shards

    def need(shards, mask, ties, token):
        while mask not in shards:
            ties = ties + steps.step(token)
        return ties

    qkv_w = gather(qkv_weight, 3)
    steps.step(modulation)
    attn_in = norm_call(tokens_flat, mods)
    out_w = gather(out_weight, 3)
    ties = steps.step(attn_in)
    qkv, mixed, lse = {}, {}, {}
    for m in masks:
        ties = need(qkv_w, m, ties, attn_in)
        qkv[m], mixed[m], lse[m] = attend_call(attn_in, qkv_w[m], (blocks, m, heads), ties)
        if m == 0:
            down_w = gather(down_weight, 4)
        elif m == 2 or m == n_mp - 1 == 1:
            up_w = gather(up_weight, 3)
        ties = steps.step(mixed[m])
    for m in masks:
        ties = need(out_w, m, ties, mixed[0])
    attn_out, mlp_in, grad_mlp = middle_call(
        [mixed[m] for m in masks], [out_w[m] for m in masks], tokens_flat, cot_flat, mods, ties
    )
    ties = steps.step(mlp_in)
    wide_sums = Sums(steps, n_mp, [0, 1, 1, 2])
    grads = {}
    steps.jobs.append(spread_job(steps, wide_sums, [0, 1], n_dp, True, grads, "down"))
    steps.jobs.append(spread_job(steps, wide_sums, [2, 3], n_dp, False, grads, "up"))
    act, grad_hidden = {}, {}
    for m in [m for m in masks if m % 2] + [m for m in reversed(masks) if m % 2 == 0]:
        ties = need(down_w, m, need(up_w, m, ties, mlp_in), mlp_in)
        act[m], grad_hidden[m], *wide_terms = mlp_call(mlp_in, grad_mlp, up_w[m], down_w[m], ties)
        wide_sums.add(m, wide_terms)
        ties = steps.step(wide_terms[0])
    block_out, grad_resid, grad_attn, late_sums = mlp_out_call(
        *[[part[m] for m in masks] for part in (act, grad_hidden, down_w, up_w)],
        tokens_flat,
        cot_flat,
        attn_out,
        mods,
        ties,
    )

    def clip_sums(window_sums):
        grouped = window_sums.reshape(micro, own_windows, -1)
        return jnp.einsum("mwc,mwe->mce", clip_hot, grouped, precision=highest).astype(BF)

    attn_sums = Sums(steps, n_mp, [0])
    steps.jobs.append(spread_job(steps, attn_sums, [0], n_dp, False, grads, "attention"))
    dqkv, block_grads = {}, None
    ties = steps.step(grad_attn)
    for m in reversed(masks):
        dqkv[m], block_grads, qkv_term = attend_back_call(
            grad_attn, out_w[m], qkv[m], mixed[m], lse[m], (blocks, m, heads), attn_in, block_grads, ties
        )
        attn_sums.add(m, [qkv_term.reshape(-1, qkv_term.shape[2])])
        ties = steps.step(qkv_term)
    token_grad, early_sums = last_call(
        [dqkv[m] for m in masks], [qkv_w[m] for m in masks], tokens_flat, grad_resid, mods, ties
    )
    ties = steps.step(token_grad)
    window_sums = after(jnp.concatenate([early_sums, late_sums], axis=1), *ties)
    rel_sums = after(block_grads, *ties)
    rel_sums = collect_blocks(rel_sums).astype(BF).reshape(n_mp, -1)
    table_size = rel_sums.shape[1]
    rel_sums = jnp.pad(rel_sums, ((0, 0), (0, -table_size % width))).reshape(n_mp, -1, width)
    clip_terms = clip_sums(window_sums).reshape(-1, width)
    summed = steps.step()
    ties = steps.step()
    mod_total, rel_total = sum_everywhere(
        after(clip_terms, *ties), after(rel_sums, *ties), n_mp, n_dp
    )
    rel_grad = rel_total.reshape(-1)[:table_size].reshape(rel_bias.shape).astype(F32)
    steps.finish()

    down_grad = unfold_call(grads["down"], 2, summed)
    up_grad = grads["up"]
    qkv_grad, out_grad = grads["attention"]
    qkv_grad = qkv_grad.reshape(qkv_weight.shape)
    mod_total = mod_total.astype(F32).reshape(micro, clips, 6 * width)
    ada_bias_grad = jnp.sum(mod_total, axis=(0, 1))
    ada_weight_grad = jnp.einsum(
        "mcd,mce->de", lowered.astype(F32), mod_total, precision=highest
    )
    grad_lowered = jnp.einsum(
        "mce,de->mcd", mod_total, ada_weight.astype(F32), precision=highest
    )
    grad_condition = jax.vjp(jax.nn.silu, condition)[1](grad_lowered)[0]
    class_grad = jnp.einsum("mck,mcd->kd", class_hot, grad_condition, precision=highest)
    return (
        block_out.reshape(tokens.shape),
        token_grad.reshape(tokens.shape),
        qkv_grad,
        out_grad,
        up_grad,
        down_grad,
        rel_grad,
        ada_weight_grad,
        ada_bias_grad,
        class_grad,
    )


def solution(mesh):
    rows = P(None, ("dp", "mp"), None)
    in_specs = (
        rows,
        rows,
        P(None, None, "mp"),
        P("mp", None),
        P(None, "mp"),
        P("mp", None),
        P("mp", None),
        P("mp", None),
        P(),
        P(None, "mp"),
        P(None, "dp"),
        P(),
        P(),
    )
    out_specs = (
        rows,
        rows,
        P(None, None, "mp"),
        P("mp", None),
        P(None, "mp"),
        P("mp", None),
        P("mp", None),
        P("mp", None),
        P(),
        P(None, "mp"),
    )
    step = functools.partial(body, mesh.shape["dp"], mesh.shape["mp"])
    return jax.shard_map(step, mesh=mesh, in_specs=in_specs, out_specs=out_specs, check_vma=False)
```

```python
import functools
import math

import jax
import jax.numpy as jnp
from jax import lax
from jax.experimental import pallas as pl
from jax.experimental.pallas import tpu as pltpu
from jax.sharding import PartitionSpec as P

WIN_T = 5
WIN_H = 8
WIN_W = 8
WIN_TOK = WIN_T * WIN_H * WIN_W
FRAME = WIN_H * WIN_W
PAD_TOK = 384
HEAD_DIM = 64
N_TIME, N_ROW, N_COL = 2 * WIN_T - 1, 2 * WIN_H - 1, 2 * WIN_W - 1

BF = jnp.bfloat16
F32 = jnp.float32
epsilon = 1e-06
highest = lax.Precision.HIGHEST
GELU_A = 0.7978845608028654
GELU_B = GELU_A * 0.044715
VMEM_LIMIT = 63 * 1024 * 1024


def dot(left, right, left_dim=1, right_dim=0):
    return lax.dot_general(
        left, right, (((left_dim,), (right_dim,)), ((), ())), preferred_element_type=F32
    )


def params():
    return pltpu.CompilerParams(vmem_limit_bytes=VMEM_LIMIT)


def shaped(shape, dtype):
    return jax.ShapeDtypeStruct(shape, dtype)


def row_spec(rows, cols):
    return pl.BlockSpec((rows, cols), lambda i: (i, 0))


def part_spec(rows, cols):
    return pl.BlockSpec((3, rows, cols), lambda i: (0, i, 0))


def per_step(rows):
    return 2 if rows % (2 * WIN_TOK) == 0 else 1


def window_span(window):
    return slice(window * WIN_TOK, (window + 1) * WIN_TOK)


def whole_spec(shape):
    return pl.BlockSpec(shape, lambda i: (0,) * len(shape))


def mod_spec(per, count, cols):
    return pl.BlockSpec((per, count, cols), lambda i: (i, 0, 0))


def cost(micros):
    return pl.CostEstimate(
        flops=int(micros * 1e9), bytes_accessed=int(micros * 3.5e6), transcendentals=0
    )


def call_after(kernel, deps, *, in_specs, **rest):
    deps = tuple(deps)
    count = len(in_specs)

    def run(*refs):
        kernel(*refs[:count], *refs[count + len(deps) :])

    call = pl.pallas_call(
        run, in_specs=list(in_specs) + [pl.BlockSpec(memory_space=pl.ANY)] * len(deps), **rest
    )
    return lambda *args: call(*args, *deps)


def after(value, *deps):
    return lax.optimization_barrier((value, *deps))[0]


def normalise(values):
    centred = values - jnp.mean(values, axis=-1, keepdims=True)
    inverse = lax.rsqrt(jnp.mean(centred * centred, axis=-1, keepdims=True) + epsilon)
    return centred * inverse, inverse


def normalise_back(normed, inverse, grad_in):
    return inverse * (
        grad_in
        - jnp.mean(grad_in, axis=-1, keepdims=True)
        - normed * jnp.mean(grad_in * normed, axis=-1, keepdims=True)
    )


def swap(value, axis, size, bit):
    return lax.ppermute(value, axis, [(i, i ^ bit) for i in range(size)])


def bits_of(size):
    return [1 << b for b in range(size.bit_length() - 1)]


def add_low(left, right):
    return (left.astype(F32) + right.astype(F32)).astype(left.dtype)


def gather_shards(own, axis, size):
    shards = {0: own}
    for bit in reversed(bits_of(size)):
        for mask in list(shards):
            shards[mask ^ bit] = swap(shards[mask], axis, size, bit)
    return shards


def reduce_all(value, axis, size):
    for bit in bits_of(size):
        value = add_low(value, swap(value, axis, size, bit))
    return value


def reduce_shards(terms, axis, size):
    terms = dict(terms)
    for bit in bits_of(size):
        for mask in [m for m in terms if m & bit]:
            terms[mask ^ bit] = add_low(terms[mask ^ bit], swap(terms.pop(mask), axis, size, bit))
    return terms[0]


def sum_kernel(*refs, groups):
    outs = refs[sum(groups) :]
    for out, group in zip(outs, groups):
        total = refs[0][...].astype(F32)
        for ref in refs[1:group]:
            total = total + ref[...].astype(F32)
        out[...] = total.astype(BF)
        refs = refs[group:]


def add_groups(groups):
    if all(len(group) == 1 for group in groups):
        return [group[0] for group in groups]
    shapes = [group[0].shape for group in groups]
    turns = 4 if all(shape[0] % 64 == 0 and shape[0] >= 512 for shape in shapes) else 1
    spec = lambda shape: row_spec(shape[0] // turns, shape[1])
    return pl.pallas_call(
        functools.partial(sum_kernel, groups=[len(group) for group in groups]),
        grid=(turns,),
        in_specs=[spec(array.shape) for group in groups for array in group],
        out_specs=[spec(shape) for shape in shapes],
        out_shape=[shaped(shape, BF) for shape in shapes],
        compiler_params=params(),
        cost_estimate=cost(0.001),
        name="add",
    )(*[array for group in groups for array in group])


def split_kernel(index_ref, *refs, count, groups, deps):
    outs = refs[sum(groups) + deps :]
    totals = []
    for group in groups:
        total = refs[0][...].astype(F32)
        for ref in refs[1:group]:
            total = total + ref[...].astype(F32)
        totals.append(total.astype(BF))
        refs = refs[group:]
    size = totals[0].shape[0]
    for k in range(count):

        @pl.when(pl.program_id(0) == k)
        def _():
            for place, total in enumerate(totals):
                outs[k][place * size : (place + 1) * size, :] = total


def split_call(groups, index, count, deps=()):
    rows, cols = groups[0][0].shape
    part = (rows // count, cols)
    piece = (len(groups) * part[0], cols)
    parts = [array for group in groups for array in group]
    spec = pltpu.PrefetchScalarGridSpec(
        num_scalar_prefetch=1,
        grid=(count,),
        in_specs=[pl.BlockSpec(part, lambda k, f: (f[0] ^ k, 0))] * len(parts)
        + [pl.BlockSpec(memory_space=pl.ANY)] * len(deps),
        out_specs=[pl.BlockSpec(piece, lambda k, f: (0, 0))] * count,
    )
    return pl.pallas_call(
        functools.partial(
            split_kernel, count=count, groups=[len(group) for group in groups], deps=len(deps)
        ),
        grid_spec=spec,
        out_shape=[shaped(piece, BF)] * count,
        compiler_params=params(),
        cost_estimate=cost(0.001),
        name="split",
    )(jnp.reshape(index, (1,)).astype(jnp.int32), *parts, *deps)


def assemble_kernel(index_ref, *refs, count, groups):
    step = pl.program_id(0)
    size = refs[-1].shape[0]
    rows = pl.ds(pl.multiple_of(step % groups * size, size), size)
    for k, ref in enumerate(refs[:count]):

        @pl.when(step // groups == k)
        def _():
            refs[-1][...] = ref[rows, :].astype(refs[-1].dtype)


def assemble_call(pieces, index, dtype, groups=1, deps=()):
    count = len(pieces)
    rows, cols = pieces[0].shape
    spec = pltpu.PrefetchScalarGridSpec(
        num_scalar_prefetch=1,
        grid=(count * groups,),
        in_specs=[pl.BlockSpec((rows, cols), lambda i, f: (0, 0))] * count
        + [pl.BlockSpec(memory_space=pl.ANY)] * len(deps),
        out_specs=pl.BlockSpec(
            (rows // groups, cols), lambda i, f: (i % groups * count + (f[0] ^ (i // groups)), 0)
        ),
    )
    return pl.pallas_call(
        functools.partial(assemble_kernel, count=count, groups=groups),
        grid_spec=spec,
        out_shape=shaped((rows * count, cols), dtype),
        compiler_params=params(),
        cost_estimate=cost(0.001),
        name="assemble",
    )(jnp.reshape(index, (1,)).astype(jnp.int32), *pieces, *deps)


def attention_grads_kernel(index_ref, own_ref, other_ref, qkv_ref, out_ref):
    step = pl.program_id(0)
    place = 2 * (index_ref[0] ^ (step // 2)) + step % 2
    size = qkv_ref.shape[0]
    rows = pl.ds(pl.multiple_of(step % 2 * size, size), size)
    for k, ref in enumerate((own_ref, other_ref)):

        @pl.when((step // 2 == k) & (place < 3))
        def _():
            qkv_ref[...] = ref[rows, :].astype(F32)

        @pl.when((step // 2 == k) & (place == 3))
        def _():
            out_ref[...] = ref[rows, :].astype(F32).T


def attention_grads_call(halves, index, dtype, groups):
    rows, cols = halves[0].shape
    size = rows // 2
    place = lambda i, f: (jnp.minimum(2 * (f[0] ^ (i // 2)) + i % 2, 2), 0)
    spec = pltpu.PrefetchScalarGridSpec(
        num_scalar_prefetch=1,
        grid=(4,),
        in_specs=[pl.BlockSpec((rows, cols), lambda i, f: (0, 0))] * 2,
        out_specs=[
            pl.BlockSpec((size, cols), place),
            pl.BlockSpec((cols, size), lambda i, f: (0, 0)),
        ],
    )
    return pl.pallas_call(
        attention_grads_kernel,
        grid_spec=spec,
        out_shape=[shaped((3 * size, cols), dtype), shaped((cols, size), dtype)],
        compiler_params=params(),
        cost_estimate=cost(0.001),
        name="attention_grads",
    )(jnp.reshape(index, (1,)).astype(jnp.int32), *halves)


def unfold_kernel(part_ref, out_ref):
    out_ref[...] = part_ref[...].astype(F32)


def unfold_call(parts, groups, deps):
    count, rows, cols = parts.shape
    far = count // 2
    own = far // groups

    def place(i):
        group, near, piece = i // (2 * own), i // own % 2, i % own
        return (2 * (group * own + piece) + near, 0, 0)

    return call_after(
        unfold_kernel,
        deps,
        grid=(count,),
        in_specs=[pl.BlockSpec((None, rows, cols), place)],
        out_specs=row_spec(rows, cols),
        out_shape=shaped((count * rows, cols), F32),
        compiler_params=params(),
        cost_estimate=cost(0.001),
        name="unfold",
    )(parts)


class Steps:
    def __init__(self):
        self.jobs, self.token, self.ties, self.first = [], None, [], []

    def swap(self, value, axis, size, bit):
        if self.token is not None:
            value = after(value, self.token)
        return swap(value, axis, size, bit)

    def arrive(self, value):
        return value if self.token is None else after(value, self.token)

    def step(self, token=None):
        self.token = token
        self.ties, jobs = [], []
        for job in self.jobs:
            try:
                self.ties = self.ties + next(job)
            except StopIteration:
                continue
            jobs.append(job)
        self.jobs = jobs
        return self.ties if token is None else self.ties + [token]

    def finish(self):
        while self.jobs:
            self.step()


def gather_job(steps, own, shards, axis, size, hold):
    shards[0] = own
    even = {0: own}
    shards[1] = steps.swap(own, axis, size, 1)
    for bit in reversed(bits_of(size)[1:]):
        new = {mask ^ bit: steps.swap(part, axis, size, bit) for mask, part in even.items()}
        for _ in range(hold):
            yield []
        new = {mask: steps.arrive(part) for mask, part in new.items()}
        even.update(new)
        for mask, part in new.items():
            shards[mask] = part
            shards[mask ^ 1] = steps.swap(part, axis, size, 1)
        yield list(new.values())


class Sums:
    def __init__(self, steps, size, lags):
        self.steps, self.size, self.lags = steps, size, lags
        self.parts = {mask: [[] for _ in lags] for mask in range(size)}
        nearest_first = sorted(range(1, size), key=lambda mask: (mask & -mask, mask))
        steps.jobs += [self.send(mask) for mask in nearest_first]

    def full(self, mask, places):
        low = mask & -mask if mask else self.size
        return all(len(self.parts[mask][i]) == low.bit_length() for i in places)

    def add(self, mask, terms):
        for part, term in zip(self.parts[mask], terms):
            part.append(term)

    def send(self, mask):
        every = range(len(self.lags))
        while not self.full(mask, every):
            yield []
        bit = mask & -mask
        values = list(add_groups(self.parts[mask]))
        lags = self.lags if bit > 1 else [0] * len(values)
        flying, ready = {}, values if bit > 1 else []
        for turn in range(max(lags) + 2):
            for i in every:
                if turn == lags[i] + 1:
                    other = self.steps.arrive(flying[i])
                    self.parts[mask ^ bit][i].append(other)
                    ready = ready + [other]
                if turn == lags[i]:
                    flying[i] = self.steps.swap(values[i], "mp", self.size, bit)
            yield ready
            ready = []


def sum_everywhere(shared, by_shard, n_mp, n_dp):
    rows = shared.shape[0]
    for axis, size in (("mp", n_mp), ("dp", n_dp)):
        for bit in bits_of(size):
            sent = by_shard
            if axis == "mp":
                pairs = (size // (2 * bit), 2, bit * by_shard.shape[1], by_shard.shape[2])
                sent = by_shard.reshape(pairs)[:, ::-1]
            sent = jnp.concatenate([shared, sent.reshape(-1, shared.shape[1])], axis=0)
            other = swap(sent, axis, size, bit)
            shared = add_low(shared, other[:rows])
            by_shard = add_low(by_shard, other[rows:].reshape(by_shard.shape))
    return shared, by_shard[0]


def spread_job(steps, sums, places, n_dp, offload, late, out, name):
    while not sums.full(0, places):
        yield []
    index = lax.axis_index("dp")
    count = n_dp // 2
    keep, send = split_call([sums.parts[0][i] for i in places], index % 2, 2)
    other = steps.swap(send, "dp", n_dp, 1)
    yield [send]
    pieces = split_call([[keep, steps.arrive(other)]], index // 2, count, steps.ties)
    others = [steps.swap(pieces[k], "dp", n_dp, 2 * k) for k in range(1, count)]
    yield [other, *pieces]
    (total,) = add_groups([[pieces[0]] + [steps.arrive(part) for part in others]])
    if offload:
        whole = lax.all_gather(total, "dp", axis=0)
        yield [total]
        yield []
        out[name] = steps.arrive(whole)
        yield [whole]
        return
    others = [steps.swap(total, "dp", n_dp, 2 * k) for k in range(1, count)]
    yield [total]
    others = [steps.arrive(part) for part in others]
    half = assemble_call([total] + others, index // 2, BF, deps=steps.first)
    if late:
        yield [half]
    other = steps.swap(half, "dp", n_dp, 1)
    yield [] if late else [half]
    other = steps.arrive(other)
    finish = attention_grads_call if name == "attention" else assemble_call
    out[name] = finish([half, other], index % 2, F32, len(places))
    yield [] if late else [other]


def place_hot():
    place = jnp.arange(FRAME)
    row, col = place // WIN_W, place % WIN_W
    offset = (row[:, None] - row[None, :] + WIN_H - 1) * N_COL + (
        col[:, None] - col[None, :] + WIN_W - 1
    )
    return (offset.reshape(1, -1) == jnp.arange(N_ROW * N_COL)[:, None]).astype(F32)


def bias_blocks(rel_table):
    heads = rel_table.shape[0]
    cube = rel_table.reshape(heads * N_TIME, N_ROW * N_COL)
    return lax.dot(cube, place_hot(), precision=highest).reshape(heads, N_TIME, FRAME, FRAME)


def collect_blocks(block_grad):
    heads = block_grad.shape[0]
    flat = block_grad.reshape(heads * N_TIME, FRAME * FRAME)
    cube = lax.dot_general(flat, place_hot(), (((1,), (1,)), ((), ())), precision=highest)
    return cube[:, ::-1].reshape(heads, -1)


def block_spec(heads, place):
    return pl.BlockSpec((heads, N_TIME, FRAME, FRAME), lambda i: (place, 0, 0, 0))


def frame_span(frame):
    return slice(frame * FRAME, (frame + 1) * FRAME)


def spread_blocks(blocks_ref, table, fill, transposed):
    for head in range(table.shape[0]):
        for offset in range(N_TIME):
            block = blocks_ref[head, offset]
            if transposed:
                block = block.T
            for query in range(WIN_T):
                key = query - (offset - WIN_T + 1)
                if 0 <= key < WIN_T:
                    row, col = (key, query) if transposed else (query, key)
                    table[head, frame_span(row), frame_span(col)] = block
        table[head, :, WIN_TOK:] = jnp.full((WIN_TOK, PAD_TOK - WIN_TOK), fill, F32)


def norm_kernel(tokens_ref, mod_ref, attn_in_ref):
    normed, _ = normalise(tokens_ref[...].astype(F32))
    attn_in_ref[...] = (normed * (1.0 + mod_ref[0, 1:2]) + mod_ref[0, 0:1]).astype(BF)


def norm_call(tokens, mods, deps=()):
    rows, width = tokens.shape
    return call_after(
        norm_kernel,
        deps,
        grid=(rows // WIN_TOK,),
        in_specs=[row_spec(WIN_TOK, width), mod_spec(1, mods.shape[1], width)],
        out_specs=row_spec(WIN_TOK, width),
        out_shape=shaped((rows, width), BF),
        compiler_params=params(),
        cost_estimate=cost(8),
        name="norm_in",
    )(tokens, mods)


def head_copies(value, heads):
    if heads == 1:
        return [value]
    lane = lax.broadcasted_iota(jnp.int32, value.shape, 1) // HEAD_DIM
    return [jnp.where(lane == head, value, jnp.zeros_like(value)) for head in range(heads)]


def pad_rows(value):
    return jnp.concatenate(
        [value, jnp.zeros((PAD_TOK - WIN_TOK, value.shape[1]), value.dtype)], axis=0
    )


def attend_kernel(x_ref, w_ref, blocks_ref, qkv_ref, mixed_ref, lse_ref, table, columns):
    heads = blocks_ref.shape[0]

    @pl.when(pl.program_id(0) == 0)
    def _():
        spread_blocks(blocks_ref, table, -1e30, False)
        columns[...] = jnp.zeros_like(columns)

    x = x_ref[...]
    queries = dot(x, w_ref[0]).astype(BF)
    keys = dot(x, w_ref[1]).astype(BF)
    values = dot(x, w_ref[2]).astype(BF)
    qkv_ref[0] = queries
    qkv_ref[1] = keys
    qkv_ref[2] = values
    scaled = queries * jnp.asarray(HEAD_DIM**-0.5, BF)
    for window in range(x.shape[0] // WIN_TOK):
        span = window_span(window)
        scores = dot(
            jnp.concatenate(head_copies(scaled[span], heads), axis=0), pad_rows(keys[span]), 1, 1
        )
        probs = []
        for head in range(heads):
            score = scores[window_span(head)] + table[head]
            top = jnp.max(score, axis=1, keepdims=True)
            exponent = jnp.exp(score - top)
            total = jnp.sum(exponent, axis=1, keepdims=True)
            probs.append((exponent * (1.0 / total)).astype(BF))
            columns[window, :WIN_TOK, head : head + 1] = top + jnp.log(total)
        value = jnp.concatenate([pad_rows(part) for part in head_copies(values[span], heads)], axis=0)
        mixed_ref[span, :] = dot(jnp.concatenate(probs, axis=1), value).astype(BF)
        lse_ref[window] = columns[window].T[: lse_ref.shape[1]]


def attend_call(attn_in, weight, blocks, deps=()):
    rows, width = attn_in.shape
    cols = weight.shape[2]
    blocks, place, heads = blocks
    windows = rows // WIN_TOK
    per = per_step(rows)
    block = per * WIN_TOK
    stat_rows = -(-heads // 8) * 8
    return call_after(
        attend_kernel,
        deps,
        grid=(windows // per,),
        in_specs=[row_spec(block, width), whole_spec(weight.shape), block_spec(heads, place)],
        out_specs=[
            part_spec(block, cols),
            row_spec(block, cols),
            mod_spec(per, stat_rows, PAD_TOK),
        ],
        out_shape=[
            shaped((3, rows, cols), BF),
            shaped((rows, cols), BF),
            shaped((windows, stat_rows, PAD_TOK), F32),
        ],
        scratch_shapes=[
            pltpu.VMEM((heads, WIN_TOK, PAD_TOK), F32),
            pltpu.VMEM((per, PAD_TOK, 128), F32),
        ],
        compiler_params=params(),
        cost_estimate=cost(19),
        name="attend",
    )(attn_in, weight, blocks)


def attend_back_kernel(*refs, held):
    grad_ref, out_w_ref, qkv_ref, mixed_ref, lse_ref, blocks_ref, x_ref = refs[:7]
    dqkv_ref, dblocks_ref, dw_ref, table, total, x_all, grad_all, d_all = refs[7 + held :]
    heads = blocks_ref.shape[0]
    cols = out_w_ref.shape[0]
    step = pl.program_id(0)

    @pl.when(step == 0)
    def _():
        spread_blocks(blocks_ref, table, 0.0, True)
        total[...] = jnp.zeros_like(total)

    grads_mixed = dot(grad_ref[...], out_w_ref[...], 1, 1).astype(BF)
    scale = jnp.asarray(HEAD_DIM**-0.5, BF)
    head_rows = (lse_ref.shape[1], cols)
    head_hot = (
        lax.broadcasted_iota(jnp.int32, head_rows, 1) // HEAD_DIM
        == lax.broadcasted_iota(jnp.int32, head_rows, 0)
    ).astype(BF)
    block = grad_ref.shape[0]
    rows = pl.ds(pl.multiple_of(step * block, block), block)
    x_all[rows, :] = x_ref[...]
    grad_all[rows, :] = grad_ref[...]
    d_all[3, rows, :] = mixed_ref[...]
    for window in range(block // WIN_TOK):
        place = window_span(window)
        grad_mixed = grads_mixed[place]
        query = qkv_ref[0, place, :]
        key = qkv_ref[1, place, :]
        value = qkv_ref[2, place, :]
        product = grad_mixed.astype(F32) * mixed_ref[place, :].astype(F32)
        upper = product.astype(BF)
        lower = (product - upper.astype(F32)).astype(BF)
        inner = dot(head_hot, pad_rows(upper), 1, 1) + dot(head_hot, pad_rows(lower), 1, 1)
        keys = jnp.concatenate(head_copies(key * scale, heads), axis=0)
        values = jnp.concatenate(head_copies(value, heads), axis=0)
        query_pad = pad_rows(query)
        grad_pad = pad_rows(grad_mixed)
        scores = dot(keys, query_pad, 1, 1)
        grad_probs = dot(values, grad_pad, 1, 1)
        probs = []
        grad_scores = []
        for head in range(heads):
            span = window_span(head)
            prob = jnp.exp(scores[span] + table[head] - lse_ref[window, head : head + 1, :])
            grad_score = (prob * (grad_probs[span] - inner[head : head + 1, :])).astype(BF)
            probs.append(prob.astype(BF))
            grad_scores.append(grad_score)
            total[head] += grad_score.astype(F32)
        wide = jnp.concatenate(grad_scores, axis=1)
        grad_value = dot(
            jnp.concatenate(probs, axis=1), jnp.concatenate(head_copies(grad_pad, heads), axis=0)
        )
        grad_key = dot(wide, jnp.concatenate(head_copies(query_pad * scale, heads), axis=0))
        grad_query = dot(jnp.concatenate(grad_scores, axis=0), keys, 0, 0)[:WIN_TOK]
        own = pl.ds(pl.multiple_of(step * block + window * WIN_TOK, WIN_TOK), WIN_TOK)
        for part, grad in enumerate((grad_query, grad_key, grad_value)):
            grad = grad.astype(BF)
            dqkv_ref[part, place, :] = grad
            d_all[part, own, :] = grad

    @pl.when(step == pl.num_programs(0) - 1)
    def _():
        for part in range(4):
            left = grad_all if part == 3 else x_all
            dw_ref[part] = dot(left[...], d_all[part], 0, 0).astype(BF)
        for head in range(heads):
            for offset in range(N_TIME):
                block = None
                for query in range(WIN_T):
                    key = query - (offset - WIN_T + 1)
                    if 0 <= key < WIN_T:
                        part = total[head, frame_span(key), frame_span(query)]
                        block = part if block is None else block + part
                dblocks_ref[head, offset] = block


def attend_back_call(grad_attn, out_weight, qkv, mixed, lse, blocks, attn_in, block_grads, deps=()):
    rows, width = grad_attn.shape
    cols = out_weight.shape[0]
    blocks, place, heads = blocks
    per = per_step(rows)
    block = per * WIN_TOK
    held = () if block_grads is None else (block_grads,)
    return call_after(
        functools.partial(attend_back_kernel, held=len(held)),
        deps,
        grid=(rows // block,),
        in_specs=[
            row_spec(block, width),
            whole_spec(out_weight.shape),
            part_spec(block, cols),
            row_spec(block, cols),
            mod_spec(per, lse.shape[1], PAD_TOK),
            block_spec(heads, place),
            row_spec(block, width),
        ]
        + [pl.BlockSpec(memory_space=pl.ANY)] * len(held),
        out_specs=[
            part_spec(block, cols),
            block_spec(heads, place),
            whole_spec((4, width, cols)),
        ],
        out_shape=[
            shaped((3, rows, cols), BF),
            shaped(blocks.shape, F32),
            shaped((4, width, cols), BF),
        ],
        scratch_shapes=[pltpu.VMEM((heads, WIN_TOK, PAD_TOK), F32)] * 2
        + [pltpu.VMEM((rows, width), BF)] * 2
        + [pltpu.VMEM((4, rows, cols), BF)],
        input_output_aliases={7: 1} if held else {},
        compiler_params=params(),
        cost_estimate=cost(30),
        name="attend_back",
    )(grad_attn, out_weight, qkv, mixed, lse, blocks, attn_in, *held)


def middle_kernel(*refs, count):
    mixed_refs = refs[:count]
    weight_refs = refs[count : 2 * count]
    tokens_ref, cot_ref, mod_ref, attn_out_ref, mlp_in_ref, grad_mlp_ref = refs[2 * count :]
    attn_out = dot(mixed_refs[0][...], weight_refs[0][...])
    for mixed_ref, weight_ref in zip(mixed_refs[1:], weight_refs[1:]):
        attn_out = attn_out + dot(mixed_ref[...], weight_ref[...])
    attn_out_ref[...] = attn_out.astype(BF)
    for window in range(attn_out.shape[0] // WIN_TOK):
        span = window_span(window)
        mod = mod_ref[window]
        resid = tokens_ref[span, :].astype(F32) + mod[2:3] * attn_out[span]
        normed, _ = normalise(resid)
        mlp_in_ref[span, :] = (normed * (1.0 + mod[4:5]) + mod[3:4]).astype(BF)
        grad_mlp_ref[span, :] = (mod[5:6] * cot_ref[span, :].astype(F32)).astype(BF)


def middle_call(mixed, weights, tokens, cotangent, mods, deps=()):
    rows, width = tokens.shape
    count = len(mixed)
    per = per_step(rows)
    block = per * WIN_TOK
    row = row_spec(block, width)
    return call_after(
        functools.partial(middle_kernel, count=count),
        deps,
        grid=(rows // block,),
        in_specs=[row_spec(block, part.shape[1]) for part in mixed]
        + [whole_spec(part.shape) for part in weights]
        + [row, row, mod_spec(per, mods.shape[1], width)],
        out_specs=[row, row, row],
        out_shape=[
            shaped((rows, width), BF),
            shaped((rows, width), BF),
            shaped((rows, width), BF),
        ],
        compiler_params=params(),
        cost_estimate=cost(16),
        name="middle",
    )(*mixed, *weights, tokens, cotangent, mods)


def mlp_kernel(
    x_ref, g_ref, up_ref, down_ref, act_ref, ghid_ref, *rest, chunk
):
    down_total, up_total = rest[4:]
    step = pl.program_id(0)
    x = x_ref[...]
    g = g_ref[...]
    for start in range(0, up_ref.shape[1], chunk):
        span = slice(start, start + chunk)
        hidden = dot(x, up_ref[:, span])
        grad_act = dot(g, down_ref[span, :], 1, 1)
        cubic = GELU_B * (hidden * hidden)
        gate = 0.5 + 0.5 * jnp.tanh(hidden * (GELU_A + cubic))
        act_ref[:, span] = (hidden * gate).astype(BF)
        slope = gate + gate * ((1.0 - gate) * (hidden * (2.0 * GELU_A + 6.0 * cubic)))
        ghid_ref[:, span] = (grad_act * slope).astype(BF)

    @pl.when(step == 0)
    def _():
        down_total[...] = dot(act_ref[...], g, 0, 0)
        up_total[...] = dot(x, ghid_ref[...], 0, 0)

    @pl.when(step > 0)
    def _():
        down_total[...] += dot(act_ref[...], g, 0, 0)
        up_total[...] += dot(x, ghid_ref[...], 0, 0)

    @pl.when(step == pl.num_programs(0) - 1)
    def _():
        for place, total in enumerate((down_total, up_total)):
            size = total.shape[0] // 2
            rest[2 * place][...] = total[:size].astype(BF)
            rest[2 * place + 1][...] = total[size:].astype(BF)


MLP_BLOCK = 1280
MLP_CHUNK = 512


def mlp_call(x, g, up, down, deps=()):
    rows, width = x.shape
    hidden = up.shape[1]
    block = MLP_BLOCK if rows % MLP_BLOCK == 0 else WIN_TOK
    row = row_spec(block, width)
    wide = row_spec(block, hidden)
    halves = [(hidden // 2, width)] * 2 + [(width // 2, hidden)] * 2
    return call_after(
        functools.partial(mlp_kernel, chunk=min(MLP_CHUNK, hidden)),
        deps,
        grid=(rows // block,),
        in_specs=[row, row, whole_spec(up.shape), whole_spec(down.shape)],
        out_specs=[wide, wide] + [whole_spec(shape) for shape in halves],
        out_shape=[
            shaped((rows, hidden), BF),
            shaped((rows, hidden), BF),
        ]
        + [shaped(shape, BF) for shape in halves],
        scratch_shapes=[pltpu.VMEM(down.shape, F32), pltpu.VMEM(up.shape, F32)],
        compiler_params=params(),
        cost_estimate=cost(30),
        name="mlp",
    )(x, g, up, down)


def mlp_out_kernel(*refs, count):
    act_refs, ghid_refs, down_refs, up_refs = [
        refs[place * count : (place + 1) * count] for place in range(4)
    ]
    tokens_ref, cot_ref, attn_out_ref, mod_ref, out_ref, gres_ref, gattn_ref, sums_ref = refs[
        4 * count :
    ]
    join = lambda parts, axis: jnp.concatenate([part[...] for part in parts], axis=axis)
    mlp_outs = dot(join(act_refs, 1), join(down_refs, 0))
    gins = dot(join(ghid_refs, 1), join(up_refs, 1), 1, 1)
    for window in range(gins.shape[0] // WIN_TOK):
        span = window_span(window)
        mod = mod_ref[window]
        mlp_out, gin = mlp_outs[span], gins[span]
        cot = cot_ref[span, :].astype(F32)
        attn_out = attn_out_ref[span, :].astype(F32)
        resid = tokens_ref[span, :].astype(F32) + mod[2:3] * attn_out
        out_ref[span, :] = (resid + mod[5:6] * mlp_out).astype(BF)
        normed, inverse = normalise(resid)
        gres = cot + normalise_back(normed, inverse, gin * (1.0 + mod[4:5]))
        gres_ref[span, :] = gres.astype(BF)
        gattn_ref[span, :] = (mod[2:3] * gres).astype(BF)
        sums_ref[window, 0:1] = jnp.sum(gres * attn_out, axis=0, keepdims=True)
        sums_ref[window, 1:2] = jnp.sum(gin, axis=0, keepdims=True)
        sums_ref[window, 2:3] = jnp.sum(gin * normed, axis=0, keepdims=True)
        sums_ref[window, 3:4] = jnp.sum(cot * mlp_out, axis=0, keepdims=True)


def kept_spec(shape):
    return pl.BlockSpec(shape, lambda i: (0,) * len(shape), pipeline_mode=pl.Buffered(1))


def mlp_out_call(act, ghid, down, up, tokens, cotangent, attn_out, mods, deps=()):
    rows, width = tokens.shape
    per = 1
    block = per * WIN_TOK
    row = row_spec(block, width)
    windows = rows // WIN_TOK
    return call_after(
        functools.partial(mlp_out_kernel, count=len(act)),
        deps,
        grid=(windows // per,),
        in_specs=[row_spec(block, part.shape[1]) for part in act + ghid]
        + [kept_spec(part.shape) for part in down + up]
        + [row, row, row, mod_spec(per, mods.shape[1], width)],
        out_specs=[row, row, row, mod_spec(per, 4, width)],
        out_shape=[
            shaped((rows, width), BF),
            shaped((rows, width), BF),
            shaped((rows, width), BF),
            shaped((windows, 4, width), F32),
        ],
        compiler_params=params(),
        cost_estimate=cost(55),
        name="mlp_out",
    )(*act, *ghid, *down, *up, tokens, cotangent, attn_out, mods)


def last_kernel(*refs, count):
    dqkv_refs = refs[:count]
    weight_refs = refs[count : 2 * count]
    tokens_ref, gres_ref, mod_ref, out_ref, sums_ref = refs[2 * count :]
    join = lambda refs: jnp.concatenate([ref[part] for ref in refs for part in range(3)], axis=1)
    gin = dot(join(dqkv_refs), join(weight_refs), 1, 1)
    for window in range(gin.shape[0] // WIN_TOK):
        span = window_span(window)
        normed, inverse = normalise(tokens_ref[span, :].astype(F32))
        grad = gin[span]
        out_ref[span, :] = (
            gres_ref[span, :].astype(F32) + normalise_back(normed, inverse, grad * (1.0 + mod_ref[window, 1:2]))
        ).astype(BF)
        sums_ref[window, 0:1] = jnp.sum(grad, axis=0, keepdims=True)
        sums_ref[window, 1:2] = jnp.sum(grad * normed, axis=0, keepdims=True)


def last_call(dqkv, weights, tokens, gres, mods, deps=()):
    rows, width = tokens.shape
    count = len(dqkv)
    per = 1
    block = per * WIN_TOK
    row = row_spec(block, width)
    windows = rows // WIN_TOK
    return call_after(
        functools.partial(last_kernel, count=count),
        deps,
        grid=(windows // per,),
        in_specs=[part_spec(block, part.shape[2]) for part in dqkv]
        + [kept_spec(part.shape) for part in weights]
        + [row, row, mod_spec(per, mods.shape[1], width)],
        out_specs=[row, mod_spec(per, 2, width)],
        out_shape=[shaped((rows, width), BF), shaped((windows, 2, width), F32)],
        compiler_params=params(),
        cost_estimate=cost(28),
        name="last",
    )(*dqkv, *weights, tokens, gres, mods)


def body(
    n_dp,
    n_mp,
    tokens,
    cotangent,
    qkv_weight,
    out_weight,
    up_weight,
    down_weight,
    rel_bias,
    ada_weight,
    ada_bias,
    class_embed,
    window_clip,
    timesteps,
    class_ids,
):
    mp_index = lax.axis_index("mp")
    micro, local_rows, width = tokens.shape
    local_cols = class_embed.shape[1]
    clips = timesteps.shape[1]
    own_windows = local_rows // WIN_TOK
    rows = micro * local_rows
    tokens_flat = tokens.reshape(rows, width)
    cot_flat = cotangent.reshape(rows, width)
    masks = range(n_mp)

    columns = mp_index * local_cols + jnp.arange(local_cols)
    half_width = width // 2
    freq_index = (columns % half_width).astype(F32)
    frequency = jnp.exp(-math.log(10000.0) * freq_index / half_width)
    angle = timesteps.astype(F32)[..., None] * frequency
    step_embed = jnp.where(columns < half_width, jnp.sin(angle), jnp.cos(angle))
    class_hot = (class_ids[..., None] == jnp.arange(class_embed.shape[0])).astype(F32)
    condition = step_embed + jnp.einsum("mck,kd->mcd", class_hot, class_embed, precision=highest)
    lowered = jax.nn.silu(condition).astype(BF)
    mod_terms = jnp.einsum("mcd,de->mce", lowered, ada_weight, preferred_element_type=F32)
    near_terms = add_low(mod_terms, swap(mod_terms, "mp", n_mp, 1))
    modulation = near_terms
    for bit in bits_of(n_mp)[1:]:
        modulation = add_low(modulation, swap(modulation, "mp", n_mp, bit))
    modulation = modulation + ada_bias
    own_clip = lax.dynamic_slice_in_dim(window_clip, mp_index * own_windows, own_windows, 1)
    clip_hot = (own_clip[..., None] == jnp.arange(clips)).astype(F32)
    mods = jnp.einsum("mwc,mce->mwe", clip_hot, modulation, precision=highest)
    mods = mods.reshape(micro * own_windows, 6, width)

    steps = Steps()
    rel_tables = gather_shards(rel_bias, "mp", n_mp)
    blocks = bias_blocks(jnp.concatenate([rel_tables[m] for m in masks], axis=0))
    heads = rel_bias.shape[0]

    def gather(own, hold):
        shards = {}
        steps.jobs.append(gather_job(steps, own, shards, "mp", n_mp, hold))
        return shards

    def need(shards, mask, ties, token):
        while mask not in shards:
            ties = ties + steps.step(token)
        return ties

    qkv_w = gather(qkv_weight, 3)
    steps.step(modulation)
    attn_in = norm_call(tokens_flat, mods)
    out_w = gather(out_weight, 3)
    ties = steps.step(attn_in)
    qkv, mixed, lse = {}, {}, {}
    for m in masks:
        ties = need(qkv_w, m, ties, attn_in)
        qkv[m], mixed[m], lse[m] = attend_call(attn_in, qkv_w[m], (blocks, m, heads), ties)
        if m == 0:
            down_w = gather(down_weight, 4)
        elif m == 2 or m == n_mp - 1 == 1:
            up_w = gather(up_weight, 3)
        ties = steps.step(mixed[m])
    for m in masks:
        ties = need(out_w, m, ties, mixed[0])
    attn_out, mlp_in, grad_mlp = middle_call(
        [mixed[m] for m in masks], [out_w[m] for m in masks], tokens_flat, cot_flat, mods, ties
    )
    ties = steps.step(mlp_in)
    wide_sums = Sums(steps, n_mp, [0, 1, 1, 2])
    grads = {}
    steps.jobs.append(spread_job(steps, wide_sums, [0, 1], n_dp, True, False, grads, "down"))
    steps.jobs.append(spread_job(steps, wide_sums, [2, 3], n_dp, False, True, grads, "up"))
    act, grad_hidden = {}, {}
    for m in [m for m in masks if m % 2] + [m for m in reversed(masks) if m % 2 == 0]:
        ties = need(down_w, m, need(up_w, m, ties, mlp_in), mlp_in)
        act[m], grad_hidden[m], *wide_terms = mlp_call(mlp_in, grad_mlp, up_w[m], down_w[m], ties)
        wide_sums.add(m, wide_terms)
        ties = steps.step(wide_terms[0])
    block_out, grad_resid, grad_attn, late_sums = mlp_out_call(
        *[[part[m] for m in masks] for part in (act, grad_hidden, down_w, up_w)],
        tokens_flat,
        cot_flat,
        attn_out,
        mods,
        ties,
    )

    def clip_sums(window_sums):
        grouped = window_sums.reshape(micro, own_windows, -1)
        return jnp.einsum("mwc,mwe->mce", clip_hot, grouped, precision=highest).astype(BF)

    attn_sums = Sums(steps, n_mp, [0])
    steps.jobs.append(spread_job(steps, attn_sums, [0], n_dp, False, False, grads, "attention"))
    dqkv, block_grads = {}, None
    ties = steps.step(grad_attn)
    for m in reversed(masks):
        dqkv[m], block_grads, qkv_term = attend_back_call(
            grad_attn, out_w[m], qkv[m], mixed[m], lse[m], (blocks, m, heads), attn_in, block_grads, ties
        )
        attn_sums.add(m, [qkv_term.reshape(-1, qkv_term.shape[2])])
        ties = steps.step(qkv_term)
    token_grad, early_sums = last_call(
        [dqkv[m] for m in masks], [qkv_w[m] for m in masks], tokens_flat, grad_resid, mods, ties
    )
    ties = steps.step(token_grad)
    window_sums = after(jnp.concatenate([early_sums, late_sums], axis=1), *ties)
    rel_sums = after(block_grads, *ties)
    rel_sums = collect_blocks(rel_sums).astype(BF).reshape(n_mp, -1)
    table_size = rel_sums.shape[1]
    rel_sums = jnp.pad(rel_sums, ((0, 0), (0, -table_size % width))).reshape(n_mp, -1, width)
    clip_terms = clip_sums(window_sums).reshape(-1, width)
    summed = steps.step()
    down_grad = unfold_call(grads["down"], 2, summed)
    steps.first = [down_grad, grads["up"]]
    ties = steps.step()
    mod_total, rel_total = sum_everywhere(
        after(clip_terms, *ties), after(rel_sums, *ties), n_mp, n_dp
    )
    rel_grad = rel_total.reshape(-1)[:table_size].reshape(rel_bias.shape).astype(F32)
    steps.finish()

    up_grad = grads["up"]
    qkv_grad, out_grad = grads["attention"]
    qkv_grad = qkv_grad.reshape(qkv_weight.shape)
    mod_total = mod_total.astype(F32).reshape(micro, clips, 6 * width)
    ada_bias_grad = jnp.sum(mod_total, axis=(0, 1))
    ada_weight_grad = jnp.einsum(
        "mcd,mce->de", lowered.astype(F32), mod_total, precision=highest
    )
    grad_lowered = jnp.einsum(
        "mce,de->mcd", mod_total, ada_weight.astype(F32), precision=highest
    )
    grad_condition = jax.vjp(jax.nn.silu, condition)[1](grad_lowered)[0]
    class_grad = jnp.einsum("mck,mcd->kd", class_hot, grad_condition, precision=highest)
    return (
        block_out.reshape(tokens.shape),
        token_grad.reshape(tokens.shape),
        qkv_grad,
        out_grad,
        up_grad,
        down_grad,
        rel_grad,
        ada_weight_grad,
        ada_bias_grad,
        class_grad,
    )


def solution(mesh):
    rows = P(None, ("dp", "mp"), None)
    in_specs = (
        rows,
        rows,
        P(None, None, "mp"),
        P("mp", None),
        P(None, "mp"),
        P("mp", None),
        P("mp", None),
        P("mp", None),
        P(),
        P(None, "mp"),
        P(None, "dp"),
        P(),
        P(),
    )
    out_specs = (
        rows,
        rows,
        P(None, None, "mp"),
        P("mp", None),
        P(None, "mp"),
        P("mp", None),
        P("mp", None),
        P("mp", None),
        P(),
        P(None, "mp"),
    )
    step = functools.partial(body, mesh.shape["dp"], mesh.shape["mp"])
    return jax.shard_map(step, mesh=mesh, in_specs=in_specs, out_specs=out_specs, check_vma=False)
```

```python
import functools
import math

import jax
import jax.numpy as jnp
from jax import lax
from jax.experimental import pallas as pl
from jax.experimental.pallas import tpu as pltpu
from jax.sharding import PartitionSpec as P

WIN_T = 5
WIN_H = 8
WIN_W = 8
WIN_TOK = WIN_T * WIN_H * WIN_W
FRAME = WIN_H * WIN_W
PAD_TOK = 384
HEAD_DIM = 64
N_TIME, N_ROW, N_COL = 2 * WIN_T - 1, 2 * WIN_H - 1, 2 * WIN_W - 1

BF = jnp.bfloat16
F32 = jnp.float32
epsilon = 1e-06
highest = lax.Precision.HIGHEST
GELU_A = 0.7978845608028654
GELU_B = GELU_A * 0.044715
VMEM_LIMIT = 63 * 1024 * 1024


def dot(left, right, left_dim=1, right_dim=0):
    return lax.dot_general(
        left, right, (((left_dim,), (right_dim,)), ((), ())), preferred_element_type=F32
    )


def params():
    return pltpu.CompilerParams(vmem_limit_bytes=VMEM_LIMIT)


def shaped(shape, dtype):
    return jax.ShapeDtypeStruct(shape, dtype)


def row_spec(rows, cols):
    return pl.BlockSpec((rows, cols), lambda i: (i, 0))


def part_spec(rows, cols):
    return pl.BlockSpec((3, rows, cols), lambda i: (0, i, 0))


def per_step(rows):
    return 2 if rows % (2 * WIN_TOK) == 0 else 1


def window_span(window):
    return slice(window * WIN_TOK, (window + 1) * WIN_TOK)


def whole_spec(shape):
    return pl.BlockSpec(shape, lambda i: (0,) * len(shape))


def mod_spec(per, count, cols):
    return pl.BlockSpec((per, count, cols), lambda i: (i, 0, 0))


def cost(micros):
    return pl.CostEstimate(
        flops=int(micros * 1e9), bytes_accessed=int(micros * 3.5e6), transcendentals=0
    )


def call_after(kernel, deps, *, in_specs, **rest):
    deps = tuple(deps)
    count = len(in_specs)

    def run(*refs):
        kernel(*refs[:count], *refs[count + len(deps) :])

    call = pl.pallas_call(
        run, in_specs=list(in_specs) + [pl.BlockSpec(memory_space=pl.ANY)] * len(deps), **rest
    )
    return lambda *args: call(*args, *deps)


def after(value, *deps):
    return lax.optimization_barrier((value, *deps))[0]


def normalise(values):
    centred = values - jnp.mean(values, axis=-1, keepdims=True)
    inverse = lax.rsqrt(jnp.mean(centred * centred, axis=-1, keepdims=True) + epsilon)
    return centred * inverse, inverse


def normalise_back(normed, inverse, grad_in):
    return inverse * (
        grad_in
        - jnp.mean(grad_in, axis=-1, keepdims=True)
        - normed * jnp.mean(grad_in * normed, axis=-1, keepdims=True)
    )


def swap(value, axis, size, bit):
    return lax.ppermute(value, axis, [(i, i ^ bit) for i in range(size)])


def bits_of(size):
    return [1 << b for b in range(size.bit_length() - 1)]


def add_low(left, right):
    return (left.astype(F32) + right.astype(F32)).astype(left.dtype)


def gather_shards(own, axis, size):
    shards = {0: own}
    for bit in reversed(bits_of(size)):
        for mask in list(shards):
            shards[mask ^ bit] = swap(shards[mask], axis, size, bit)
    return shards


def reduce_all(value, axis, size):
    for bit in bits_of(size):
        value = add_low(value, swap(value, axis, size, bit))
    return value


def reduce_shards(terms, axis, size):
    terms = dict(terms)
    for bit in bits_of(size):
        for mask in [m for m in terms if m & bit]:
            terms[mask ^ bit] = add_low(terms[mask ^ bit], swap(terms.pop(mask), axis, size, bit))
    return terms[0]


def sum_kernel(*refs, groups):
    outs = refs[sum(groups) :]
    for out, group in zip(outs, groups):
        total = refs[0][...].astype(F32)
        for ref in refs[1:group]:
            total = total + ref[...].astype(F32)
        out[...] = total.astype(BF)
        refs = refs[group:]


def add_groups(groups):
    if all(len(group) == 1 for group in groups):
        return [group[0] for group in groups]
    shapes = [group[0].shape for group in groups]
    turns = 4 if all(shape[0] % 64 == 0 and shape[0] >= 512 for shape in shapes) else 1
    spec = lambda shape: row_spec(shape[0] // turns, shape[1])
    return pl.pallas_call(
        functools.partial(sum_kernel, groups=[len(group) for group in groups]),
        grid=(turns,),
        in_specs=[spec(array.shape) for group in groups for array in group],
        out_specs=[spec(shape) for shape in shapes],
        out_shape=[shaped(shape, BF) for shape in shapes],
        compiler_params=params(),
        cost_estimate=cost(0.001),
        name="add",
    )(*[array for group in groups for array in group])


def split_kernel(index_ref, *refs, count, groups, deps):
    outs = refs[sum(groups) + deps :]
    totals = []
    for group in groups:
        total = refs[0][...].astype(F32)
        for ref in refs[1:group]:
            total = total + ref[...].astype(F32)
        totals.append(total.astype(BF))
        refs = refs[group:]
    size = totals[0].shape[0]
    for k in range(count):

        @pl.when(pl.program_id(0) == k)
        def _():
            for place, total in enumerate(totals):
                outs[k][place * size : (place + 1) * size, :] = total


def split_call(groups, index, count, deps=()):
    rows, cols = groups[0][0].shape
    part = (rows // count, cols)
    piece = (len(groups) * part[0], cols)
    parts = [array for group in groups for array in group]
    spec = pltpu.PrefetchScalarGridSpec(
        num_scalar_prefetch=1,
        grid=(count,),
        in_specs=[pl.BlockSpec(part, lambda k, f: (f[0] ^ k, 0))] * len(parts)
        + [pl.BlockSpec(memory_space=pl.ANY)] * len(deps),
        out_specs=[pl.BlockSpec(piece, lambda k, f: (0, 0))] * count,
    )
    return pl.pallas_call(
        functools.partial(
            split_kernel, count=count, groups=[len(group) for group in groups], deps=len(deps)
        ),
        grid_spec=spec,
        out_shape=[shaped(piece, BF)] * count,
        compiler_params=params(),
        cost_estimate=cost(0.001),
        name="split",
    )(jnp.reshape(index, (1,)).astype(jnp.int32), *parts, *deps)


def assemble_kernel(index_ref, *refs, count, groups):
    step = pl.program_id(0)
    size = refs[-1].shape[0]
    rows = pl.ds(pl.multiple_of(step % groups * size, size), size)
    for k, ref in enumerate(refs[:count]):

        @pl.when(step // groups == k)
        def _():
            refs[-1][...] = ref[rows, :].astype(refs[-1].dtype)


def assemble_call(pieces, index, dtype, groups=1, deps=()):
    count = len(pieces)
    rows, cols = pieces[0].shape
    spec = pltpu.PrefetchScalarGridSpec(
        num_scalar_prefetch=1,
        grid=(count * groups,),
        in_specs=[pl.BlockSpec((rows, cols), lambda i, f: (0, 0))] * count
        + [pl.BlockSpec(memory_space=pl.ANY)] * len(deps),
        out_specs=pl.BlockSpec(
            (rows // groups, cols), lambda i, f: (i % groups * count + (f[0] ^ (i // groups)), 0)
        ),
    )
    return pl.pallas_call(
        functools.partial(assemble_kernel, count=count, groups=groups),
        grid_spec=spec,
        out_shape=shaped((rows * count, cols), dtype),
        compiler_params=params(),
        cost_estimate=cost(0.001),
        name="assemble",
    )(jnp.reshape(index, (1,)).astype(jnp.int32), *pieces, *deps)


def attention_grads_kernel(index_ref, own_ref, other_ref, qkv_ref, out_ref):
    step = pl.program_id(0)
    place = 2 * (index_ref[0] ^ (step // 2)) + step % 2
    size = qkv_ref.shape[0]
    rows = pl.ds(pl.multiple_of(step % 2 * size, size), size)
    for k, ref in enumerate((own_ref, other_ref)):

        @pl.when((step // 2 == k) & (place < 3))
        def _():
            qkv_ref[...] = ref[rows, :].astype(F32)

        @pl.when((step // 2 == k) & (place == 3))
        def _():
            out_ref[...] = ref[rows, :].astype(F32).T


def attention_grads_call(halves, index, dtype, groups):
    rows, cols = halves[0].shape
    size = rows // 2
    place = lambda i, f: (jnp.minimum(2 * (f[0] ^ (i // 2)) + i % 2, 2), 0)
    spec = pltpu.PrefetchScalarGridSpec(
        num_scalar_prefetch=1,
        grid=(4,),
        in_specs=[pl.BlockSpec((rows, cols), lambda i, f: (0, 0))] * 2,
        out_specs=[
            pl.BlockSpec((size, cols), place),
            pl.BlockSpec((cols, size), lambda i, f: (0, 0)),
        ],
    )
    return pl.pallas_call(
        attention_grads_kernel,
        grid_spec=spec,
        out_shape=[shaped((3 * size, cols), dtype), shaped((cols, size), dtype)],
        compiler_params=params(),
        cost_estimate=cost(0.001),
        name="attention_grads",
    )(jnp.reshape(index, (1,)).astype(jnp.int32), *halves)


def unfold_kernel(part_ref, out_ref):
    out_ref[...] = part_ref[...].astype(F32)


def unfold_call(parts, groups, deps):
    count, rows, cols = parts.shape
    far = count // 2
    own = far // groups

    def place(i):
        group, near, piece = i // (2 * own), i // own % 2, i % own
        return (2 * (group * own + piece) + near, 0, 0)

    return call_after(
        unfold_kernel,
        deps,
        grid=(count,),
        in_specs=[pl.BlockSpec((None, rows, cols), place)],
        out_specs=row_spec(rows, cols),
        out_shape=shaped((count * rows, cols), F32),
        compiler_params=params(),
        cost_estimate=cost(0.001),
        name="unfold",
    )(parts)


class Steps:
    def __init__(self):
        self.jobs, self.token, self.ties, self.first = [], None, [], []

    def swap(self, value, axis, size, bit):
        if self.token is not None:
            value = after(value, self.token)
        return swap(value, axis, size, bit)

    def arrive(self, value):
        return value if self.token is None else after(value, self.token)

    def step(self, token=None):
        self.token = token
        self.ties, jobs = [], []
        for job in self.jobs:
            try:
                self.ties = self.ties + next(job)
            except StopIteration:
                continue
            jobs.append(job)
        self.jobs = jobs
        return self.ties if token is None else self.ties + [token]

    def finish(self):
        while self.jobs:
            self.step()


def gather_job(steps, own, shards, axis, size, hold):
    shards[0] = own
    even = {0: own}
    shards[1] = steps.swap(own, axis, size, 1)
    for bit in reversed(bits_of(size)[1:]):
        new = {mask ^ bit: steps.swap(part, axis, size, bit) for mask, part in even.items()}
        for _ in range(hold):
            yield []
        new = {mask: steps.arrive(part) for mask, part in new.items()}
        even.update(new)
        for mask, part in new.items():
            shards[mask] = part
            shards[mask ^ 1] = steps.swap(part, axis, size, 1)
        yield list(new.values())


class Sums:
    def __init__(self, steps, size, lags):
        self.steps, self.size, self.lags = steps, size, lags
        self.parts = {mask: [[] for _ in lags] for mask in range(size)}
        nearest_first = sorted(range(1, size), key=lambda mask: (mask & -mask, mask))
        steps.jobs += [self.send(mask) for mask in nearest_first]

    def full(self, mask, places):
        low = mask & -mask if mask else self.size
        return all(len(self.parts[mask][i]) == low.bit_length() for i in places)

    def add(self, mask, terms):
        for part, term in zip(self.parts[mask], terms):
            part.append(term)

    def send(self, mask):
        every = range(len(self.lags))
        while not self.full(mask, every):
            yield []
        bit = mask & -mask
        values = list(add_groups(self.parts[mask]))
        lags = self.lags if bit > 1 else [0] * len(values)
        flying, ready = {}, values if bit > 1 else []
        for turn in range(max(lags) + 2):
            for i in every:
                if turn == lags[i] + 1:
                    other = self.steps.arrive(flying[i])
                    self.parts[mask ^ bit][i].append(other)
                    ready = ready + [other]
                if turn == lags[i]:
                    flying[i] = self.steps.swap(values[i], "mp", self.size, bit)
            yield ready
            ready = []


def sum_everywhere(shared, by_shard, n_mp, n_dp):
    rows = shared.shape[0]
    for axis, size in (("mp", n_mp), ("dp", n_dp)):
        for bit in bits_of(size):
            sent = by_shard
            if axis == "mp":
                pairs = (size // (2 * bit), 2, bit * by_shard.shape[1], by_shard.shape[2])
                sent = by_shard.reshape(pairs)[:, ::-1]
            sent = jnp.concatenate([shared, sent.reshape(-1, shared.shape[1])], axis=0)
            other = swap(sent, axis, size, bit)
            shared = add_low(shared, other[:rows])
            by_shard = add_low(by_shard, other[rows:].reshape(by_shard.shape))
    return shared, by_shard[0]


def spread_job(steps, sums, places, n_dp, offload, late, out, name):
    while not sums.full(0, places):
        yield []
    index = lax.axis_index("dp")
    count = n_dp // 2
    keep, send = split_call([sums.parts[0][i] for i in places], index % 2, 2)
    other = steps.swap(send, "dp", n_dp, 1)
    yield [send]
    pieces = split_call([[keep, steps.arrive(other)]], index // 2, count, steps.ties)
    others = [steps.swap(pieces[k], "dp", n_dp, 2 * k) for k in range(1, count)]
    yield [other, *pieces]
    (total,) = add_groups([[pieces[0]] + [steps.arrive(part) for part in others]])
    if offload:
        whole = lax.all_gather(total, "dp", axis=0)
        yield [total]
        yield []
        out[name] = steps.arrive(whole)
        yield [whole]
        return
    others = [steps.swap(total, "dp", n_dp, 2 * k) for k in range(1, count)]
    yield [total]
    others = [steps.arrive(part) for part in others]
    half = assemble_call([total] + others, index // 2, BF, deps=steps.first)
    if late:
        yield [half]
    other = steps.swap(half, "dp", n_dp, 1)
    yield [] if late else [half]
    other = steps.arrive(other)
    finish = attention_grads_call if name == "attention" else assemble_call
    out[name] = finish([half, other], index % 2, F32, len(places))
    yield [] if late else [other]


def place_hot():
    place = jnp.arange(FRAME)
    row, col = place // WIN_W, place % WIN_W
    offset = (row[:, None] - row[None, :] + WIN_H - 1) * N_COL + (
        col[:, None] - col[None, :] + WIN_W - 1
    )
    return (offset.reshape(1, -1) == jnp.arange(N_ROW * N_COL)[:, None]).astype(F32)


def bias_blocks(rel_table):
    heads = rel_table.shape[0]
    cube = rel_table.reshape(heads * N_TIME, N_ROW * N_COL)
    return lax.dot(cube, place_hot(), precision=highest).reshape(heads, N_TIME, FRAME, FRAME)


def collect_blocks(block_grad):
    heads = block_grad.shape[0]
    flat = block_grad.reshape(heads * N_TIME, FRAME * FRAME)
    cube = lax.dot_general(flat, place_hot(), (((1,), (1,)), ((), ())), precision=highest)
    return cube[:, ::-1].reshape(heads, -1)


def block_spec(heads, place):
    return pl.BlockSpec((heads, N_TIME, FRAME, FRAME), lambda i: (place, 0, 0, 0))


def frame_span(frame):
    return slice(frame * FRAME, (frame + 1) * FRAME)


def spread_blocks(blocks_ref, table, fill, transposed):
    for head in range(table.shape[0]):
        for offset in range(N_TIME):
            block = blocks_ref[head, offset]
            if transposed:
                block = block.T
            for query in range(WIN_T):
                key = query - (offset - WIN_T + 1)
                if 0 <= key < WIN_T:
                    row, col = (key, query) if transposed else (query, key)
                    table[head, frame_span(row), frame_span(col)] = block
        table[head, :, WIN_TOK:] = jnp.full((WIN_TOK, PAD_TOK - WIN_TOK), fill, F32)


def norm_kernel(tokens_ref, mod_ref, attn_in_ref):
    normed, _ = normalise(tokens_ref[...].astype(F32))
    attn_in_ref[...] = (normed * (1.0 + mod_ref[0, 1:2]) + mod_ref[0, 0:1]).astype(BF)


def norm_call(tokens, mods, deps=()):
    rows, width = tokens.shape
    return call_after(
        norm_kernel,
        deps,
        grid=(rows // WIN_TOK,),
        in_specs=[row_spec(WIN_TOK, width), mod_spec(1, mods.shape[1], width)],
        out_specs=row_spec(WIN_TOK, width),
        out_shape=shaped((rows, width), BF),
        compiler_params=params(),
        cost_estimate=cost(8),
        name="norm_in",
    )(tokens, mods)


def head_copies(value, heads):
    if heads == 1:
        return [value]
    lane = lax.broadcasted_iota(jnp.int32, value.shape, 1) // HEAD_DIM
    return [jnp.where(lane == head, value, jnp.zeros_like(value)) for head in range(heads)]


def pad_rows(value):
    return jnp.concatenate(
        [value, jnp.zeros((PAD_TOK - WIN_TOK, value.shape[1]), value.dtype)], axis=0
    )


def attend_kernel(x_ref, w_ref, blocks_ref, qkv_ref, mixed_ref, lse_ref, table, columns):
    heads = blocks_ref.shape[0]

    @pl.when(pl.program_id(0) == 0)
    def _():
        spread_blocks(blocks_ref, table, -1e30, False)
        columns[...] = jnp.zeros_like(columns)

    x = x_ref[...]
    queries = dot(x, w_ref[0]).astype(BF)
    keys = dot(x, w_ref[1]).astype(BF)
    values = dot(x, w_ref[2]).astype(BF)
    qkv_ref[0] = queries
    qkv_ref[1] = keys
    qkv_ref[2] = values
    scaled = queries * jnp.asarray(HEAD_DIM**-0.5, BF)
    for window in range(x.shape[0] // WIN_TOK):
        span = window_span(window)
        scores = dot(
            jnp.concatenate(head_copies(scaled[span], heads), axis=0), pad_rows(keys[span]), 1, 1
        )
        probs = []
        for head in range(heads):
            score = scores[window_span(head)] + table[head]
            top = jnp.max(score, axis=1, keepdims=True)
            exponent = jnp.exp(score - top)
            total = jnp.sum(exponent, axis=1, keepdims=True)
            probs.append((exponent * (1.0 / total)).astype(BF))
            columns[window, :WIN_TOK, head : head + 1] = top + jnp.log(total)
        value = jnp.concatenate([pad_rows(part) for part in head_copies(values[span], heads)], axis=0)
        mixed_ref[span, :] = dot(jnp.concatenate(probs, axis=1), value).astype(BF)
        lse_ref[window] = columns[window].T[: lse_ref.shape[1]]


def attend_call(attn_in, weight, blocks, deps=(), most=2):
    rows, width = attn_in.shape
    cols = weight.shape[2]
    blocks, place, heads = blocks
    windows = rows // WIN_TOK
    per = min(most, per_step(rows))
    block = per * WIN_TOK
    stat_rows = -(-heads // 8) * 8
    return call_after(
        attend_kernel,
        deps,
        grid=(windows // per,),
        in_specs=[row_spec(block, width), whole_spec(weight.shape), block_spec(heads, place)],
        out_specs=[
            part_spec(block, cols),
            row_spec(block, cols),
            mod_spec(per, stat_rows, PAD_TOK),
        ],
        out_shape=[
            shaped((3, rows, cols), BF),
            shaped((rows, cols), BF),
            shaped((windows, stat_rows, PAD_TOK), F32),
        ],
        scratch_shapes=[
            pltpu.VMEM((heads, WIN_TOK, PAD_TOK), F32),
            pltpu.VMEM((per, PAD_TOK, 128), F32),
        ],
        compiler_params=params(),
        cost_estimate=cost(19),
        name="attend",
    )(attn_in, weight, blocks)


def attend_back_kernel(*refs, held):
    grad_ref, out_w_ref, qkv_ref, mixed_ref, lse_ref, blocks_ref, x_ref = refs[:7]
    dqkv_ref, dblocks_ref, dw_ref, table, total, x_all, grad_all, d_all = refs[7 + held :]
    heads = blocks_ref.shape[0]
    cols = out_w_ref.shape[0]
    step = pl.program_id(0)

    @pl.when(step == 0)
    def _():
        spread_blocks(blocks_ref, table, 0.0, True)
        total[...] = jnp.zeros_like(total)

    grads_mixed = dot(grad_ref[...], out_w_ref[...], 1, 1).astype(BF)
    scale = jnp.asarray(HEAD_DIM**-0.5, BF)
    head_rows = (lse_ref.shape[1], cols)
    head_hot = (
        lax.broadcasted_iota(jnp.int32, head_rows, 1) // HEAD_DIM
        == lax.broadcasted_iota(jnp.int32, head_rows, 0)
    ).astype(BF)
    block = grad_ref.shape[0]
    rows = pl.ds(pl.multiple_of(step * block, block), block)
    x_all[rows, :] = x_ref[...]
    grad_all[rows, :] = grad_ref[...]
    d_all[3, rows, :] = mixed_ref[...]
    for window in range(block // WIN_TOK):
        place = window_span(window)
        grad_mixed = grads_mixed[place]
        query = qkv_ref[0, place, :]
        key = qkv_ref[1, place, :]
        value = qkv_ref[2, place, :]
        product = grad_mixed.astype(F32) * mixed_ref[place, :].astype(F32)
        upper = product.astype(BF)
        lower = (product - upper.astype(F32)).astype(BF)
        inner = dot(head_hot, pad_rows(upper), 1, 1) + dot(head_hot, pad_rows(lower), 1, 1)
        keys = jnp.concatenate(head_copies(key * scale, heads), axis=0)
        values = jnp.concatenate(head_copies(value, heads), axis=0)
        query_pad = pad_rows(query)
        grad_pad = pad_rows(grad_mixed)
        scores = dot(keys, query_pad, 1, 1)
        grad_probs = dot(values, grad_pad, 1, 1)
        probs = []
        grad_scores = []
        for head in range(heads):
            span = window_span(head)
            prob = jnp.exp(scores[span] + table[head] - lse_ref[window, head : head + 1, :])
            grad_score = (prob * (grad_probs[span] - inner[head : head + 1, :])).astype(BF)
            probs.append(prob.astype(BF))
            grad_scores.append(grad_score)
            total[head] += grad_score.astype(F32)
        wide = jnp.concatenate(grad_scores, axis=1)
        grad_value = dot(
            jnp.concatenate(probs, axis=1), jnp.concatenate(head_copies(grad_pad, heads), axis=0)
        )
        grad_key = dot(wide, jnp.concatenate(head_copies(query_pad * scale, heads), axis=0))
        grad_query = dot(jnp.concatenate(grad_scores, axis=0), keys, 0, 0)[:WIN_TOK]
        own = pl.ds(pl.multiple_of(step * block + window * WIN_TOK, WIN_TOK), WIN_TOK)
        for part, grad in enumerate((grad_query, grad_key, grad_value)):
            grad = grad.astype(BF)
            dqkv_ref[part, place, :] = grad
            d_all[part, own, :] = grad

    @pl.when(step == pl.num_programs(0) - 1)
    def _():
        for part in range(4):
            left = grad_all if part == 3 else x_all
            dw_ref[part] = dot(left[...], d_all[part], 0, 0).astype(BF)
        for head in range(heads):
            for offset in range(N_TIME):
                block = None
                for query in range(WIN_T):
                    key = query - (offset - WIN_T + 1)
                    if 0 <= key < WIN_T:
                        part = total[head, frame_span(key), frame_span(query)]
                        block = part if block is None else block + part
                dblocks_ref[head, offset] = block


def attend_back_call(grad_attn, out_weight, qkv, mixed, lse, blocks, attn_in, block_grads, deps=()):
    rows, width = grad_attn.shape
    cols = out_weight.shape[0]
    blocks, place, heads = blocks
    per = per_step(rows)
    block = per * WIN_TOK
    held = () if block_grads is None else (block_grads,)
    return call_after(
        functools.partial(attend_back_kernel, held=len(held)),
        deps,
        grid=(rows // block,),
        in_specs=[
            row_spec(block, width),
            whole_spec(out_weight.shape),
            part_spec(block, cols),
            row_spec(block, cols),
            mod_spec(per, lse.shape[1], PAD_TOK),
            block_spec(heads, place),
            row_spec(block, width),
        ]
        + [pl.BlockSpec(memory_space=pl.ANY)] * len(held),
        out_specs=[
            part_spec(block, cols),
            block_spec(heads, place),
            whole_spec((4, width, cols)),
        ],
        out_shape=[
            shaped((3, rows, cols), BF),
            shaped(blocks.shape, F32),
            shaped((4, width, cols), BF),
        ],
        scratch_shapes=[pltpu.VMEM((heads, WIN_TOK, PAD_TOK), F32)] * 2
        + [pltpu.VMEM((rows, width), BF)] * 2
        + [pltpu.VMEM((4, rows, cols), BF)],
        input_output_aliases={7: 1} if held else {},
        compiler_params=params(),
        cost_estimate=cost(30),
        name="attend_back",
    )(grad_attn, out_weight, qkv, mixed, lse, blocks, attn_in, *held)


def middle_kernel(*refs, count):
    mixed_refs = refs[:count]
    weight_refs = refs[count : 2 * count]
    tokens_ref, cot_ref, mod_ref, attn_out_ref, mlp_in_ref, grad_mlp_ref = refs[2 * count :]
    attn_out = dot(mixed_refs[0][...], weight_refs[0][...])
    for mixed_ref, weight_ref in zip(mixed_refs[1:], weight_refs[1:]):
        attn_out = attn_out + dot(mixed_ref[...], weight_ref[...])
    attn_out_ref[...] = attn_out.astype(BF)
    for window in range(attn_out.shape[0] // WIN_TOK):
        span = window_span(window)
        mod = mod_ref[window]
        resid = tokens_ref[span, :].astype(F32) + mod[2:3] * attn_out[span]
        normed, _ = normalise(resid)
        mlp_in_ref[span, :] = (normed * (1.0 + mod[4:5]) + mod[3:4]).astype(BF)
        grad_mlp_ref[span, :] = (mod[5:6] * cot_ref[span, :].astype(F32)).astype(BF)


def middle_call(mixed, weights, tokens, cotangent, mods, deps=()):
    rows, width = tokens.shape
    count = len(mixed)
    per = per_step(rows)
    block = per * WIN_TOK
    row = row_spec(block, width)
    return call_after(
        functools.partial(middle_kernel, count=count),
        deps,
        grid=(rows // block,),
        in_specs=[row_spec(block, part.shape[1]) for part in mixed]
        + [whole_spec(part.shape) for part in weights]
        + [row, row, mod_spec(per, mods.shape[1], width)],
        out_specs=[row, row, row],
        out_shape=[
            shaped((rows, width), BF),
            shaped((rows, width), BF),
            shaped((rows, width), BF),
        ],
        compiler_params=params(),
        cost_estimate=cost(16),
        name="middle",
    )(*mixed, *weights, tokens, cotangent, mods)


def mlp_kernel(
    x_ref, g_ref, up_ref, down_ref, act_ref, ghid_ref, *rest, chunk
):
    down_total, up_total = rest[4:]
    step = pl.program_id(0)
    x = x_ref[...]
    g = g_ref[...]
    for start in range(0, up_ref.shape[1], chunk):
        span = slice(start, start + chunk)
        hidden = dot(x, up_ref[:, span])
        grad_act = dot(g, down_ref[span, :], 1, 1)
        cubic = GELU_B * (hidden * hidden)
        gate = 0.5 + 0.5 * jnp.tanh(hidden * (GELU_A + cubic))
        act_ref[:, span] = (hidden * gate).astype(BF)
        slope = gate + gate * ((1.0 - gate) * (hidden * (2.0 * GELU_A + 6.0 * cubic)))
        ghid_ref[:, span] = (grad_act * slope).astype(BF)

    @pl.when(step == 0)
    def _():
        down_total[...] = dot(act_ref[...], g, 0, 0)
        up_total[...] = dot(x, ghid_ref[...], 0, 0)

    @pl.when(step > 0)
    def _():
        down_total[...] += dot(act_ref[...], g, 0, 0)
        up_total[...] += dot(x, ghid_ref[...], 0, 0)

    @pl.when(step == pl.num_programs(0) - 1)
    def _():
        for place, total in enumerate((down_total, up_total)):
            size = total.shape[0] // 2
            rest[2 * place][...] = total[:size].astype(BF)
            rest[2 * place + 1][...] = total[size:].astype(BF)


MLP_BLOCK = 640
MLP_CHUNK = 512


def mlp_call(x, g, up, down, deps=()):
    rows, width = x.shape
    hidden = up.shape[1]
    block = MLP_BLOCK if rows % MLP_BLOCK == 0 else WIN_TOK
    row = row_spec(block, width)
    wide = row_spec(block, hidden)
    halves = [(hidden // 2, width)] * 2 + [(width // 2, hidden)] * 2
    return call_after(
        functools.partial(mlp_kernel, chunk=min(MLP_CHUNK, hidden)),
        deps,
        grid=(rows // block,),
        in_specs=[row, row, whole_spec(up.shape), whole_spec(down.shape)],
        out_specs=[wide, wide] + [whole_spec(shape) for shape in halves],
        out_shape=[
            shaped((rows, hidden), BF),
            shaped((rows, hidden), BF),
        ]
        + [shaped(shape, BF) for shape in halves],
        scratch_shapes=[pltpu.VMEM(down.shape, F32), pltpu.VMEM(up.shape, F32)],
        compiler_params=params(),
        cost_estimate=cost(30),
        name="mlp",
    )(x, g, up, down)


def mlp_out_kernel(*refs, count):
    act_refs, ghid_refs, down_refs, up_refs = [
        refs[place * count : (place + 1) * count] for place in range(4)
    ]
    tokens_ref, cot_ref, attn_out_ref, mod_ref, out_ref, gres_ref, gattn_ref, sums_ref = refs[
        4 * count :
    ]
    join = lambda parts, axis: jnp.concatenate([part[...] for part in parts], axis=axis)
    mlp_outs = dot(join(act_refs, 1), join(down_refs, 0))
    gins = dot(join(ghid_refs, 1), join(up_refs, 1), 1, 1)
    for window in range(gins.shape[0] // WIN_TOK):
        span = window_span(window)
        mod = mod_ref[window]
        mlp_out, gin = mlp_outs[span], gins[span]
        cot = cot_ref[span, :].astype(F32)
        attn_out = attn_out_ref[span, :].astype(F32)
        resid = tokens_ref[span, :].astype(F32) + mod[2:3] * attn_out
        out_ref[span, :] = (resid + mod[5:6] * mlp_out).astype(BF)
        normed, inverse = normalise(resid)
        gres = cot + normalise_back(normed, inverse, gin * (1.0 + mod[4:5]))
        gres_ref[span, :] = gres.astype(BF)
        gattn_ref[span, :] = (mod[2:3] * gres).astype(BF)
        sums_ref[window, 0:1] = jnp.sum(gres * attn_out, axis=0, keepdims=True)
        sums_ref[window, 1:2] = jnp.sum(gin, axis=0, keepdims=True)
        sums_ref[window, 2:3] = jnp.sum(gin * normed, axis=0, keepdims=True)
        sums_ref[window, 3:4] = jnp.sum(cot * mlp_out, axis=0, keepdims=True)


def kept_spec(shape):
    return pl.BlockSpec(shape, lambda i: (0,) * len(shape), pipeline_mode=pl.Buffered(1))


def mlp_out_call(act, ghid, down, up, tokens, cotangent, attn_out, mods, deps=()):
    rows, width = tokens.shape
    per = 1
    block = per * WIN_TOK
    row = row_spec(block, width)
    windows = rows // WIN_TOK
    return call_after(
        functools.partial(mlp_out_kernel, count=len(act)),
        deps,
        grid=(windows // per,),
        in_specs=[row_spec(block, part.shape[1]) for part in act + ghid]
        + [kept_spec(part.shape) for part in down + up]
        + [row, row, row, mod_spec(per, mods.shape[1], width)],
        out_specs=[row, row, row, mod_spec(per, 4, width)],
        out_shape=[
            shaped((rows, width), BF),
            shaped((rows, width), BF),
            shaped((rows, width), BF),
            shaped((windows, 4, width), F32),
        ],
        compiler_params=params(),
        cost_estimate=cost(55),
        name="mlp_out",
    )(*act, *ghid, *down, *up, tokens, cotangent, attn_out, mods)


def last_kernel(*refs, count):
    dqkv_refs = refs[:count]
    weight_refs = refs[count : 2 * count]
    tokens_ref, gres_ref, mod_ref, out_ref, sums_ref = refs[2 * count :]
    join = lambda refs: jnp.concatenate([ref[part] for ref in refs for part in range(3)], axis=1)
    gin = dot(join(dqkv_refs), join(weight_refs), 1, 1)
    for window in range(gin.shape[0] // WIN_TOK):
        span = window_span(window)
        normed, inverse = normalise(tokens_ref[span, :].astype(F32))
        grad = gin[span]
        out_ref[span, :] = (
            gres_ref[span, :].astype(F32) + normalise_back(normed, inverse, grad * (1.0 + mod_ref[window, 1:2]))
        ).astype(BF)
        sums_ref[window, 0:1] = jnp.sum(grad, axis=0, keepdims=True)
        sums_ref[window, 1:2] = jnp.sum(grad * normed, axis=0, keepdims=True)


def last_call(dqkv, weights, tokens, gres, mods, deps=()):
    rows, width = tokens.shape
    count = len(dqkv)
    per = 1
    block = per * WIN_TOK
    row = row_spec(block, width)
    windows = rows // WIN_TOK
    return call_after(
        functools.partial(last_kernel, count=count),
        deps,
        grid=(windows // per,),
        in_specs=[part_spec(block, part.shape[2]) for part in dqkv]
        + [kept_spec(part.shape) for part in weights]
        + [row, row, mod_spec(per, mods.shape[1], width)],
        out_specs=[row, mod_spec(per, 2, width)],
        out_shape=[shaped((rows, width), BF), shaped((windows, 2, width), F32)],
        compiler_params=params(),
        cost_estimate=cost(28),
        name="last",
    )(*dqkv, *weights, tokens, gres, mods)


def body(
    n_dp,
    n_mp,
    tokens,
    cotangent,
    qkv_weight,
    out_weight,
    up_weight,
    down_weight,
    rel_bias,
    ada_weight,
    ada_bias,
    class_embed,
    window_clip,
    timesteps,
    class_ids,
):
    mp_index = lax.axis_index("mp")
    micro, local_rows, width = tokens.shape
    local_cols = class_embed.shape[1]
    clips = timesteps.shape[1]
    own_windows = local_rows // WIN_TOK
    rows = micro * local_rows
    tokens_flat = tokens.reshape(rows, width)
    cot_flat = cotangent.reshape(rows, width)
    masks = range(n_mp)

    columns = mp_index * local_cols + jnp.arange(local_cols)
    half_width = width // 2
    freq_index = (columns % half_width).astype(F32)
    frequency = jnp.exp(-math.log(10000.0) * freq_index / half_width)
    angle = timesteps.astype(F32)[..., None] * frequency
    step_embed = jnp.where(columns < half_width, jnp.sin(angle), jnp.cos(angle))
    class_hot = (class_ids[..., None] == jnp.arange(class_embed.shape[0])).astype(F32)
    condition = step_embed + jnp.einsum("mck,kd->mcd", class_hot, class_embed, precision=highest)
    lowered = jax.nn.silu(condition).astype(BF)
    mod_terms = jnp.einsum("mcd,de->mce", lowered, ada_weight, preferred_element_type=F32)
    near_terms = add_low(mod_terms, swap(mod_terms, "mp", n_mp, 1))
    modulation = near_terms
    for bit in bits_of(n_mp)[1:]:
        modulation = add_low(modulation, swap(modulation, "mp", n_mp, bit))
    modulation = modulation + ada_bias
    own_clip = lax.dynamic_slice_in_dim(window_clip, mp_index * own_windows, own_windows, 1)
    clip_hot = (own_clip[..., None] == jnp.arange(clips)).astype(F32)
    mods = jnp.einsum("mwc,mce->mwe", clip_hot, modulation, precision=highest)
    mods = mods.reshape(micro * own_windows, 6, width)

    steps = Steps()
    rel_tables = gather_shards(rel_bias, "mp", n_mp)
    blocks = bias_blocks(jnp.concatenate([rel_tables[m] for m in masks], axis=0))
    heads = rel_bias.shape[0]

    def gather(own, hold):
        shards = {}
        steps.jobs.append(gather_job(steps, own, shards, "mp", n_mp, hold))
        return shards

    def need(shards, mask, ties, token):
        while mask not in shards:
            ties = ties + steps.step(token)
        return ties

    qkv_w = gather(qkv_weight, 3)
    steps.step(modulation)
    attn_in = norm_call(tokens_flat, mods)
    out_w = gather(out_weight, 3)
    ties = steps.step(attn_in)
    qkv, mixed, lse = {}, {}, {}
    for m in masks:
        ties = need(qkv_w, m, ties, attn_in)
        qkv[m], mixed[m], lse[m] = attend_call(
            attn_in, qkv_w[m], (blocks, m, heads), ties, 1 if m == n_mp - 1 else 2
        )
        if m == 0:
            down_w = gather(down_weight, 4)
        elif m == 2 or m == n_mp - 1 == 1:
            up_w = gather(up_weight, 3)
        ties = steps.step(mixed[m])
    for m in masks:
        ties = need(out_w, m, ties, mixed[0])
    attn_out, mlp_in, grad_mlp = middle_call(
        [mixed[m] for m in masks], [out_w[m] for m in masks], tokens_flat, cot_flat, mods, ties
    )
    ties = steps.step(mlp_in)
    wide_sums = Sums(steps, n_mp, [0, 1, 1, 2])
    grads = {}
    steps.jobs.append(spread_job(steps, wide_sums, [0, 1], n_dp, True, False, grads, "down"))
    steps.jobs.append(spread_job(steps, wide_sums, [2, 3], n_dp, False, True, grads, "up"))
    act, grad_hidden = {}, {}
    for m in [m for m in masks if m % 2] + [m for m in reversed(masks) if m % 2 == 0]:
        ties = need(down_w, m, need(up_w, m, ties, mlp_in), mlp_in)
        act[m], grad_hidden[m], *wide_terms = mlp_call(mlp_in, grad_mlp, up_w[m], down_w[m], ties)
        wide_sums.add(m, wide_terms)
        ties = steps.step(wide_terms[0])
    block_out, grad_resid, grad_attn, late_sums = mlp_out_call(
        *[[part[m] for m in masks] for part in (act, grad_hidden, down_w, up_w)],
        tokens_flat,
        cot_flat,
        attn_out,
        mods,
        ties,
    )

    def clip_sums(window_sums):
        grouped = window_sums.reshape(micro, own_windows, -1)
        return jnp.einsum("mwc,mwe->mce", clip_hot, grouped, precision=highest).astype(BF)

    attn_sums = Sums(steps, n_mp, [0])
    steps.jobs.append(spread_job(steps, attn_sums, [0], n_dp, False, False, grads, "attention"))
    dqkv, block_grads = {}, None
    ties = steps.step(grad_attn)
    for m in reversed(masks):
        dqkv[m], block_grads, qkv_term = attend_back_call(
            grad_attn, out_w[m], qkv[m], mixed[m], lse[m], (blocks, m, heads), attn_in, block_grads, ties
        )
        attn_sums.add(m, [qkv_term.reshape(-1, qkv_term.shape[2])])
        ties = steps.step(qkv_term)
    token_grad, early_sums = last_call(
        [dqkv[m] for m in masks], [qkv_w[m] for m in masks], tokens_flat, grad_resid, mods, ties
    )
    ties = steps.step(token_grad)
    window_sums = after(jnp.concatenate([early_sums, late_sums], axis=1), *ties)
    rel_sums = after(block_grads, *ties)
    rel_sums = collect_blocks(rel_sums).astype(BF).reshape(n_mp, -1)
    table_size = rel_sums.shape[1]
    rel_sums = jnp.pad(rel_sums, ((0, 0), (0, -table_size % width))).reshape(n_mp, -1, width)
    clip_terms = clip_sums(window_sums).reshape(-1, width)
    summed = steps.step()
    down_grad = unfold_call(grads["down"], 2, summed)
    steps.first = [down_grad, grads["up"]]
    ties = steps.step()
    mod_total, rel_total = sum_everywhere(
        after(clip_terms, *ties), after(rel_sums, *ties), n_mp, n_dp
    )
    rel_grad = rel_total.reshape(-1)[:table_size].reshape(rel_bias.shape).astype(F32)
    steps.finish()

    up_grad = grads["up"]
    qkv_grad, out_grad = grads["attention"]
    qkv_grad = qkv_grad.reshape(qkv_weight.shape)
    mod_total = mod_total.astype(F32).reshape(micro, clips, 6 * width)
    ada_bias_grad = jnp.sum(mod_total, axis=(0, 1))
    ada_weight_grad = jnp.einsum(
        "mcd,mce->de", lowered.astype(F32), mod_total, precision=highest
    )
    grad_lowered = jnp.einsum(
        "mce,de->mcd", mod_total, ada_weight.astype(F32), precision=highest
    )
    grad_condition = jax.vjp(jax.nn.silu, condition)[1](grad_lowered)[0]
    class_grad = jnp.einsum("mck,mcd->kd", class_hot, grad_condition, precision=highest)
    return (
        block_out.reshape(tokens.shape),
        token_grad.reshape(tokens.shape),
        qkv_grad,
        out_grad,
        up_grad,
        down_grad,
        rel_grad,
        ada_weight_grad,
        ada_bias_grad,
        class_grad,
    )


def solution(mesh):
    rows = P(None, ("dp", "mp"), None)
    in_specs = (
        rows,
        rows,
        P(None, None, "mp"),
        P("mp", None),
        P(None, "mp"),
        P("mp", None),
        P("mp", None),
        P("mp", None),
        P(),
        P(None, "mp"),
        P(None, "dp"),
        P(),
        P(),
    )
    out_specs = (
        rows,
        rows,
        P(None, None, "mp"),
        P("mp", None),
        P(None, "mp"),
        P("mp", None),
        P("mp", None),
        P("mp", None),
        P(),
        P(None, "mp"),
    )
    step = functools.partial(body, mesh.shape["dp"], mesh.shape["mp"])
    return jax.shard_map(step, mesh=mesh, in_specs=in_specs, out_specs=out_specs, check_vma=False)
```

```python
import functools
import math

import jax
import jax.numpy as jnp
from jax import lax
from jax.experimental import pallas as pl
from jax.experimental.pallas import tpu as pltpu
from jax.sharding import PartitionSpec as P

WIN_T = 5
WIN_H = 8
WIN_W = 8
WIN_TOK = WIN_T * WIN_H * WIN_W
FRAME = WIN_H * WIN_W
PAD_TOK = 384
HEAD_DIM = 64
N_TIME, N_ROW, N_COL = 2 * WIN_T - 1, 2 * WIN_H - 1, 2 * WIN_W - 1

BF = jnp.bfloat16
F32 = jnp.float32
epsilon = 1e-06
highest = lax.Precision.HIGHEST
GELU_A = 0.7978845608028654
GELU_B = GELU_A * 0.044715
VMEM_LIMIT = 63 * 1024 * 1024


def dot(left, right, left_dim=1, right_dim=0):
    return lax.dot_general(
        left, right, (((left_dim,), (right_dim,)), ((), ())), preferred_element_type=F32
    )


def params():
    return pltpu.CompilerParams(vmem_limit_bytes=VMEM_LIMIT)


def shaped(shape, dtype):
    return jax.ShapeDtypeStruct(shape, dtype)


def row_spec(rows, cols):
    return pl.BlockSpec((rows, cols), lambda i: (i, 0))


def part_spec(rows, cols):
    return pl.BlockSpec((3, rows, cols), lambda i: (0, i, 0))


def per_step(rows):
    return 2 if rows % (2 * WIN_TOK) == 0 else 1


def window_span(window):
    return slice(window * WIN_TOK, (window + 1) * WIN_TOK)


def whole_spec(shape):
    return pl.BlockSpec(shape, lambda i: (0,) * len(shape))


def mod_spec(per, count, cols):
    return pl.BlockSpec((per, count, cols), lambda i: (i, 0, 0))


def cost(micros):
    return pl.CostEstimate(
        flops=int(micros * 1e9), bytes_accessed=int(micros * 3.5e6), transcendentals=0
    )


def call_after(kernel, deps, *, in_specs, **rest):
    deps = tuple(deps)
    count = len(in_specs)

    def run(*refs):
        kernel(*refs[:count], *refs[count + len(deps) :])

    call = pl.pallas_call(
        run, in_specs=list(in_specs) + [pl.BlockSpec(memory_space=pl.ANY)] * len(deps), **rest
    )
    return lambda *args: call(*args, *deps)


def after(value, *deps):
    return lax.optimization_barrier((value, *deps))[0]


def normalise(values):
    centred = values - jnp.mean(values, axis=-1, keepdims=True)
    inverse = lax.rsqrt(jnp.mean(centred * centred, axis=-1, keepdims=True) + epsilon)
    return centred * inverse, inverse


def normalise_back(normed, inverse, grad_in):
    return inverse * (
        grad_in
        - jnp.mean(grad_in, axis=-1, keepdims=True)
        - normed * jnp.mean(grad_in * normed, axis=-1, keepdims=True)
    )


def swap(value, axis, size, bit):
    return lax.ppermute(value, axis, [(i, i ^ bit) for i in range(size)])


def bits_of(size):
    return [1 << b for b in range(size.bit_length() - 1)]


def add_low(left, right):
    return (left.astype(F32) + right.astype(F32)).astype(left.dtype)


def gather_shards(own, axis, size):
    shards = {0: own}
    for bit in reversed(bits_of(size)):
        for mask in list(shards):
            shards[mask ^ bit] = swap(shards[mask], axis, size, bit)
    return shards


def reduce_all(value, axis, size):
    for bit in bits_of(size):
        value = add_low(value, swap(value, axis, size, bit))
    return value


def reduce_shards(terms, axis, size):
    terms = dict(terms)
    for bit in bits_of(size):
        for mask in [m for m in terms if m & bit]:
            terms[mask ^ bit] = add_low(terms[mask ^ bit], swap(terms.pop(mask), axis, size, bit))
    return terms[0]


def sum_kernel(*refs, groups):
    outs = refs[sum(groups) :]
    for out, group in zip(outs, groups):
        total = refs[0][...].astype(F32)
        for ref in refs[1:group]:
            total = total + ref[...].astype(F32)
        out[...] = total.astype(BF)
        refs = refs[group:]


def add_groups(groups):
    if all(len(group) == 1 for group in groups):
        return [group[0] for group in groups]
    shapes = [group[0].shape for group in groups]
    turns = 4 if all(shape[0] % 64 == 0 and shape[0] >= 512 for shape in shapes) else 1
    spec = lambda shape: row_spec(shape[0] // turns, shape[1])
    return pl.pallas_call(
        functools.partial(sum_kernel, groups=[len(group) for group in groups]),
        grid=(turns,),
        in_specs=[spec(array.shape) for group in groups for array in group],
        out_specs=[spec(shape) for shape in shapes],
        out_shape=[shaped(shape, BF) for shape in shapes],
        compiler_params=params(),
        cost_estimate=cost(0.001),
        name="add",
    )(*[array for group in groups for array in group])


def split_kernel(index_ref, *refs, count, groups, deps):
    outs = refs[sum(groups) + deps :]
    totals = []
    for group in groups:
        total = refs[0][...].astype(F32)
        for ref in refs[1:group]:
            total = total + ref[...].astype(F32)
        totals.append(total.astype(BF))
        refs = refs[group:]
    size = totals[0].shape[0]
    for k in range(count):

        @pl.when(pl.program_id(0) == k)
        def _():
            for place, total in enumerate(totals):
                outs[k][place * size : (place + 1) * size, :] = total


def split_call(groups, index, count, deps=()):
    rows, cols = groups[0][0].shape
    part = (rows // count, cols)
    piece = (len(groups) * part[0], cols)
    parts = [array for group in groups for array in group]
    spec = pltpu.PrefetchScalarGridSpec(
        num_scalar_prefetch=1,
        grid=(count,),
        in_specs=[pl.BlockSpec(part, lambda k, f: (f[0] ^ k, 0))] * len(parts)
        + [pl.BlockSpec(memory_space=pl.ANY)] * len(deps),
        out_specs=[pl.BlockSpec(piece, lambda k, f: (0, 0))] * count,
    )
    return pl.pallas_call(
        functools.partial(
            split_kernel, count=count, groups=[len(group) for group in groups], deps=len(deps)
        ),
        grid_spec=spec,
        out_shape=[shaped(piece, BF)] * count,
        compiler_params=params(),
        cost_estimate=cost(0.001),
        name="split",
    )(jnp.reshape(index, (1,)).astype(jnp.int32), *parts, *deps)


def assemble_kernel(index_ref, *refs, count, groups):
    step = pl.program_id(0)
    size = refs[-1].shape[0]
    rows = pl.ds(pl.multiple_of(step % groups * size, size), size)
    for k, ref in enumerate(refs[:count]):

        @pl.when(step // groups == k)
        def _():
            refs[-1][...] = ref[rows, :].astype(refs[-1].dtype)


def assemble_call(pieces, index, dtype, groups=1, deps=()):
    count = len(pieces)
    rows, cols = pieces[0].shape
    spec = pltpu.PrefetchScalarGridSpec(
        num_scalar_prefetch=1,
        grid=(count * groups,),
        in_specs=[pl.BlockSpec((rows, cols), lambda i, f: (0, 0))] * count
        + [pl.BlockSpec(memory_space=pl.ANY)] * len(deps),
        out_specs=pl.BlockSpec(
            (rows // groups, cols), lambda i, f: (i % groups * count + (f[0] ^ (i // groups)), 0)
        ),
    )
    return pl.pallas_call(
        functools.partial(assemble_kernel, count=count, groups=groups),
        grid_spec=spec,
        out_shape=shaped((rows * count, cols), dtype),
        compiler_params=params(),
        cost_estimate=cost(0.001),
        name="assemble",
    )(jnp.reshape(index, (1,)).astype(jnp.int32), *pieces, *deps)


def attention_grads_kernel(index_ref, own_ref, other_ref, qkv_ref, out_ref):
    step = pl.program_id(0)
    place = 2 * (index_ref[0] ^ (step // 2)) + step % 2
    size = qkv_ref.shape[0]
    rows = pl.ds(pl.multiple_of(step % 2 * size, size), size)
    for k, ref in enumerate((own_ref, other_ref)):

        @pl.when((step // 2 == k) & (place < 3))
        def _():
            qkv_ref[...] = ref[rows, :].astype(F32)

        @pl.when((step // 2 == k) & (place == 3))
        def _():
            out_ref[...] = ref[rows, :].astype(F32).T


def attention_grads_call(halves, index, dtype, groups):
    rows, cols = halves[0].shape
    size = rows // 2
    place = lambda i, f: (jnp.minimum(2 * (f[0] ^ (i // 2)) + i % 2, 2), 0)
    spec = pltpu.PrefetchScalarGridSpec(
        num_scalar_prefetch=1,
        grid=(4,),
        in_specs=[pl.BlockSpec((rows, cols), lambda i, f: (0, 0))] * 2,
        out_specs=[
            pl.BlockSpec((size, cols), place),
            pl.BlockSpec((cols, size), lambda i, f: (0, 0)),
        ],
    )
    return pl.pallas_call(
        attention_grads_kernel,
        grid_spec=spec,
        out_shape=[shaped((3 * size, cols), dtype), shaped((cols, size), dtype)],
        compiler_params=params(),
        cost_estimate=cost(0.001),
        name="attention_grads",
    )(jnp.reshape(index, (1,)).astype(jnp.int32), *halves)


def unfold_kernel(part_ref, out_ref):
    out_ref[...] = part_ref[...].astype(F32)


def unfold_call(parts, groups, deps):
    count, rows, cols = parts.shape
    far = count // 2
    own = far // groups

    def place(i):
        group, near, piece = i // (2 * own), i // own % 2, i % own
        return (2 * (group * own + piece) + near, 0, 0)

    return call_after(
        unfold_kernel,
        deps,
        grid=(count,),
        in_specs=[pl.BlockSpec((None, rows, cols), place)],
        out_specs=row_spec(rows, cols),
        out_shape=shaped((count * rows, cols), F32),
        compiler_params=params(),
        cost_estimate=cost(0.001),
        name="unfold",
    )(parts)


class Steps:
    def __init__(self):
        self.jobs, self.token, self.ties, self.first = [], None, [], []

    def swap(self, value, axis, size, bit):
        if self.token is not None:
            value = after(value, self.token)
        return swap(value, axis, size, bit)

    def arrive(self, value):
        return value if self.token is None else after(value, self.token)

    def step(self, token=None):
        self.token = token
        self.ties, jobs = [], []
        for job in self.jobs:
            try:
                self.ties = self.ties + next(job)
            except StopIteration:
                continue
            jobs.append(job)
        self.jobs = jobs
        return self.ties if token is None else self.ties + [token]

    def finish(self):
        while self.jobs:
            self.step()


def gather_job(steps, own, shards, axis, size, hold):
    shards[0] = own
    even = {0: own}
    shards[1] = steps.swap(own, axis, size, 1)
    for bit in reversed(bits_of(size)[1:]):
        new = {mask ^ bit: steps.swap(part, axis, size, bit) for mask, part in even.items()}
        for _ in range(hold):
            yield []
        new = {mask: steps.arrive(part) for mask, part in new.items()}
        even.update(new)
        for mask, part in new.items():
            shards[mask] = part
            shards[mask ^ 1] = steps.swap(part, axis, size, 1)
        yield list(new.values())


class Sums:
    def __init__(self, steps, size, lags):
        self.steps, self.size, self.lags = steps, size, lags
        self.parts = {mask: [[] for _ in lags] for mask in range(size)}
        nearest_first = sorted(range(1, size), key=lambda mask: (mask & -mask, mask))
        steps.jobs += [self.send(mask) for mask in nearest_first]

    def full(self, mask, places):
        low = mask & -mask if mask else self.size
        return all(len(self.parts[mask][i]) == low.bit_length() for i in places)

    def add(self, mask, terms):
        for part, term in zip(self.parts[mask], terms):
            part.append(term)

    def send(self, mask):
        every = range(len(self.lags))
        while not self.full(mask, every):
            yield []
        bit = mask & -mask
        values = list(add_groups(self.parts[mask]))
        lags = self.lags if bit > 1 else [0] * len(values)
        flying, ready = {}, values if bit > 1 else []
        for turn in range(max(lags) + 2):
            for i in every:
                if turn == lags[i] + 1:
                    other = self.steps.arrive(flying[i])
                    self.parts[mask ^ bit][i].append(other)
                    ready = ready + [other]
                if turn == lags[i]:
                    flying[i] = self.steps.swap(values[i], "mp", self.size, bit)
            yield ready
            ready = []


def sum_everywhere(shared, by_shard, n_mp, n_dp):
    rows = shared.shape[0]
    for axis, size in (("mp", n_mp), ("dp", n_dp)):
        for bit in bits_of(size):
            sent = by_shard
            if axis == "mp":
                pairs = (size // (2 * bit), 2, bit * by_shard.shape[1], by_shard.shape[2])
                sent = by_shard.reshape(pairs)[:, ::-1]
            sent = jnp.concatenate([shared, sent.reshape(-1, shared.shape[1])], axis=0)
            other = swap(sent, axis, size, bit)
            shared = add_low(shared, other[:rows])
            by_shard = add_low(by_shard, other[rows:].reshape(by_shard.shape))
    return shared, by_shard[0]


def spread_job(steps, sums, places, n_dp, offload, late, out, name):
    while not sums.full(0, places):
        yield []
    index = lax.axis_index("dp")
    count = n_dp // 2
    keep, send = split_call([sums.parts[0][i] for i in places], index % 2, 2)
    other = steps.swap(send, "dp", n_dp, 1)
    yield [send]
    pieces = split_call([[keep, steps.arrive(other)]], index // 2, count, steps.ties)
    others = [steps.swap(pieces[k], "dp", n_dp, 2 * k) for k in range(1, count)]
    yield [other, *pieces]
    (total,) = add_groups([[pieces[0]] + [steps.arrive(part) for part in others]])
    if offload:
        whole = lax.all_gather(total, "dp", axis=0)
        yield [total]
        yield []
        out[name] = steps.arrive(whole)
        yield [whole]
        return
    others = [steps.swap(total, "dp", n_dp, 2 * k) for k in range(1, count)]
    yield [total]
    others = [steps.arrive(part) for part in others]
    half = assemble_call([total] + others, index // 2, BF, deps=steps.first)
    if late:
        yield [half]
    other = steps.swap(half, "dp", n_dp, 1)
    yield [] if late else [half]
    other = steps.arrive(other)
    finish = attention_grads_call if name == "attention" else assemble_call
    out[name] = finish([half, other], index % 2, F32, len(places))
    yield [] if late else [other]


def place_hot():
    place = jnp.arange(FRAME)
    row, col = place // WIN_W, place % WIN_W
    offset = (row[:, None] - row[None, :] + WIN_H - 1) * N_COL + (
        col[:, None] - col[None, :] + WIN_W - 1
    )
    return (offset.reshape(1, -1) == jnp.arange(N_ROW * N_COL)[:, None]).astype(F32)


def bias_blocks(rel_table):
    heads = rel_table.shape[0]
    cube = rel_table.reshape(heads * N_TIME, N_ROW * N_COL)
    return lax.dot(cube, place_hot(), precision=highest).reshape(heads, N_TIME, FRAME, FRAME)


def collect_blocks(block_grad):
    heads = block_grad.shape[0]
    flat = block_grad.reshape(heads * N_TIME, FRAME * FRAME)
    cube = lax.dot_general(flat, place_hot(), (((1,), (1,)), ((), ())), precision=highest)
    return cube[:, ::-1].reshape(heads, -1)


def block_spec(heads, place):
    return pl.BlockSpec((heads, N_TIME, FRAME, FRAME), lambda i: (place, 0, 0, 0))


def frame_span(frame):
    return slice(frame * FRAME, (frame + 1) * FRAME)


def spread_blocks(blocks_ref, table, fill, transposed):
    for head in range(table.shape[0]):
        for offset in range(N_TIME):
            block = blocks_ref[head, offset]
            if transposed:
                block = block.T
            for query in range(WIN_T):
                key = query - (offset - WIN_T + 1)
                if 0 <= key < WIN_T:
                    row, col = (key, query) if transposed else (query, key)
                    table[head, frame_span(row), frame_span(col)] = block
        table[head, :, WIN_TOK:] = jnp.full((WIN_TOK, PAD_TOK - WIN_TOK), fill, F32)


def norm_kernel(tokens_ref, mod_ref, attn_in_ref):
    normed, _ = normalise(tokens_ref[...].astype(F32))
    attn_in_ref[...] = (normed * (1.0 + mod_ref[0, 1:2]) + mod_ref[0, 0:1]).astype(BF)


def norm_call(tokens, mods, deps=()):
    rows, width = tokens.shape
    return call_after(
        norm_kernel,
        deps,
        grid=(rows // WIN_TOK,),
        in_specs=[row_spec(WIN_TOK, width), mod_spec(1, mods.shape[1], width)],
        out_specs=row_spec(WIN_TOK, width),
        out_shape=shaped((rows, width), BF),
        compiler_params=params(),
        cost_estimate=cost(8),
        name="norm_in",
    )(tokens, mods)


def head_copies(value, heads):
    if heads == 1:
        return [value]
    lane = lax.broadcasted_iota(jnp.int32, value.shape, 1) // HEAD_DIM
    return [jnp.where(lane == head, value, jnp.zeros_like(value)) for head in range(heads)]


def pad_rows(value):
    return jnp.concatenate(
        [value, jnp.zeros((PAD_TOK - WIN_TOK, value.shape[1]), value.dtype)], axis=0
    )


def attend_kernel(x_ref, w_ref, blocks_ref, qkv_ref, mixed_ref, lse_ref, table, columns):
    heads = blocks_ref.shape[0]

    @pl.when(pl.program_id(0) == 0)
    def _():
        spread_blocks(blocks_ref, table, -1e30, False)
        columns[...] = jnp.zeros_like(columns)

    x = x_ref[...]
    queries = dot(x, w_ref[0]).astype(BF)
    keys = dot(x, w_ref[1]).astype(BF)
    values = dot(x, w_ref[2]).astype(BF)
    qkv_ref[0] = queries
    qkv_ref[1] = keys
    qkv_ref[2] = values
    scaled = queries * jnp.asarray(HEAD_DIM**-0.5, BF)
    for window in range(x.shape[0] // WIN_TOK):
        span = window_span(window)
        scores = dot(
            jnp.concatenate(head_copies(scaled[span], heads), axis=0), pad_rows(keys[span]), 1, 1
        )
        probs = []
        for head in range(heads):
            score = scores[window_span(head)] + table[head]
            top = jnp.max(score, axis=1, keepdims=True)
            exponent = jnp.exp(score - top)
            total = jnp.sum(exponent, axis=1, keepdims=True)
            probs.append((exponent * (1.0 / total)).astype(BF))
            columns[window, :WIN_TOK, head : head + 1] = top + jnp.log(total)
        value = jnp.concatenate([pad_rows(part) for part in head_copies(values[span], heads)], axis=0)
        mixed_ref[span, :] = dot(jnp.concatenate(probs, axis=1), value).astype(BF)
        lse_ref[window] = columns[window].T[: lse_ref.shape[1]]


def attend_call(attn_in, weight, blocks, deps=(), most=2):
    rows, width = attn_in.shape
    cols = weight.shape[2]
    blocks, place, heads = blocks
    windows = rows // WIN_TOK
    per = min(most, per_step(rows))
    block = per * WIN_TOK
    stat_rows = -(-heads // 8) * 8
    return call_after(
        attend_kernel,
        deps,
        grid=(windows // per,),
        in_specs=[row_spec(block, width), whole_spec(weight.shape), block_spec(heads, place)],
        out_specs=[
            part_spec(block, cols),
            row_spec(block, cols),
            mod_spec(per, stat_rows, PAD_TOK),
        ],
        out_shape=[
            shaped((3, rows, cols), BF),
            shaped((rows, cols), BF),
            shaped((windows, stat_rows, PAD_TOK), F32),
        ],
        scratch_shapes=[
            pltpu.VMEM((heads, WIN_TOK, PAD_TOK), F32),
            pltpu.VMEM((per, PAD_TOK, 128), F32),
        ],
        compiler_params=params(),
        cost_estimate=cost(19),
        name="attend",
    )(attn_in, weight, blocks)


def attend_back_kernel(*refs, held):
    grad_ref, out_w_ref, qkv_ref, mixed_ref, lse_ref, blocks_ref, x_ref = refs[:7]
    dqkv_ref, dblocks_ref, dw_ref, table, total, x_all, grad_all, d_all = refs[7 + held :]
    heads = blocks_ref.shape[0]
    cols = out_w_ref.shape[0]
    step = pl.program_id(0)

    @pl.when(step == 0)
    def _():
        spread_blocks(blocks_ref, table, 0.0, True)
        total[...] = jnp.zeros_like(total)

    grads_mixed = dot(grad_ref[...], out_w_ref[...], 1, 1).astype(BF)
    scale = jnp.asarray(HEAD_DIM**-0.5, BF)
    head_rows = (lse_ref.shape[1], cols)
    head_hot = (
        lax.broadcasted_iota(jnp.int32, head_rows, 1) // HEAD_DIM
        == lax.broadcasted_iota(jnp.int32, head_rows, 0)
    ).astype(BF)
    block = grad_ref.shape[0]
    rows = pl.ds(pl.multiple_of(step * block, block), block)
    x_all[rows, :] = x_ref[...]
    grad_all[rows, :] = grad_ref[...]
    d_all[3, rows, :] = mixed_ref[...]
    for window in range(block // WIN_TOK):
        place = window_span(window)
        grad_mixed = grads_mixed[place]
        query = qkv_ref[0, place, :]
        key = qkv_ref[1, place, :]
        value = qkv_ref[2, place, :]
        product = grad_mixed.astype(F32) * mixed_ref[place, :].astype(F32)
        upper = product.astype(BF)
        lower = (product - upper.astype(F32)).astype(BF)
        inner = dot(head_hot, pad_rows(upper), 1, 1) + dot(head_hot, pad_rows(lower), 1, 1)
        keys = jnp.concatenate(head_copies(key * scale, heads), axis=0)
        values = jnp.concatenate(head_copies(value, heads), axis=0)
        query_pad = pad_rows(query)
        grad_pad = pad_rows(grad_mixed)
        scores = dot(keys, query_pad, 1, 1)
        grad_probs = dot(values, grad_pad, 1, 1)
        probs = []
        grad_scores = []
        for head in range(heads):
            span = window_span(head)
            prob = jnp.exp(scores[span] + table[head] - lse_ref[window, head : head + 1, :])
            grad_score = (prob * (grad_probs[span] - inner[head : head + 1, :])).astype(BF)
            probs.append(prob.astype(BF))
            grad_scores.append(grad_score)
            total[head] += grad_score.astype(F32)
        wide = jnp.concatenate(grad_scores, axis=1)
        grad_value = dot(
            jnp.concatenate(probs, axis=1), jnp.concatenate(head_copies(grad_pad, heads), axis=0)
        )
        grad_key = dot(wide, jnp.concatenate(head_copies(query_pad * scale, heads), axis=0))
        grad_query = dot(jnp.concatenate(grad_scores, axis=0), keys, 0, 0)[:WIN_TOK]
        own = pl.ds(pl.multiple_of(step * block + window * WIN_TOK, WIN_TOK), WIN_TOK)
        for part, grad in enumerate((grad_query, grad_key, grad_value)):
            grad = grad.astype(BF)
            dqkv_ref[part, place, :] = grad
            d_all[part, own, :] = grad

    @pl.when(step == pl.num_programs(0) - 1)
    def _():
        for part in range(4):
            left = grad_all if part == 3 else x_all
            dw_ref[part] = dot(left[...], d_all[part], 0, 0).astype(BF)
        for head in range(heads):
            for offset in range(N_TIME):
                block = None
                for query in range(WIN_T):
                    key = query - (offset - WIN_T + 1)
                    if 0 <= key < WIN_T:
                        part = total[head, frame_span(key), frame_span(query)]
                        block = part if block is None else block + part
                dblocks_ref[head, offset] = block


def attend_back_call(grad_attn, out_weight, qkv, mixed, lse, blocks, attn_in, block_grads, deps=()):
    rows, width = grad_attn.shape
    cols = out_weight.shape[0]
    blocks, place, heads = blocks
    per = per_step(rows)
    block = per * WIN_TOK
    held = () if block_grads is None else (block_grads,)
    return call_after(
        functools.partial(attend_back_kernel, held=len(held)),
        deps,
        grid=(rows // block,),
        in_specs=[
            row_spec(block, width),
            whole_spec(out_weight.shape),
            part_spec(block, cols),
            row_spec(block, cols),
            mod_spec(per, lse.shape[1], PAD_TOK),
            block_spec(heads, place),
            row_spec(block, width),
        ]
        + [pl.BlockSpec(memory_space=pl.ANY)] * len(held),
        out_specs=[
            part_spec(block, cols),
            block_spec(heads, place),
            whole_spec((4, width, cols)),
        ],
        out_shape=[
            shaped((3, rows, cols), BF),
            shaped(blocks.shape, F32),
            shaped((4, width, cols), BF),
        ],
        scratch_shapes=[pltpu.VMEM((heads, WIN_TOK, PAD_TOK), F32)] * 2
        + [pltpu.VMEM((rows, width), BF)] * 2
        + [pltpu.VMEM((4, rows, cols), BF)],
        input_output_aliases={7: 1} if held else {},
        compiler_params=params(),
        cost_estimate=cost(30),
        name="attend_back",
    )(grad_attn, out_weight, qkv, mixed, lse, blocks, attn_in, *held)


def middle_kernel(*refs, count):
    mixed_refs = refs[:count]
    weight_refs = refs[count : 2 * count]
    tokens_ref, cot_ref, mod_ref, attn_out_ref, mlp_in_ref, grad_mlp_ref = refs[2 * count :]
    attn_out = dot(mixed_refs[0][...], weight_refs[0][...])
    for mixed_ref, weight_ref in zip(mixed_refs[1:], weight_refs[1:]):
        attn_out = attn_out + dot(mixed_ref[...], weight_ref[...])
    attn_out_ref[...] = attn_out.astype(BF)
    for window in range(attn_out.shape[0] // WIN_TOK):
        span = window_span(window)
        mod = mod_ref[window]
        resid = tokens_ref[span, :].astype(F32) + mod[2:3] * attn_out[span]
        normed, _ = normalise(resid)
        mlp_in_ref[span, :] = (normed * (1.0 + mod[4:5]) + mod[3:4]).astype(BF)
        grad_mlp_ref[span, :] = (mod[5:6] * cot_ref[span, :].astype(F32)).astype(BF)


def middle_call(mixed, weights, tokens, cotangent, mods, deps=()):
    rows, width = tokens.shape
    count = len(mixed)
    per = per_step(rows)
    block = per * WIN_TOK
    row = row_spec(block, width)
    return call_after(
        functools.partial(middle_kernel, count=count),
        deps,
        grid=(rows // block,),
        in_specs=[row_spec(block, part.shape[1]) for part in mixed]
        + [whole_spec(part.shape) for part in weights]
        + [row, row, mod_spec(per, mods.shape[1], width)],
        out_specs=[row, row, row],
        out_shape=[
            shaped((rows, width), BF),
            shaped((rows, width), BF),
            shaped((rows, width), BF),
        ],
        compiler_params=params(),
        cost_estimate=cost(16),
        name="middle",
    )(*mixed, *weights, tokens, cotangent, mods)


def mlp_kernel(
    x_ref, g_ref, up_ref, down_ref, act_ref, ghid_ref, *rest, chunk
):
    down_total, up_total = rest[4:]
    step = pl.program_id(0)
    x = x_ref[...]
    g = g_ref[...]
    for start in range(0, up_ref.shape[1], chunk):
        span = slice(start, start + chunk)
        hidden = dot(x, up_ref[:, span])
        grad_act = dot(g, down_ref[span, :], 1, 1)
        cubic = GELU_B * (hidden * hidden)
        gate = 0.5 + 0.5 * jnp.tanh(hidden * (GELU_A + cubic))
        act_ref[:, span] = (hidden * gate).astype(BF)
        slope = gate + gate * ((1.0 - gate) * (hidden * (2.0 * GELU_A + 6.0 * cubic)))
        ghid_ref[:, span] = (grad_act * slope).astype(BF)

    @pl.when(step == 0)
    def _():
        down_total[...] = dot(act_ref[...], g, 0, 0)
        up_total[...] = dot(x, ghid_ref[...], 0, 0)

    @pl.when(step > 0)
    def _():
        down_total[...] += dot(act_ref[...], g, 0, 0)
        up_total[...] += dot(x, ghid_ref[...], 0, 0)

    @pl.when(step == pl.num_programs(0) - 1)
    def _():
        for place, total in enumerate((down_total, up_total)):
            size = total.shape[0] // 2
            rest[2 * place][...] = total[:size].astype(BF)
            rest[2 * place + 1][...] = total[size:].astype(BF)


MLP_BLOCK = 640
MLP_CHUNK = 512


def mlp_call(x, g, up, down, deps=()):
    rows, width = x.shape
    hidden = up.shape[1]
    block = MLP_BLOCK if rows % MLP_BLOCK == 0 else WIN_TOK
    row = row_spec(block, width)
    wide = row_spec(block, hidden)
    halves = [(hidden // 2, width)] * 2 + [(width // 2, hidden)] * 2
    return call_after(
        functools.partial(mlp_kernel, chunk=min(MLP_CHUNK, hidden)),
        deps,
        grid=(rows // block,),
        in_specs=[row, row, whole_spec(up.shape), whole_spec(down.shape)],
        out_specs=[wide, wide] + [whole_spec(shape) for shape in halves],
        out_shape=[
            shaped((rows, hidden), BF),
            shaped((rows, hidden), BF),
        ]
        + [shaped(shape, BF) for shape in halves],
        scratch_shapes=[pltpu.VMEM(down.shape, F32), pltpu.VMEM(up.shape, F32)],
        compiler_params=params(),
        cost_estimate=cost(30),
        name="mlp",
    )(x, g, up, down)


def mlp_out_kernel(*refs, count):
    act_refs, ghid_refs, down_refs, up_refs = [
        refs[place * count : (place + 1) * count] for place in range(4)
    ]
    tokens_ref, cot_ref, attn_out_ref, mod_ref, out_ref, gres_ref, gattn_ref, sums_ref = refs[
        4 * count :
    ]
    join = lambda parts, axis: jnp.concatenate([part[...] for part in parts], axis=axis)
    mlp_outs = dot(join(act_refs, 1), join(down_refs, 0))
    gins = dot(join(ghid_refs, 1), join(up_refs, 1), 1, 1)
    for window in range(gins.shape[0] // WIN_TOK):
        span = window_span(window)
        mod = mod_ref[window]
        mlp_out, gin = mlp_outs[span], gins[span]
        cot = cot_ref[span, :].astype(F32)
        attn_out = attn_out_ref[span, :].astype(F32)
        resid = tokens_ref[span, :].astype(F32) + mod[2:3] * attn_out
        out_ref[span, :] = (resid + mod[5:6] * mlp_out).astype(BF)
        normed, inverse = normalise(resid)
        gres = cot + normalise_back(normed, inverse, gin * (1.0 + mod[4:5]))
        gres_ref[span, :] = gres.astype(BF)
        gattn_ref[span, :] = (mod[2:3] * gres).astype(BF)
        sums_ref[window, 0:1] = jnp.sum(gres * attn_out, axis=0, keepdims=True)
        sums_ref[window, 1:2] = jnp.sum(gin, axis=0, keepdims=True)
        sums_ref[window, 2:3] = jnp.sum(gin * normed, axis=0, keepdims=True)
        sums_ref[window, 3:4] = jnp.sum(cot * mlp_out, axis=0, keepdims=True)


def kept_spec(shape):
    return pl.BlockSpec(shape, lambda i: (0,) * len(shape), pipeline_mode=pl.Buffered(1))


def mlp_out_call(act, ghid, down, up, tokens, cotangent, attn_out, mods, deps=()):
    rows, width = tokens.shape
    per = 1
    block = per * WIN_TOK
    row = row_spec(block, width)
    windows = rows // WIN_TOK
    return call_after(
        functools.partial(mlp_out_kernel, count=len(act)),
        deps,
        grid=(windows // per,),
        in_specs=[row_spec(block, part.shape[1]) for part in act + ghid]
        + [kept_spec(part.shape) for part in down + up]
        + [row, row, row, mod_spec(per, mods.shape[1], width)],
        out_specs=[row, row, row, mod_spec(per, 4, width)],
        out_shape=[
            shaped((rows, width), BF),
            shaped((rows, width), BF),
            shaped((rows, width), BF),
            shaped((windows, 4, width), F32),
        ],
        compiler_params=params(),
        cost_estimate=cost(55),
        name="mlp_out",
    )(*act, *ghid, *down, *up, tokens, cotangent, attn_out, mods)


def last_kernel(*refs, count):
    dqkv_refs = refs[:count]
    weight_refs = refs[count : 2 * count]
    tokens_ref, gres_ref, mod_ref, out_ref, sums_ref = refs[2 * count :]
    join = lambda refs: jnp.concatenate([ref[part] for ref in refs for part in range(3)], axis=1)
    gin = dot(join(dqkv_refs), join(weight_refs), 1, 1)
    for window in range(gin.shape[0] // WIN_TOK):
        span = window_span(window)
        normed, inverse = normalise(tokens_ref[span, :].astype(F32))
        grad = gin[span]
        out_ref[span, :] = (
            gres_ref[span, :].astype(F32) + normalise_back(normed, inverse, grad * (1.0 + mod_ref[window, 1:2]))
        ).astype(BF)
        sums_ref[window, 0:1] = jnp.sum(grad, axis=0, keepdims=True)
        sums_ref[window, 1:2] = jnp.sum(grad * normed, axis=0, keepdims=True)


def last_call(dqkv, weights, tokens, gres, mods, deps=()):
    rows, width = tokens.shape
    count = len(dqkv)
    per = 1
    block = per * WIN_TOK
    row = row_spec(block, width)
    windows = rows // WIN_TOK
    return call_after(
        functools.partial(last_kernel, count=count),
        deps,
        grid=(windows // per,),
        in_specs=[part_spec(block, part.shape[2]) for part in dqkv]
        + [kept_spec(part.shape) for part in weights]
        + [row, row, mod_spec(per, mods.shape[1], width)],
        out_specs=[row, mod_spec(per, 2, width)],
        out_shape=[shaped((rows, width), BF), shaped((windows, 2, width), F32)],
        compiler_params=params(),
        cost_estimate=cost(28),
        name="last",
    )(*dqkv, *weights, tokens, gres, mods)


def body(
    n_dp,
    n_mp,
    tokens,
    cotangent,
    qkv_weight,
    out_weight,
    up_weight,
    down_weight,
    rel_bias,
    ada_weight,
    ada_bias,
    class_embed,
    window_clip,
    timesteps,
    class_ids,
):
    mp_index = lax.axis_index("mp")
    micro, local_rows, width = tokens.shape
    local_cols = class_embed.shape[1]
    clips = timesteps.shape[1]
    own_windows = local_rows // WIN_TOK
    rows = micro * local_rows
    tokens_flat = tokens.reshape(rows, width)
    cot_flat = cotangent.reshape(rows, width)
    masks = range(n_mp)

    columns = mp_index * local_cols + jnp.arange(local_cols)
    half_width = width // 2
    freq_index = (columns % half_width).astype(F32)
    frequency = jnp.exp(-math.log(10000.0) * freq_index / half_width)
    angle = timesteps.astype(F32)[..., None] * frequency
    step_embed = jnp.where(columns < half_width, jnp.sin(angle), jnp.cos(angle))
    class_hot = (class_ids[..., None] == jnp.arange(class_embed.shape[0])).astype(F32)
    condition = step_embed + jnp.einsum("mck,kd->mcd", class_hot, class_embed, precision=highest)
    lowered = jax.nn.silu(condition).astype(BF)
    mod_terms = jnp.einsum("mcd,de->mce", lowered, ada_weight, preferred_element_type=F32)
    near_terms = add_low(mod_terms, swap(mod_terms, "mp", n_mp, 1))
    modulation = near_terms
    for bit in bits_of(n_mp)[1:]:
        modulation = add_low(modulation, swap(modulation, "mp", n_mp, bit))
    modulation = modulation + ada_bias
    own_clip = lax.dynamic_slice_in_dim(window_clip, mp_index * own_windows, own_windows, 1)
    clip_hot = (own_clip[..., None] == jnp.arange(clips)).astype(F32)
    mods = jnp.einsum("mwc,mce->mwe", clip_hot, modulation, precision=highest)
    mods = mods.reshape(micro * own_windows, 6, width)

    steps = Steps()
    rel_tables = gather_shards(rel_bias, "mp", n_mp)
    blocks = bias_blocks(jnp.concatenate([rel_tables[m] for m in masks], axis=0))
    heads = rel_bias.shape[0]

    def gather(own, hold):
        shards = {}
        steps.jobs.append(gather_job(steps, own, shards, "mp", n_mp, hold))
        return shards

    def need(shards, mask, ties, token):
        while mask not in shards:
            ties = ties + steps.step(token)
        return ties

    qkv_w = gather(qkv_weight, 3)
    steps.step(near_terms)
    attn_in = norm_call(tokens_flat, mods)
    out_w = gather(out_weight, 3)
    ties = steps.step(attn_in)
    qkv, mixed, lse = {}, {}, {}
    for m in masks:
        ties = need(qkv_w, m, ties, attn_in)
        qkv[m], mixed[m], lse[m] = attend_call(
            attn_in, qkv_w[m], (blocks, m, heads), ties, 1 if m == n_mp - 1 else 2
        )
        if m == 0:
            down_w = gather(down_weight, 4)
        elif m == 2 or m == n_mp - 1 == 1:
            up_w = gather(up_weight, 3)
        ties = steps.step(mixed[m])
    for m in masks:
        ties = need(out_w, m, ties, mixed[0])
    attn_out, mlp_in, grad_mlp = middle_call(
        [mixed[m] for m in masks], [out_w[m] for m in masks], tokens_flat, cot_flat, mods, ties
    )
    ties = steps.step(mlp_in)
    wide_sums = Sums(steps, n_mp, [0, 1, 1, 2])
    grads = {}
    steps.jobs.append(spread_job(steps, wide_sums, [0, 1], n_dp, True, False, grads, "down"))
    steps.jobs.append(spread_job(steps, wide_sums, [2, 3], n_dp, False, True, grads, "up"))
    act, grad_hidden = {}, {}
    for m in [m for m in masks if m % 2] + [m for m in reversed(masks) if m % 2 == 0]:
        ties = need(down_w, m, need(up_w, m, ties, mlp_in), mlp_in)
        act[m], grad_hidden[m], *wide_terms = mlp_call(mlp_in, grad_mlp, up_w[m], down_w[m], ties)
        wide_sums.add(m, wide_terms)
        ties = steps.step(wide_terms[0])
    block_out, grad_resid, grad_attn, late_sums = mlp_out_call(
        *[[part[m] for m in masks] for part in (act, grad_hidden, down_w, up_w)],
        tokens_flat,
        cot_flat,
        attn_out,
        mods,
        ties,
    )

    def clip_sums(window_sums):
        grouped = window_sums.reshape(micro, own_windows, -1)
        return jnp.einsum("mwc,mwe->mce", clip_hot, grouped, precision=highest).astype(BF)

    attn_sums = Sums(steps, n_mp, [0])
    steps.jobs.append(spread_job(steps, attn_sums, [0], n_dp, False, False, grads, "attention"))
    dqkv, block_grads = {}, None
    ties = steps.step(grad_attn)
    for m in reversed(masks):
        dqkv[m], block_grads, qkv_term = attend_back_call(
            grad_attn, out_w[m], qkv[m], mixed[m], lse[m], (blocks, m, heads), attn_in, block_grads, ties
        )
        attn_sums.add(m, [qkv_term.reshape(-1, qkv_term.shape[2])])
        ties = steps.step(qkv_term)
    token_grad, early_sums = last_call(
        [dqkv[m] for m in masks], [qkv_w[m] for m in masks], tokens_flat, grad_resid, mods, ties
    )
    ties = steps.step(token_grad)
    window_sums = after(jnp.concatenate([early_sums, late_sums], axis=1), *ties)
    rel_sums = after(block_grads, *ties)
    rel_sums = collect_blocks(rel_sums).astype(BF).reshape(n_mp, -1)
    table_size = rel_sums.shape[1]
    rel_sums = jnp.pad(rel_sums, ((0, 0), (0, -table_size % width))).reshape(n_mp, -1, width)
    clip_terms = clip_sums(window_sums).reshape(-1, width)
    summed = steps.step()
    down_grad = unfold_call(grads["down"], 2, summed)
    steps.first = [down_grad, grads["up"]]
    ties = steps.step()
    mod_total, rel_total = sum_everywhere(
        after(clip_terms, *ties), after(rel_sums, *ties), n_mp, n_dp
    )
    rel_grad = rel_total.reshape(-1)[:table_size].reshape(rel_bias.shape).astype(F32)
    steps.finish()

    up_grad = grads["up"]
    qkv_grad, out_grad = grads["attention"]
    qkv_grad = qkv_grad.reshape(qkv_weight.shape)
    mod_total = mod_total.astype(F32).reshape(micro, clips, 6 * width)
    ada_bias_grad = jnp.sum(mod_total, axis=(0, 1))
    ada_weight_grad = jnp.einsum(
        "mcd,mce->de", lowered.astype(F32), mod_total, precision=highest
    )
    grad_lowered = jnp.einsum(
        "mce,de->mcd", mod_total, ada_weight.astype(F32), precision=highest
    )
    grad_condition = jax.vjp(jax.nn.silu, condition)[1](grad_lowered)[0]
    class_grad = jnp.einsum("mck,mcd->kd", class_hot, grad_condition, precision=highest)
    return (
        block_out.reshape(tokens.shape),
        token_grad.reshape(tokens.shape),
        qkv_grad,
        out_grad,
        up_grad,
        down_grad,
        rel_grad,
        ada_weight_grad,
        ada_bias_grad,
        class_grad,
    )


def solution(mesh):
    rows = P(None, ("dp", "mp"), None)
    in_specs = (
        rows,
        rows,
        P(None, None, "mp"),
        P("mp", None),
        P(None, "mp"),
        P("mp", None),
        P("mp", None),
        P("mp", None),
        P(),
        P(None, "mp"),
        P(None, "dp"),
        P(),
        P(),
    )
    out_specs = (
        rows,
        rows,
        P(None, None, "mp"),
        P("mp", None),
        P(None, "mp"),
        P("mp", None),
        P("mp", None),
        P("mp", None),
        P(),
        P(None, "mp"),
    )
    step = functools.partial(body, mesh.shape["dp"], mesh.shape["mp"])
    return jax.shard_map(step, mesh=mesh, in_specs=in_specs, out_specs=out_specs, check_vma=False)
```
